128 devices in a mesh: blk: 16 (over z_hi, y, core), hid: 8 (over x, z_lo).
Axes of the slice: x: 4, y: 4, z: 4 (z_hi: 2, z_lo: 2; z = z_hi * 2 + z_lo), core: 2. Of those that a mesh axis runs over, the one named last changes fastest.
Arguments:
- tokens: bfloat16 [8192, 1152], P('blk')
- cotangent: bfloat16 [8192, 1152], P('blk', 'hid'), may hold values from -6 to 6
- route_weight: float32 [8192, 2], P('blk'), may hold values from 0.1 to 1
- expert_ids: int32 [8192, 2], P('blk'), may hold values from 0 to 15, all different within a row; in each aligned block of 512 rows (0 to 511, 512 to 1023, ...) at most 128 rows name the same one
- timesteps: int32 [32], P('blk'), may hold values from 0 to 999
- time_table: float32 [1000, 1152], replicated, may hold values from -6 to 6
- up_weight: bfloat16 [16, 1152, 4608], P('blk', None, 'hid'), may hold values from -0.25 to 0.25
- down_weight: bfloat16 [16, 4608, 1152], P('blk', 'hid'), may hold values from -0.125 to 0.125
- modulation_weight: float32 [1152, 3, 1152], P(None, None, 'hid'), may hold values from -0.1875 to 0.1875
- modulation_bias: float32 [3, 1152], P(None, 'hid'), may hold values from -3 to 3
Outputs:
- token_grads: bfloat16 [8192, 1152], P('blk', 'hid')
- up_grads: float32 [16, 1152, 4608], P('blk', None, 'hid')
- down_grads: float32 [16, 4608, 1152], P('blk', 'hid')
- modulation_weight_grads: float32 [1152, 3, 1152], P('blk', None, 'hid')
- modulation_bias_grads: float32 [3, 1152], P(None, 'hid')
The draws below stay inside these ranges and needn't reach their ends.
Inputs may be any that keep to these rules, and one draw needn't show every extreme that they name: `expert_ids`: each row names 2 different experts. In the rows of one index of blk (aligned blocks of 512 tokens) no expert is named more than 128 times, and in every draw some expert is named exactly 128 times in some block.
All inputs are finite; a program needn't handle non-finite values.
Results may differ from the reference program's by a relative error of at most 0.023.
Values may be sent and summed in bfloat16 or wider, within the bound.
A program may use at most 128 MiB of HBM per device.

```python
import math
import jax
import jax.numpy as jnp
import numpy as np
from jax import lax

D = 1152
F = 4608
TOP = 2
PATCHES = 256
STEPS = 1000
EXPERTS = 16
TOK_DEV = 512
TOKENS = 8192
IMAGES = 32
CAP = 128
N_BLK = 16
N_HID = 8


def draw_tokens(key, part):
    key = jax.random.fold_in(key, 11)
    key_values, key_rows = jax.random.split(key)
    position = jnp.arange(D, dtype=jnp.float32) / D
    values = jax.random.normal(key_values, (TOKENS, D), jnp.float32)
    columns = jnp.exp(math.log(10.0) * position)
    rows = jnp.exp(jax.random.uniform(key_rows, (TOKENS, 1), jnp.float32, 0.0, math.log(10.0)))
    return (0.1 * values * rows * columns[None, :]).astype(jnp.bfloat16)


def place_ends(values, stream_key, smallest, high):
    longest = values.shape.index(max(values.shape))
    spots = []
    for shift in (0, 1):
        where = [jax.random.randint(jax.random.fold_in(stream_key, axis), (), 0, length) for axis, length in enumerate(values.shape)]
        where[longest] = (where[longest] + shift) % values.shape[longest]
        spots.append(tuple(where))
    return values.at[spots[0]].set(smallest).at[spots[1]].set(high)


def spiked(array, own_key, source, target, shards_of, factor):
    owner, partner = [(jnp.arange(array.shape[dim]) // (array.shape[dim] // shards_of)).reshape([-1 if axis == dim else 1 for axis in range(array.ndim)]) for dim in (source, target)]
    chosen = jax.random.permutation(own_key, shards_of)[partner]
    strong = (owner == chosen) | (owner == (partner + shards_of // 2) % shards_of)
    return jnp.where(strong, factor * array, array)


def steps_of(stream_key, shape, cuts, smallest, largest):
    def one(dim, blocks):
        steps = jax.random.uniform(jax.random.fold_in(jax.random.fold_in(stream_key, 6), dim), (blocks,), jnp.float32, smallest / len(cuts), largest / len(cuts))
        return jnp.repeat(jnp.exp(steps), shape[dim] // blocks).reshape((-1,) + (1,) * (len(shape) - dim - 1))

    gain = one(*cuts[0])
    for cut in cuts[1:]:
        gain = gain * one(*cut)
    return gain


def routed_block(key, own, number, rows, amount, top, bound, lean):
    sequence = jax.random.permutation(key, amount)
    crowded, ordinary = load_shares(amount, rows * top, bound, lean, True), load_shares(amount, rows * top, bound, lean, False)
    places = jnp.arange(amount)

    def named(sizes, rotation):
        used = int((sizes > 0).sum())
        fixed = max(1, used // 4)
        passed = fixed + (places - fixed + rotation * (used - fixed)) % max(1, amount - fixed)
        return jnp.zeros((amount,), jnp.int32).at[sequence[jnp.where(places < fixed, places, passed)]].set(jnp.asarray(sizes, jnp.int32))

    sizes = jnp.where(number % 4 == 0, named(crowded, number // 4), named(ordinary, number - number // 4 - 1))
    mixed = jax.random.permutation(jax.random.fold_in(own, 3), amount)
    donor, taker = mixed[0:amount // 2 * 2:2], mixed[1:amount // 2 * 2:2]
    slack = jnp.minimum(sizes[donor] - 1, bound - sizes[taker]) // 2
    slack = jnp.where((donor == sequence[0]) | (taker == sequence[0]) | (sizes[taker] == 0), 0, jnp.maximum(slack, 0))
    passed = jax.random.randint(jax.random.fold_in(own, 4), (amount // 2,), 0, 1 << 20) % (slack + 1)
    sizes = sizes.at[donor].add(-passed).at[taker].add(passed)
    labels = jnp.searchsorted(jnp.cumsum(sizes), jnp.arange(rows * top), side="right").astype(jnp.int32)
    listing = labels.reshape(top, rows).T
    listing = listing[jax.random.permutation(jax.random.fold_in(own, 1), rows)]
    rotation = jax.random.randint(jax.random.fold_in(own, 2), (rows, 1), 0, top)
    return jnp.take_along_axis(listing, (jnp.arange(top)[None, :] + rotation) % top, axis=1)


def load_shares(count, total, limit, slope, full):
    weights = [(1 << 20) // math.isqrt(standing ** slope) + 1 for standing in range(1, count + 1)]
    largest = limit if full else min(limit, max(-(-total // count), total * weights[0] // sum(weights)))
    least = 1 if total - largest >= count - 1 else 0
    counts, spare = [largest] + [least] * (count - 1), total - largest - least * (count - 1)
    while spare > 0:
        movable = [i for i in range(1, count) if counts[i] < largest] or [i for i in range(1, count) if counts[i] < limit]
        mass, remaining = sum([weights[i] for i in movable]), spare
        for i in movable:
            extra = min(limit - counts[i], max(1, remaining * weights[i] // mass), spare)
            counts[i] = counts[i] + extra
            spare = spare - extra
    return np.array(counts)


def centred(key, dims, deviation, bound, cuts=(), kind=jnp.bfloat16):
    factor_of = steps_of(key, dims, cuts, -0.22, 0.18) if cuts else 1.0
    values = jax.random.normal(key, dims, jnp.float32) * deviation * factor_of
    return jnp.minimum(jnp.maximum(values, -bound), bound).astype(kind)


def bell_draw_with(rng, extent, scale, most, cuts, heavy, held_as=jnp.bfloat16):
    array = scale * jax.random.normal(rng, extent, jnp.float32)
    if cuts:
        array = array * steps_of(rng, extent, cuts, -0.22, 0.18)
    return jnp.clip(spiked(array, jax.random.fold_in(rng, 3), *heavy), -most, most).astype(held_as)


def setup_inputs(seed: int = 0) -> dict:
    key_of = jax.random.split(jax.random.key(seed), 11)
    tokens = draw_tokens(jax.random.fold_in(key_of[10], 71), 0)
    cotangent = centred(key_of[1], (TOKENS, D), 1.0, 6.0, ((0, 16), (1, 8)))
    route_weight = jnp.clip(0.1 + 0.9 * jax.random.uniform(key_of[2], (TOKENS, TOP), jnp.float32) ** steps_of(key_of[2], (TOKENS, TOP), ((0, 16),), -0.2, 0.2), 0.1, 1.0)
    expert_ids_keys = jax.random.split(jax.random.fold_in(key_of[3], 1), TOKENS // TOK_DEV)
    expert_ids_turns = jax.random.permutation(jax.random.fold_in(key_of[3], 3), TOKENS // TOK_DEV)
    expert_ids = jax.vmap(lambda own, number: routed_block(jax.random.fold_in(key_of[3], 2), own, number, TOK_DEV, EXPERTS, TOP, CAP, 2))(expert_ids_keys, expert_ids_turns).reshape((TOKENS, TOP))
    timesteps = place_ends(jax.random.randint(key_of[4], (IMAGES,), 0, STEPS), jax.random.fold_in(key_of[4], 1), 0, STEPS - 1).astype(jnp.int32)
    time_table = centred(key_of[5], (STEPS, D), 1.0, 6.0, (), jnp.float32)
    up_weight = bell_draw_with(key_of[6], (EXPERTS, D, F), D ** -0.5, 0.25, ((0, 16), (2, 8)), (2, 1, 8, 2.0))
    down_weight = bell_draw_with(key_of[7], (EXPERTS, F, D), F ** -0.5, 0.125, ((0, 16), (1, 8)), (1, 2, 8, 2.0))
    modulation_weight = centred(key_of[8], (D, 3, D), D ** -0.5, 0.1875, ((2, 8),), jnp.float32)
    modulation_bias = centred(key_of[9], (3, D), 0.5, 3.0, ((1, 8),), jnp.float32)
    return dict(tokens=tokens, cotangent=cotangent, route_weight=route_weight, expert_ids=expert_ids, timesteps=timesteps, time_table=time_table, up_weight=up_weight, down_weight=down_weight, modulation_weight=modulation_weight, modulation_bias=modulation_bias)


norm_epsilon = 1e-06
gelu_cubic = 0.044715
gelu_factor = math.sqrt(2.0 / math.pi)

def gelu_tanh(values):
    inner = gelu_factor * (values + gelu_cubic * values * values * values)
    return 0.5 * values * (1.0 + jnp.tanh(inner))

def gelu_slope(values):
    inner = gelu_factor * (values + gelu_cubic * values * values * values)
    tangent = jnp.tanh(inner)
    return 0.5 * (1.0 + tangent) + 0.5 * values * (1.0 - tangent * tangent) * gelu_factor * (1.0 + 3.0 * gelu_cubic * values * values)

def rounded_sum(partials):
    kept = lax.optimization_barrier(partials.astype(jnp.bfloat16))
    return lax.optimization_barrier(jnp.sum(kept.astype(jnp.float32), axis=0))

def expert_step(operands):
    hidden_in, hidden_cot, up_matrix, down_matrix = operands
    group_width = F // N_HID
    pre_act = jnp.dot(hidden_in, up_matrix, preferred_element_type=jnp.float32)
    activated = gelu_tanh(pre_act).astype(jnp.bfloat16)
    act_groups = activated.astype(jnp.float32).reshape(-1, N_HID, group_width)
    down_groups = down_matrix.astype(jnp.float32).reshape(N_HID, group_width, D)
    expert_out = rounded_sum(jnp.einsum('sgf,gfd->gsd', act_groups, down_groups))
    act_grad = lax.dot_general(hidden_cot, down_matrix, (((1,), (1,)), ((), ())), preferred_element_type=jnp.float32)
    pre_grad = (act_grad * gelu_slope(pre_act)).astype(jnp.bfloat16)
    grad_groups = pre_grad.astype(jnp.float32).reshape(-1, N_HID, group_width)
    up_groups = up_matrix.astype(jnp.float32).reshape(D, N_HID, group_width)
    in_grad = rounded_sum(jnp.einsum('sgf,dgf->gsd', grad_groups, up_groups))
    up_part = lax.dot_general(hidden_in, pre_grad, (((0,), (0,)), ((), ())), preferred_element_type=jnp.float32)
    down_part = lax.dot_general(activated, hidden_cot, (((0,), (0,)), ((), ())), preferred_element_type=jnp.float32)
    return (up_part, down_part, expert_out, in_grad)

def reference(tokens, cotangent, route_weight, expert_ids, timesteps, time_table, up_weight, down_weight, modulation_weight, modulation_bias):
    condition = jax.nn.silu(time_table[timesteps.astype(jnp.int32)])
    modulation = jnp.einsum('bi,icd->bcd', condition, modulation_weight, precision=lax.Precision.HIGHEST) + modulation_bias[None]
    image_of = (jnp.arange(TOKENS) // PATCHES).astype(jnp.int32)
    shift_tok = modulation[image_of, 0]
    scale_tok = modulation[image_of, 1]
    gate_tok = modulation[image_of, 2]
    inputs = tokens.astype(jnp.float32)
    row_mean = lax.optimization_barrier(jnp.mean(inputs, axis=1, keepdims=True))
    spread = lax.optimization_barrier(jnp.mean((inputs - row_mean) ** 2, axis=1, keepdims=True))
    inv_spread = 1.0 / jnp.sqrt(spread + norm_epsilon)
    normed = (inputs - row_mean) * inv_spread
    expert_in = (normed * (1.0 + scale_tok) + shift_tok).astype(jnp.bfloat16)
    grad_out = cotangent.astype(jnp.float32)
    expert_cot = (route_weight[:, :, None] * (gate_tok * grad_out)[:, None, :]).astype(jnp.bfloat16)
    pair_ids = expert_ids.astype(jnp.int32).reshape(N_BLK, TOK_DEV * TOP)
    one_hot = (pair_ids[:, :, None] == jnp.arange(EXPERTS).astype(jnp.int32)[None, None, :]).astype(jnp.int32)
    before = jnp.cumsum(one_hot, axis=1) - one_hot
    slot = lax.optimization_barrier(jnp.sum(one_hot * before, axis=2))
    source = jnp.arange(N_BLK).astype(jnp.int32)[:, None]
    flat_index = ((pair_ids * N_BLK + source) * CAP + slot).reshape(TOKENS * TOP).astype(jnp.int32)
    buffer_rows = EXPERTS * N_BLK * CAP
    in_buffer = jnp.zeros((buffer_rows, D), jnp.bfloat16).at[flat_index].set(jnp.repeat(expert_in, TOP, axis=0))
    cot_buffer = jnp.zeros((buffer_rows, D), jnp.bfloat16).at[flat_index].set(expert_cot.reshape(TOKENS * TOP, D))
    in_buffer = in_buffer.reshape(EXPERTS, N_BLK * CAP, D)
    cot_buffer = cot_buffer.reshape(EXPERTS, N_BLK * CAP, D)
    up_grads, down_grads, outputs, input_grads = lax.map(expert_step, (in_buffer, cot_buffer, up_weight, down_weight))
    out_rows = outputs.reshape(buffer_rows, D)[flat_index].reshape(TOKENS, TOP, D)
    grad_rows = input_grads.reshape(buffer_rows, D)[flat_index].reshape(TOKENS, TOP, D)
    moe = lax.optimization_barrier(jnp.sum(route_weight[:, :, None] * out_rows, axis=1))
    mixed_grad = lax.optimization_barrier(jnp.sum(grad_rows, axis=1))
    shift_grad = lax.optimization_barrier(jnp.sum(mixed_grad.reshape(IMAGES, PATCHES, D), axis=1))
    scale_grad = lax.optimization_barrier(jnp.sum((mixed_grad * normed).reshape(IMAGES, PATCHES, D), axis=1))
    gate_grad = lax.optimization_barrier(jnp.sum((grad_out * moe).reshape(IMAGES, PATCHES, D), axis=1))
    modulation_grads = jnp.stack([shift_grad, scale_grad, gate_grad], axis=1)
    norm_grad = mixed_grad * (1.0 + scale_tok)
    first_mean = lax.optimization_barrier(jnp.mean(norm_grad, axis=1, keepdims=True))
    second_mean = lax.optimization_barrier(jnp.mean(norm_grad * normed, axis=1, keepdims=True))
    token_grads = (grad_out + inv_spread * (norm_grad - first_mean - normed * second_mean)).astype(jnp.bfloat16)
    modulation_weight_grads = jnp.einsum('bi,bcd->icd', condition, modulation_grads, precision=lax.Precision.HIGHEST)
    modulation_bias_grads = lax.optimization_barrier(jnp.sum(modulation_grads, axis=0))
    return (token_grads, up_grads, down_grads, modulation_weight_grads, modulation_bias_grads)
```

```python
import math

import jax
import jax.numpy as jnp
from jax import lax
from jax.experimental import pallas as pl
from jax.experimental.pallas import tpu as pltpu
from jax.sharding import PartitionSpec as P

MESH = pl.DeviceIdType.MESH
norm_epsilon = 1e-06
gelu_cubic = 0.044715
gelu_factor = math.sqrt(2.0 / math.pi)

N_BLK, N_HID = 16, 8
WIDTH, NARROW, CAP = 1152, 144, 128
SLOTS = N_BLK * CAP
GROUPS = 4
LANES = SLOTS // GROUPS
HALF = LANES // 2
ORDER = (0, 1, 6, 2, 7, 3, 5, 4)


def shift(j):
    return j // 8, ORDER[j % 8]


class Place:
    def __init__(self):
        self.blk = lax.axis_index("blk")
        self.hid = lax.axis_index("hid")
        self.z_hi, self.m = self.blk // 8, self.blk % 8
        self.x, self.z_lo = self.hid // 2, self.hid % 2
        self.x_right, self.x_left, self.x_far = [(self.x + i) % 4 for i in (1, 3, 2)]
        self.right = (self.blk, self.x_right * 2 + self.z_lo)
        self.left = (self.blk, self.x_left * 2 + self.z_lo)
        self.across = (self.blk, self.home(1))

    def home(self, a):
        return self.hid if a == 0 else self.hid + 1 - 2 * self.z_lo

    def later(self, j):
        a, m = shift(j)
        return (self.z_hi + a) % 2 * 8 + (self.m + m) % 8

    def earlier(self, j):
        a, m = shift(j)
        return (self.z_hi + a) % 2 * 8 + (self.m + 8 - m) % 8

    def hid_peer(self, i):
        return (self.blk, (self.hid + i) % 8)


def greet(devices):
    barrier = pltpu.get_barrier_semaphore()
    for device in devices:
        pl.semaphore_signal(barrier, inc=1, device_id=device, device_id_type=MESH)
    pl.semaphore_wait(barrier, len(devices))


def send(src, dst, send_sem, recv_sem, device, sent):
    copy = pltpu.make_async_remote_copy(
        src_ref=src, dst_ref=dst, send_sem=send_sem, recv_sem=recv_sem, device_id=device, device_id_type=MESH
    )
    copy.start()
    sent.append(copy)


def arrived(region, send_sem, recv_sem, device):
    pltpu.make_async_remote_copy(
        src_ref=region, dst_ref=region, send_sem=send_sem, recv_sem=recv_sem, device_id=device, device_id_type=MESH
    ).wait_recv()


def rows_of(slice_index, count=1):
    return pl.ds(pl.multiple_of(slice_index * NARROW, 16), count * NARROW)


def block_of(index):
    return pl.ds(pl.multiple_of(index * CAP, CAP), CAP)


def dispatch_kernel(
    px, pc, info, xt, ct, table, a2a_send, a2a_recv, ring_send, ring_recv, info_send, info_recv, local_sem
):
    at = Place()
    peers = [(at.later(j), at.home(j // 8)) for j in range(N_BLK)]
    greet(peers[1:] + [at.hid_peer(i) for i in range(1, N_HID)])
    own = rows_of(at.hid)
    sent = []
    local = []
    for j in range(N_BLK):
        lanes = pl.ds(j * CAP, CAP)
        target = at.later(j)
        parts = (
            (px.at[:, block_of(target)], xt.at[own, lanes]),
            (pc.at[:, block_of(target)], ct.at[own, lanes]),
            (info.at[target], table.at[at.hid, j]),
        )
        for i, (src, dst) in enumerate(parts):
            if j == 0:
                copy = pltpu.make_async_copy(src, dst, local_sem.at[i])
                copy.start()
                local.append(copy)
            else:
                send(src, dst, a2a_send.at[j, i], a2a_recv.at[j, i], peers[j], sent)

    def from_peer(j, i, region):
        if j == 0:
            local[i].wait()
        else:
            arrived(region, a2a_send.at[j, i], a2a_recv.at[j, i], peers[j])

    def ring(g):
        a = g // (GROUPS // 2)
        f = at.home(a)
        other = at.home(1 - a)
        zf = f % 2
        lanes = pl.ds(g * LANES, LANES)
        halves = [pl.ds(g * LANES + i * HALF, HALF) for i in range(2)]
        far_slice = at.x_far * 2 + zf

        def go(array, rows, cols, k, device):
            region = array.at[rows, cols]
            send(region, region, ring_send.at[g, k], ring_recv.at[g, k], device, sent)

        def come(array, rows, cols, k):
            arrived(array.at[rows, cols], ring_send.at[g, k], ring_recv.at[g, k], at.across)

        def first():
            for j in range(g * LANES // CAP, (g + 1) * LANES // CAP):
                from_peer(j, 0, xt.at[rows_of(f), pl.ds(j * CAP, CAP)])
                from_peer(j, 1, ct.at[rows_of(f), pl.ds(j * CAP, CAP)])
            go(xt, rows_of(f), lanes, 0, at.across)
            go(ct, rows_of(f), lanes, 6, at.right)
            go(ct, rows_of(f), lanes, 7, at.left)
            go(ct, rows_of(f), lanes, 5, at.across)

        def second():
            come(xt, rows_of(other), lanes, 0)
            go(xt, rows_of(at.x * 2, 2), lanes, 1, at.right)
            go(xt, rows_of(at.x * 2, 2), lanes, 2, at.left)
            left, right = rows_of(at.x_left * 2 + zf), rows_of(at.x_right * 2 + zf)
            come(ct, left, lanes, 6)
            go(ct, left, halves[0], 8, at.right)
            go(ct, left, lanes, 10, at.across)
            come(ct, right, lanes, 7)
            go(ct, right, halves[1], 9, at.left)
            go(ct, right, lanes, 11, at.across)

        def third():
            come(xt, rows_of(at.x_left * 2, 2), lanes, 1)
            go(xt, rows_of(at.x_left * 2), lanes, 3, at.right)
            come(xt, rows_of(at.x_right * 2, 2), lanes, 2)
            go(xt, rows_of(at.x_right * 2 + 1), lanes, 4, at.left)
            for i in range(2):
                come(ct, rows_of(far_slice), halves[i], 8 + i)
                go(ct, rows_of(far_slice), halves[i], 12 + i, at.across)

        def fourth():
            come(xt, rows_of(at.x_far * 2), lanes, 3)
            come(xt, rows_of(at.x_far * 2 + 1), lanes, 4)
            come(ct, rows_of(other), lanes, 5)
            come(ct, rows_of(at.x_left * 2 + 1 - zf), lanes, 10)
            come(ct, rows_of(at.x_right * 2 + 1 - zf), lanes, 11)
            for i in range(2):
                come(ct, rows_of(at.x_far * 2 + 1 - zf), halves[i], 12 + i)

        return first, second, third, fourth

    steps = [ring(g) for g in range(GROUPS)]

    def spread_info():
        for a in range(2):
            f = at.home(a)
            for j in range(8 * a, 8 * a + 8):
                from_peer(j, 2, table.at[f, j])
            half = table.at[f, pl.ds(8 * a, 8)]
            for i in range(1, N_HID):
                send(half, half, info_send.at[a, i], info_recv.at[a, i], at.hid_peer(i), sent)

    def gather_info():
        for a in range(2):
            for i in range(1, N_HID):
                q = (at.hid + 8 - i) % 8
                f = q if a == 0 else q + 1 - 2 * (q % 2)
                arrived(table.at[f, pl.ds(8 * a, 8)], info_send.at[a, i], info_recv.at[a, i], at.across)

    for tick in range(GROUPS + 3):
        for k in range(4):
            if 0 <= tick - k < GROUPS:
                steps[tick - k][k]()
        if tick == 1:
            spread_info()
    gather_info()
    for copy in sent:
        copy.wait_send()


def dispatch(px, pc, info):
    vmem = pl.BlockSpec(memory_space=pltpu.VMEM)
    return pl.pallas_call(
        dispatch_kernel,
        out_shape=(
            jax.ShapeDtypeStruct((WIDTH, SLOTS), jnp.bfloat16),
            jax.ShapeDtypeStruct((WIDTH, SLOTS), jnp.bfloat16),
            jax.ShapeDtypeStruct((N_HID, N_BLK, 2, 256), jnp.float32),
        ),
        in_specs=[vmem] * 3,
        out_specs=[vmem] * 3,
        scratch_shapes=[
            pltpu.SemaphoreType.DMA((N_BLK, 3)),
            pltpu.SemaphoreType.DMA((N_BLK, 3)),
            pltpu.SemaphoreType.DMA((GROUPS, 14)),
            pltpu.SemaphoreType.DMA((GROUPS, 14)),
            pltpu.SemaphoreType.DMA((2, N_HID)),
            pltpu.SemaphoreType.DMA((2, N_HID)),
            pltpu.SemaphoreType.DMA((3,)),
        ],
        compiler_params=pltpu.CompilerParams(
            collective_id=0, has_side_effects=True, vmem_limit_bytes=56 * 2**20
        ),
    )(px, pc, info)


def combine_kernel(
    part, gate_part, back, gate_back,
    first_a, second_a, third_a, first_b, second_b, mine_b, total, gate_in, gate_sum,
    ring_send, ring_recv, back_send, back_recv, gate_send, gate_recv, local_sem,
):
    at = Place()
    owners = [(at.earlier(j), at.home(j // 8)) for j in range(N_BLK)]
    greet(owners[1:] + [at.hid_peer(i) for i in range(1, N_HID)])
    sent = []
    wide = jnp.float32

    def put(ref, value):
        ref[...] = value.astype(ref.dtype)

    def ring(g):
        a = g // (GROUPS // 2)
        zf = at.home(a) % 2
        lanes_a = pl.ds(g * LANES, HALF)
        start_b = g * LANES + HALF
        lanes_b = pl.ds(start_b, HALF)

        def mine(x, z, lanes):
            return part.at[rows_of(x * 2 + z), lanes]

        def go(src, dst, k, device):
            send(src, dst, ring_send.at[g, k], ring_recv.at[g, k], device, sent)

        def come(region, k):
            arrived(region, ring_send.at[g, k], ring_recv.at[g, k], at.across)

        def first():
            for x in range(4):
                go(mine(x, 1 - zf, lanes_b), first_b.at[g, x], 8 + x, at.across)
            go(mine(at.x_far, 0, lanes_a), first_a.at[g, 0], 0, at.right)
            go(mine(at.x_far, 1, lanes_a), first_a.at[g, 1], 1, at.left)
            go(mine(at.x_right, 1, lanes_a), second_a.at[g, 1], 2, at.right)
            go(mine(at.x_left, 0, lanes_a), second_a.at[g, 2], 3, at.left)

        def second():
            come(first_a.at[g, 0], 0)
            put(
                third_a.at[g, 0],
                first_a[g, 0].astype(wide) + mine(at.x_right, 0, lanes_a)[...].astype(wide),
            )
            go(third_a.at[g, 0], second_a.at[g, 0], 4, at.right)
            come(first_a.at[g, 1], 1)
            put(
                third_a.at[g, 1],
                first_a[g, 1].astype(wide) + mine(at.x_left, 1, lanes_a)[...].astype(wide),
            )
            go(third_a.at[g, 1], second_a.at[g, 3], 5, at.left)
            for x in range(4):
                come(first_b.at[g, x], 8 + x)
            for i, x in enumerate((at.x_far, at.x_right, at.x_left, at.x)):
                put(
                    mine_b.at[g, i],
                    first_b[g, x].astype(wide) + mine(x, zf, lanes_b)[...].astype(wide),
                )
                if i == 0:
                    go(mine_b.at[g, 0, :, pl.ds(0, HALF // 2)], second_b.at[g, 0], 12, at.right)
                    go(mine_b.at[g, 0, :, pl.ds(HALF // 2, HALF // 2)], second_b.at[g, 1], 13, at.left)
                if i == 1:
                    go(mine_b.at[g, 1, :, pl.ds(HALF // 2, HALF // 2)], second_b.at[g, 2], 14, at.right)
                if i == 2:
                    go(mine_b.at[g, 2, :, pl.ds(0, HALF // 2)], second_b.at[g, 3], 15, at.left)

        def third():
            come(second_a.at[g, 0], 4)
            come(second_a.at[g, 1], 2)
            come(second_a.at[g, 2], 3)
            come(second_a.at[g, 3], 5)
            sums = [
                second_a[g, z].astype(wide)
                + second_a[g, 2 + z].astype(wide)
                + mine(at.x, z, lanes_a)[...].astype(wide)
                for z in range(2)
            ]
            keep = jnp.where(zf == 0, sums[0], sums[1])
            give = jnp.where(zf == 0, sums[1], sums[0])
            put(third_a.at[g, 2], give)
            go(third_a.at[g, 2], third_a.at[g, 3], 6, at.across)
            put(total.at[g, :, pl.ds(0, HALF)], keep)
            come(second_b.at[g, 0], 12)
            put(
                second_b.at[g, 4],
                second_b[g, 0].astype(wide) + mine_b[g, 1, :, pl.ds(0, HALF // 2)].astype(wide),
            )
            go(second_b.at[g, 4], second_b.at[g, 6], 16, at.right)
            come(second_b.at[g, 1], 13)
            put(
                second_b.at[g, 5],
                second_b[g, 1].astype(wide) + mine_b[g, 2, :, pl.ds(HALF // 2, HALF // 2)].astype(wide),
            )
            go(second_b.at[g, 5], second_b.at[g, 7], 17, at.left)

        def fourth():
            come(third_a.at[g, 3], 6)
            put(
                total.at[g, :, pl.ds(0, HALF)],
                total[g, :, pl.ds(0, HALF)].astype(wide) + third_a[g, 3].astype(wide),
            )
            come(second_b.at[g, 6], 16)
            come(second_b.at[g, 2], 14)
            come(second_b.at[g, 3], 15)
            come(second_b.at[g, 7], 17)
            for i, (l, r) in enumerate(((6, 3), (2, 7))):
                put(
                    total.at[g, :, pl.ds(HALF + i * (HALF // 2), HALF // 2)],
                    second_b[g, l].astype(wide)
                    + second_b[g, r].astype(wide)
                    + mine_b[g, 3, :, pl.ds(i * (HALF // 2), HALF // 2)].astype(wide),
                )
            for i in range(LANES // CAP):
                j = g * (LANES // CAP) + i
                src = total.at[g, :, pl.ds(i * CAP, CAP)]
                dst = back.at[:, block_of(at.blk)]
                if j == 0:
                    pltpu.make_async_copy(src, dst, local_sem.at[0]).start()
                else:
                    send(src, dst, back_send.at[j, 0], back_recv.at[j, 0], owners[j], sent)

        return first, second, third, fourth

    steps = [ring(g) for g in range(GROUPS)]

    def gate_first():
        for a in range(2):
            cols = pl.ds(8 * a, 8)
            for i in range(1, N_HID):
                q = (at.hid + i) % 8
                f = q if a == 0 else q + 1 - 2 * (q % 2)
                send(
                    gate_part.at[f, cols], gate_in.at[i, cols], gate_send.at[a, i], gate_recv.at[a, i],
                    at.hid_peer(i), sent,
                )

    def gate_second():
        for a in range(2):
            cols = pl.ds(8 * a, 8)
            value = gate_part[at.home(a), cols]
            for i in range(1, N_HID):
                arrived(gate_in.at[i, cols], gate_send.at[a, i], gate_recv.at[a, i], at.across)
                value = value + gate_in[i, cols]
            gate_sum[cols] = value
        for j in range(N_BLK):
            src, dst = gate_sum.at[j], gate_back.at[at.blk]
            if j == 0:
                pltpu.make_async_copy(src, dst, local_sem.at[1]).start()
            else:
                send(src, dst, back_send.at[j, 1], back_recv.at[j, 1], owners[j], sent)

    for tick in range(GROUPS + 3):
        for k in range(4):
            if 0 <= tick - k < GROUPS:
                steps[tick - k][k]()
        if tick == 0:
            gate_first()
        if tick == 2:
            gate_second()
    for j in range(N_BLK):
        e = at.later(j)
        if j == 0:
            pltpu.make_async_copy(total.at[0, :, pl.ds(0, CAP)], back.at[:, block_of(e)], local_sem.at[0]).wait()
            pltpu.make_async_copy(gate_sum.at[0], gate_back.at[e], local_sem.at[1]).wait()
        else:
            arrived(back.at[:, block_of(e)], back_send.at[j, 0], back_recv.at[j, 0], at.across)
            arrived(gate_back.at[e], back_send.at[j, 1], back_recv.at[j, 1], at.across)
    for copy in sent:
        copy.wait_send()


def combine(part, gate_part):
    vmem = pl.BlockSpec(memory_space=pltpu.VMEM)
    bf16, f32 = jnp.bfloat16, jnp.float32
    return pl.pallas_call(
        combine_kernel,
        out_shape=(
            jax.ShapeDtypeStruct((NARROW, SLOTS), bf16),
            jax.ShapeDtypeStruct((N_BLK, 2, 256), f32),
        ),
        in_specs=[vmem] * 2,
        out_specs=[vmem] * 2,
        scratch_shapes=[
            pltpu.VMEM((GROUPS, 2, NARROW, HALF), bf16),
            pltpu.VMEM((GROUPS, 4, NARROW, HALF), bf16),
            pltpu.VMEM((GROUPS, 4, NARROW, HALF), bf16),
            pltpu.VMEM((GROUPS, 4, NARROW, HALF), bf16),
            pltpu.VMEM((GROUPS, 8, NARROW, HALF // 2), bf16),
            pltpu.VMEM((GROUPS, 4, NARROW, HALF), bf16),
            pltpu.VMEM((GROUPS, NARROW, LANES), bf16),
            pltpu.VMEM((N_HID, N_BLK, 2, 256), f32),
            pltpu.VMEM((N_BLK, 2, 256), f32),
            pltpu.SemaphoreType.DMA((GROUPS, 18)),
            pltpu.SemaphoreType.DMA((GROUPS, 18)),
            pltpu.SemaphoreType.DMA((N_BLK, 2)),
            pltpu.SemaphoreType.DMA((N_BLK, 2)),
            pltpu.SemaphoreType.DMA((2, N_HID)),
            pltpu.SemaphoreType.DMA((2, N_HID)),
            pltpu.SemaphoreType.DMA((2,)),
        ],
        compiler_params=pltpu.CompilerParams(
            collective_id=1, has_side_effects=True, vmem_limit_bytes=56 * 2**20
        ),
    )(part, gate_part)


def finish_kernel(sums, grads, sums_all, grads_all, send_sem, recv_sem, local_sem):
    at = Place()
    hid_peers = [at.hid_peer(i) for i in range(1, N_HID)]
    blk_peers = [((at.blk + i) % N_BLK, at.hid) for i in range(1, N_BLK)]
    greet(hid_peers + blk_peers)
    sent = []
    keep = [
        pltpu.make_async_copy(sums, sums_all.at[at.hid], local_sem.at[0]),
        pltpu.make_async_copy(grads, grads_all.at[at.blk], local_sem.at[1]),
    ]
    for i, peer in enumerate(hid_peers):
        send(sums, sums_all.at[at.hid], send_sem.at[i], recv_sem.at[i], peer, sent)
    for i, peer in enumerate(blk_peers):
        send(grads, grads_all.at[at.blk], send_sem.at[8 + i], recv_sem.at[8 + i], peer, sent)
    for copy in keep:
        copy.start()
    for i in range(7):
        arrived(sums_all.at[(at.hid + 7 - i) % 8], send_sem.at[i], recv_sem.at[i], at.across)
    for i in range(15):
        arrived(grads_all.at[(at.blk + 15 - i) % 16], send_sem.at[8 + i], recv_sem.at[8 + i], at.across)
    for copy in keep:
        copy.wait()
    for copy in sent:
        copy.wait_send()


def finish(sums, grads):
    vmem = pl.BlockSpec(memory_space=pltpu.VMEM)
    return pl.pallas_call(
        finish_kernel,
        out_shape=(
            jax.ShapeDtypeStruct((N_HID, *sums.shape), jnp.float32),
            jax.ShapeDtypeStruct((N_BLK, *grads.shape), jnp.float32),
        ),
        in_specs=[vmem] * 2,
        out_specs=[vmem] * 2,
        scratch_shapes=[
            pltpu.SemaphoreType.DMA((23,)),
            pltpu.SemaphoreType.DMA((23,)),
            pltpu.SemaphoreType.DMA((2,)),
        ],
        compiler_params=pltpu.CompilerParams(collective_id=2, has_side_effects=True),
    )(sums, grads)


def gelu_both(values):
    square = values * values
    inner = gelu_factor * (values + gelu_cubic * values * square)
    tangent = jnp.tanh(inner)
    slope = 0.5 * (1.0 + tangent) + 0.5 * values * (1.0 - tangent * tangent) * gelu_factor * (
        1.0 + 3.0 * gelu_cubic * square
    )
    return 0.5 * values * (1.0 + tangent), slope


def on_device(
    tokens,
    cotangent,
    route_weight,
    expert_ids,
    timesteps,
    time_table,
    up_weight,
    down_weight,
    modulation_weight,
    modulation_bias,
):
    tok_count, width = tokens.shape
    f32, bf16 = jnp.float32, jnp.bfloat16
    column_first = lax.axis_index("hid") * NARROW
    image_count = timesteps.shape[0]
    per_image = tok_count // image_count

    condition = jax.nn.silu(
        jnp.concatenate(
            [lax.dynamic_slice_in_dim(time_table, timesteps[b], 1, 0) for b in range(image_count)], axis=0
        )
    )
    mod_part = (
        jnp.einsum("bi,icd->bcd", condition, modulation_weight, precision=lax.Precision.HIGHEST)
        + modulation_bias[None]
    )
    own_tok = jnp.repeat(mod_part, per_image, axis=0)
    inputs = tokens.astype(f32)
    row_mean = jnp.mean(inputs, axis=1, keepdims=True)
    spread = jnp.mean((inputs - row_mean) ** 2, axis=1, keepdims=True)
    inv_spread = 1.0 / jnp.sqrt(spread + norm_epsilon)
    own_inputs = lax.dynamic_slice_in_dim(tokens, column_first, NARROW, 1).astype(f32)
    normed_own = (own_inputs - row_mean) * inv_spread
    hin_own = (normed_own * (1.0 + own_tok[:, 1]) + own_tok[:, 0]).astype(bf16)

    experts = jnp.arange(N_BLK, dtype=jnp.int32)
    named = [(expert_ids[:, k, None] == experts[None, :]) for k in range(2)]
    both = (named[0] | named[1]).astype(bf16)
    earlier = jnp.tril(jnp.ones((tok_count, tok_count), bf16), -1)
    before = jnp.dot(earlier, both, preferred_element_type=f32)
    slot = [jnp.sum(jnp.where(n, before, 0.0), axis=1).astype(jnp.int32) for n in named]
    target = [expert_ids[:, k] * CAP + slot[k] for k in range(2)]
    slot_ids = jnp.arange(SLOTS, dtype=jnp.int32)
    hits = [(t[:, None] == slot_ids[None, :]) for t in target]
    chosen = (hits[0] | hits[1]).astype(bf16)
    weight_of_slot = jnp.sum(
        jnp.where(hits[0], route_weight[:, 0, None], 0.0) + jnp.where(hits[1], route_weight[:, 1, None], 0.0),
        axis=0,
    )

    def to_slots(values):
        return lax.dot_general(values, chosen, (((0,), (0,)), ((), ())), preferred_element_type=f32)

    px = to_slots(hin_own).astype(bf16)
    pc = (to_slots(cotangent) * weight_of_slot[None, :]).astype(bf16)
    first_count = before[per_image]
    condition_parts = condition.reshape(image_count, N_BLK, width // N_BLK).transpose(1, 0, 2)
    info = jnp.concatenate(
        [
            jnp.broadcast_to(mod_part[None, :, 2], (N_BLK, image_count, NARROW)),
            jnp.broadcast_to(first_count[:, None, None], (N_BLK, image_count, 16)),
            condition_parts,
            jnp.zeros((N_BLK, image_count, 256 - NARROW - 16 - width // N_BLK), f32),
        ],
        axis=2,
    )
    rows_in, rows_wc, table = dispatch(px, pc, info)

    up_matrix = up_weight[0]
    down_matrix = down_weight[0]
    own_table = table[lax.axis_index("hid"), :8], table[
        lax.axis_index("hid") + 1 - 2 * (lax.axis_index("hid") % 2), 8:
    ]
    own_table = jnp.concatenate(own_table, axis=0)
    first_of = own_table[:, 0, NARROW]
    is_first = jnp.arange(CAP, dtype=f32)[None, :] < first_of[:, None]
    gates = table[..., :NARROW].transpose(0, 3, 1, 2).reshape(width, N_BLK, 2)
    wc = rows_wc.reshape(width, N_BLK, CAP).astype(f32)
    gated = jnp.where(is_first[None], gates[:, :, 0, None], gates[:, :, 1, None])
    rows_cot = (gated * wc).astype(bf16).reshape(width, SLOTS)
    pre_act = lax.dot_general(up_matrix, rows_in, (((0,), (0,)), ((), ())), preferred_element_type=f32)
    act, slope = gelu_both(pre_act)
    act = act.astype(bf16)
    act_grad = jnp.dot(down_matrix, rows_cot, preferred_element_type=f32)
    pre_grad = (act_grad * slope).astype(bf16)
    up_grads = lax.dot_general(rows_in, pre_grad, (((1,), (1,)), ((), ())), preferred_element_type=f32)[None]
    down_grads = lax.dot_general(act, rows_cot, (((1,), (1,)), ((), ())), preferred_element_type=f32)[None]
    out_rows = lax.dot_general(down_matrix, act, (((0,), (0,)), ((), ())), preferred_element_type=f32)
    grad_rows = jnp.dot(up_matrix, pre_grad, preferred_element_type=f32).astype(bf16)
    product = out_rows.reshape(width, N_BLK, CAP) * wc
    of_first = jnp.sum(jnp.where(is_first[None], product, 0.0), axis=2)
    of_second = jnp.sum(jnp.where(is_first[None], 0.0, product), axis=2)
    gate_part = jnp.stack([of_first, of_second], axis=2).reshape(N_HID, NARROW, N_BLK, 2).transpose(0, 2, 3, 1)
    gate_part = jnp.pad(gate_part, ((0, 0), (0, 0), (0, 0), (0, 256 - NARROW)))
    back, gate_back = combine(grad_rows, gate_part)

    mixed_grad = lax.dot_general(chosen, back, (((1,), (1,)), ((), ())), preferred_element_type=f32)
    shift_grad = jnp.sum(mixed_grad.reshape(image_count, per_image, NARROW), axis=1)
    scale_grad = jnp.sum((mixed_grad * normed_own).reshape(image_count, per_image, NARROW), axis=1)
    gate_grad = jnp.sum(gate_back, axis=0)[:, :NARROW]
    modulation_grads = jnp.concatenate([shift_grad, scale_grad, gate_grad], axis=0)
    norm_grad = mixed_grad * (1.0 + own_tok[:, 1])
    sums = jnp.stack([jnp.sum(norm_grad, axis=1), jnp.sum(norm_grad * normed_own, axis=1)])
    sums_all, grads_all = finish(
        jnp.pad(sums, ((0, 6), (0, 0))), jnp.pad(modulation_grads, ((0, 2), (0, 256 - NARROW)))
    )
    means = jnp.sum(sums_all[:, :2], axis=0) / width
    token_grads = (
        cotangent.astype(f32) + inv_spread * (norm_grad - means[0][:, None] - normed_own * means[1][:, None])
    ).astype(bf16)
    image_grads = grads_all[:, :6, :NARROW].reshape(N_BLK, 3, image_count, NARROW)
    at_blk = lax.axis_index("blk")
    order = jnp.array([shift(j) for j in range(N_BLK)], jnp.int32)
    sources = (at_blk // 8 + order[:, 0]) % 2 * 8 + (at_blk % 8 + 8 - order[:, 1]) % 8
    conditions = own_table[:, :, NARROW + 16 : NARROW + 16 + width // N_BLK]
    modulation_weight_grads = jnp.einsum(
        "jbi,jcbd->icd", conditions, image_grads[sources], precision=lax.Precision.HIGHEST
    )
    modulation_bias_grads = jnp.sum(image_grads, axis=(0, 2))
    return (token_grads, up_grads, down_grads, modulation_weight_grads, modulation_bias_grads)


def solution(mesh):
    in_specs = (
        P("blk", None),
        P("blk", "hid"),
        P("blk", None),
        P("blk", None),
        P("blk"),
        P(),
        P("blk", None, "hid"),
        P("blk", "hid", None),
        P(None, None, "hid"),
        P(None, "hid"),
    )
    out_specs = (
        P("blk", "hid"),
        P("blk", None, "hid"),
        P("blk", "hid", None),
        P("blk", None, "hid"),
        P(None, "hid"),
    )
    return jax.shard_map(
        on_device, mesh=mesh, in_specs=in_specs, out_specs=out_specs, check_vma=False
    )
```

```python
import math

import jax
import jax.numpy as jnp
from jax import lax
from jax.experimental import pallas as pl
from jax.experimental.pallas import tpu as pltpu
from jax.sharding import PartitionSpec as P

MESH = pl.DeviceIdType.MESH
norm_epsilon = 1e-06
gelu_cubic = 0.044715
gelu_factor = math.sqrt(2.0 / math.pi)

N_BLK, N_HID = 16, 8
WIDTH, NARROW, CAP = 1152, 144, 128
SLOTS = N_BLK * CAP
GROUPS = 4
LANES = SLOTS // GROUPS
HALF = LANES // 2
ORDER = (0, 1, 6, 2, 7, 3, 5, 4)


def shift(j):
    return j // 8, ORDER[j % 8]


class Place:
    def __init__(self):
        self.blk = lax.axis_index("blk")
        self.hid = lax.axis_index("hid")
        self.z_hi, self.m = self.blk // 8, self.blk % 8
        self.x, self.z_lo = self.hid // 2, self.hid % 2
        self.x_right, self.x_left, self.x_far = [(self.x + i) % 4 for i in (1, 3, 2)]
        self.right = (self.blk, self.x_right * 2 + self.z_lo)
        self.left = (self.blk, self.x_left * 2 + self.z_lo)
        self.across = (self.blk, self.home(1))

    def home(self, a):
        return self.hid if a == 0 else self.hid + 1 - 2 * self.z_lo

    def later(self, j):
        a, m = shift(j)
        return (self.z_hi + a) % 2 * 8 + (self.m + m) % 8

    def earlier(self, j):
        a, m = shift(j)
        return (self.z_hi + a) % 2 * 8 + (self.m + 8 - m) % 8

    def hid_peer(self, i):
        return (self.blk, (self.hid + i) % 8)


def greet(devices):
    barrier = pltpu.get_barrier_semaphore()
    for device in devices:
        pl.semaphore_signal(barrier, inc=1, device_id=device, device_id_type=MESH)
    pl.semaphore_wait(barrier, len(devices))


def send(src, dst, send_sem, recv_sem, device, sent):
    copy = pltpu.make_async_remote_copy(
        src_ref=src, dst_ref=dst, send_sem=send_sem, recv_sem=recv_sem, device_id=device, device_id_type=MESH
    )
    copy.start()
    sent.append(copy)


def arrived(region, send_sem, recv_sem, device):
    pltpu.make_async_remote_copy(
        src_ref=region, dst_ref=region, send_sem=send_sem, recv_sem=recv_sem, device_id=device, device_id_type=MESH
    ).wait_recv()


def rows_of(slice_index, count=1):
    return pl.ds(pl.multiple_of(slice_index * NARROW, 16), count * NARROW)


def block_of(index):
    return pl.ds(pl.multiple_of(index * CAP, CAP), CAP)


def gelu_both(values):
    square = values * values
    inner = gelu_factor * (values + gelu_cubic * values * square)
    tangent = jnp.tanh(inner)
    slope = 0.5 * (1.0 + tangent) + 0.5 * values * (1.0 - tangent * tangent) * gelu_factor * (
        1.0 + 3.0 * gelu_cubic * square
    )
    return 0.5 * values * (1.0 + tangent), slope


def dot(a, b, contract=(1, 0), precision=None):
    return lax.dot_general(
        a, b, (((contract[0],), (contract[1],)), ((), ())), precision=precision, preferred_element_type=jnp.float32
    )


def expert_kernel(
    px, pc, info, up, down,
    back, gate_back, own_info, up_grads, down_grads,
    xt, ct, hcot, act, pre_grad, part, up_t, down_t, table, gate_rows, gate_part,
    first_a, second_a, third_a, first_b, second_b, mine_b, total, gate_in, gate_sum, gate_out,
    a2a_send, a2a_recv, ring_send, ring_recv, info_send, info_recv,
    sum_send, sum_recv, back_send, back_recv, gate_send, gate_recv, local_sem,
):
    at = Place()
    wide = jnp.float32
    peers = [(at.later(j), at.home(j // 8)) for j in range(N_BLK)]
    owners = [(at.earlier(j), at.home(j // 8)) for j in range(N_BLK)]
    greet(peers[1:] + [at.hid_peer(i) for i in range(1, N_HID)])
    own = rows_of(at.hid)
    sent = []
    local = []
    for i in (2, 0, 1):
        for j in range(N_BLK):
            lanes = pl.ds(j * CAP, CAP)
            target = at.later(j)
            src, dst = (
                (px.at[:, block_of(target)], xt.at[own, lanes]),
                (pc.at[:, block_of(target)], ct.at[own, lanes]),
                (info.at[target], table.at[at.hid, j]),
            )[i]
            if j == 0:
                copy = pltpu.make_async_copy(src, dst, local_sem.at[i])
                copy.start()
                local.append((i, copy))
            else:
                send(src, dst, a2a_send.at[j, i], a2a_recv.at[j, i], peers[j], sent)
    local = dict(local)

    def from_peer(j, i, region):
        if j == 0:
            local[i].wait()
        else:
            arrived(region, a2a_send.at[j, i], a2a_recv.at[j, i], peers[j])

    def put(ref, value):
        ref[...] = value.astype(ref.dtype)

    def spread(g):
        a = g // (GROUPS // 2)
        f = at.home(a)
        other = at.home(1 - a)
        zf = f % 2
        lanes = pl.ds(g * LANES, LANES)
        halves = [pl.ds(g * LANES + i * HALF, HALF) for i in range(2)]
        far_slice = at.x_far * 2 + zf

        def go(array, rows, cols, k, device):
            region = array.at[rows, cols]
            send(region, region, ring_send.at[g, k], ring_recv.at[g, k], device, sent)

        def come(array, rows, cols, k):
            arrived(array.at[rows, cols], ring_send.at[g, k], ring_recv.at[g, k], at.across)

        def first():
            for j in range(g * LANES // CAP, (g + 1) * LANES // CAP):
                from_peer(j, 0, xt.at[rows_of(f), pl.ds(j * CAP, CAP)])
                from_peer(j, 1, ct.at[rows_of(f), pl.ds(j * CAP, CAP)])
            go(xt, rows_of(f), lanes, 0, at.across)
            go(ct, rows_of(f), lanes, 6, at.right)
            go(ct, rows_of(f), lanes, 7, at.left)
            go(ct, rows_of(f), lanes, 5, at.across)

        def second():
            come(xt, rows_of(other), lanes, 0)
            go(xt, rows_of(at.x * 2, 2), lanes, 1, at.right)
            go(xt, rows_of(at.x * 2, 2), lanes, 2, at.left)
            left, right = rows_of(at.x_left * 2 + zf), rows_of(at.x_right * 2 + zf)
            come(ct, left, lanes, 6)
            go(ct, left, halves[0], 8, at.right)
            go(ct, left, lanes, 10, at.across)
            come(ct, right, lanes, 7)
            go(ct, right, halves[1], 9, at.left)
            go(ct, right, lanes, 11, at.across)

        def third():
            come(xt, rows_of(at.x_left * 2, 2), lanes, 1)
            go(xt, rows_of(at.x_left * 2), lanes, 3, at.right)
            come(xt, rows_of(at.x_right * 2, 2), lanes, 2)
            go(xt, rows_of(at.x_right * 2 + 1), lanes, 4, at.left)
            for i in range(2):
                come(ct, rows_of(far_slice), halves[i], 8 + i)
                go(ct, rows_of(far_slice), halves[i], 12 + i, at.across)

        def fourth():
            come(xt, rows_of(at.x_far * 2), lanes, 3)
            come(xt, rows_of(at.x_far * 2 + 1), lanes, 4)
            come(ct, rows_of(other), lanes, 5)
            come(ct, rows_of(at.x_left * 2 + 1 - zf), lanes, 10)
            come(ct, rows_of(at.x_right * 2 + 1 - zf), lanes, 11)
            for i in range(2):
                come(ct, rows_of(at.x_far * 2 + 1 - zf), halves[i], 12 + i)

        return first, second, third, fourth

    def spread_info():
        for a in range(2):
            f = at.home(a)
            for j in range(8 * a, 8 * a + 8):
                from_peer(j, 2, table.at[f, j])
            half = table.at[f, pl.ds(8 * a, 8)]
            for i in range(1, N_HID):
                send(half, half, info_send.at[a, i], info_recv.at[a, i], at.hid_peer(i), sent)

    def gather_info():
        for a in range(2):
            for i in range(1, N_HID):
                q = (at.hid + 8 - i) % 8
                f = q if a == 0 else q + 1 - 2 * (q % 2)
                arrived(table.at[f, pl.ds(8 * a, 8)], info_send.at[a, i], info_recv.at[a, i], at.across)
        for j in range(N_BLK):
            own_info[j] = table[at.home(j // 8), j]
            for f in range(N_HID):
                gate_rows[f, pl.ds(2 * j, 2)] = table[f, j]

    def image_of_lane(g):
        shape = (2 * N_BLK, LANES)
        row = lax.broadcasted_iota(jnp.int32, shape, 0)
        lane = lax.broadcasted_iota(jnp.int32, shape, 1)
        counts = gate_rows[0, :, pl.ds(128, 128)][:, 16:17].astype(jnp.int32)
        block = lane // CAP + g * (LANES // CAP)
        is_first = (lane % CAP) < counts
        return jnp.where((row // 2 == block) & (is_first == (row % 2 == 0)), 1.0, 0.0).astype(wide)

    def forward(g):
        lanes = pl.ds(g * LANES, LANES)
        images = image_of_lane(g)

        @pl.loop(0, N_HID)
        def _(f):
            gates = dot(gate_rows[f], images, (0, 0), lax.Precision.HIGHEST)[:NARROW]
            rows = rows_of(f)
            hcot[rows, lanes] = (gates * ct[rows, lanes].astype(wide)).astype(hcot.dtype)

        @pl.loop(0, 3)
        def _(i):
            rows = pl.ds(pl.multiple_of(i * 192, 64), 192)
            activated, slope = gelu_both(dot(up_t[rows, :], xt[:, lanes]))
            act[rows, :] = activated.astype(act.dtype)
            pre_grad[rows, :] = (dot(down[rows, :], hcot[:, lanes]) * slope).astype(pre_grad.dtype)

        @pl.loop(0, 4)
        def _(i):
            rows = rows_of(2 * i, 2)
            part[rows, lanes] = dot(up[rows, :], pre_grad[...]).astype(part.dtype)

    def gates_of(g):
        lanes = pl.ds(g * LANES, LANES)
        images = image_of_lane(g).astype(jnp.bfloat16)

        @pl.loop(0, 4)
        def _(i):
            rows = rows_of(2 * i, 2)
            product = (dot(down_t[rows, :], act[...]) * ct[rows, lanes].astype(wide)).astype(jnp.bfloat16)
            for k in range(2):
                value = dot(images, product[k * NARROW : (k + 1) * NARROW], (1, 1))
                index = 2 * i + k
                if g == 0:
                    gate_part[index, :, pl.ds(0, NARROW)] = value
                else:
                    gate_part[index, :, pl.ds(0, NARROW)] += value

    def up_weights(g):
        lanes = pl.ds(g * LANES, LANES)

        @pl.loop(0, 4)
        def _(i):
            rows = rows_of(2 * i, 2)
            value = dot(xt[rows, lanes], pre_grad[...], (1, 1))
            if g == 0:
                up_grads[rows, :] = value
            else:
                up_grads[rows, :] += value

    def down_weights(g):
        lanes = pl.ds(g * LANES, LANES)

        @pl.loop(0, 3)
        def _(i):
            rows = pl.ds(pl.multiple_of(i * 192, 64), 192)
            value = dot(act[rows, :], hcot[:, lanes], (1, 1))
            if g == 0:
                down_grads[rows, :] = value
            else:
                down_grads[rows, :] += value

    def reduce(g):
        a = g // (GROUPS // 2)
        zf = at.home(a) % 2
        lanes_a = pl.ds(g * LANES, HALF)
        lanes_b = pl.ds(g * LANES + HALF, HALF)

        def mine(x, z, lanes):
            return part.at[rows_of(x * 2 + z), lanes]

        def go(src, dst, k, device):
            send(src, dst, sum_send.at[g, k], sum_recv.at[g, k], device, sent)

        def come(region, k):
            arrived(region, sum_send.at[g, k], sum_recv.at[g, k], at.across)

        def first():
            for x in range(4):
                go(mine(x, 1 - zf, lanes_b), first_b.at[g, x], 8 + x, at.across)
            go(mine(at.x_far, 0, lanes_a), first_a.at[g, 0], 0, at.right)
            go(mine(at.x_far, 1, lanes_a), first_a.at[g, 1], 1, at.left)
            go(mine(at.x_right, 1, lanes_a), second_a.at[g, 1], 2, at.right)
            go(mine(at.x_left, 0, lanes_a), second_a.at[g, 2], 3, at.left)

        def second():
            come(first_a.at[g, 0], 0)
            put(
                third_a.at[g, 0],
                first_a[g, 0].astype(wide) + mine(at.x_right, 0, lanes_a)[...].astype(wide),
            )
            go(third_a.at[g, 0], second_a.at[g, 0], 4, at.right)
            come(first_a.at[g, 1], 1)
            put(
                third_a.at[g, 1],
                first_a[g, 1].astype(wide) + mine(at.x_left, 1, lanes_a)[...].astype(wide),
            )
            go(third_a.at[g, 1], second_a.at[g, 3], 5, at.left)
            for x in range(4):
                come(first_b.at[g, x], 8 + x)
            for i, x in enumerate((at.x_far, at.x_right, at.x_left, at.x)):
                put(
                    mine_b.at[g, i],
                    first_b[g, x].astype(wide) + mine(x, zf, lanes_b)[...].astype(wide),
                )
                if i == 0:
                    go(mine_b.at[g, 0, :, pl.ds(0, HALF // 2)], second_b.at[g, 0], 12, at.right)
                    go(mine_b.at[g, 0, :, pl.ds(HALF // 2, HALF // 2)], second_b.at[g, 1], 13, at.left)
                if i == 1:
                    go(mine_b.at[g, 1, :, pl.ds(HALF // 2, HALF // 2)], second_b.at[g, 2], 14, at.right)
                if i == 2:
                    go(mine_b.at[g, 2, :, pl.ds(0, HALF // 2)], second_b.at[g, 3], 15, at.left)

        def third():
            come(second_a.at[g, 0], 4)
            come(second_a.at[g, 1], 2)
            come(second_a.at[g, 2], 3)
            come(second_a.at[g, 3], 5)
            sums = [
                second_a[g, z].astype(wide)
                + second_a[g, 2 + z].astype(wide)
                + mine(at.x, z, lanes_a)[...].astype(wide)
                for z in range(2)
            ]
            keep = jnp.where(zf == 0, sums[0], sums[1])
            give = jnp.where(zf == 0, sums[1], sums[0])
            put(third_a.at[g, 2], give)
            go(third_a.at[g, 2], third_a.at[g, 3], 6, at.across)
            put(total.at[g, :, pl.ds(0, HALF)], keep)
            come(second_b.at[g, 0], 12)
            put(
                second_b.at[g, 4],
                second_b[g, 0].astype(wide) + mine_b[g, 1, :, pl.ds(0, HALF // 2)].astype(wide),
            )
            go(second_b.at[g, 4], second_b.at[g, 6], 16, at.right)
            come(second_b.at[g, 1], 13)
            put(
                second_b.at[g, 5],
                second_b[g, 1].astype(wide) + mine_b[g, 2, :, pl.ds(HALF // 2, HALF // 2)].astype(wide),
            )
            go(second_b.at[g, 5], second_b.at[g, 7], 17, at.left)

        def fourth():
            come(third_a.at[g, 3], 6)
            put(
                total.at[g, :, pl.ds(0, HALF)],
                total[g, :, pl.ds(0, HALF)].astype(wide) + third_a[g, 3].astype(wide),
            )
            come(second_b.at[g, 6], 16)
            come(second_b.at[g, 2], 14)
            come(second_b.at[g, 3], 15)
            come(second_b.at[g, 7], 17)
            for i, (l, r) in enumerate(((6, 3), (2, 7))):
                put(
                    total.at[g, :, pl.ds(HALF + i * (HALF // 2), HALF // 2)],
                    second_b[g, l].astype(wide)
                    + second_b[g, r].astype(wide)
                    + mine_b[g, 3, :, pl.ds(i * (HALF // 2), HALF // 2)].astype(wide),
                )
            for i in range(LANES // CAP):
                j = g * (LANES // CAP) + i
                src = total.at[g, :, pl.ds(i * CAP, CAP)]
                dst = back.at[:, block_of(at.blk)]
                if j == 0:
                    pltpu.make_async_copy(src, dst, local_sem.at[3]).start()
                else:
                    send(src, dst, back_send.at[j, 0], back_recv.at[j, 0], owners[j], sent)

        return first, second, third, fourth

    def gate_first():
        for a in range(2):
            rows = pl.ds(16 * a, 16)
            for i in range(1, N_HID):
                q = (at.hid + i) % 8
                f = q if a == 0 else q + 1 - 2 * (q % 2)
                send(
                    gate_part.at[f, rows], gate_in.at[i, rows], gate_send.at[a, i], gate_recv.at[a, i],
                    at.hid_peer(i), sent,
                )

    def gate_second():
        for a in range(2):
            rows = pl.ds(16 * a, 16)
            value = gate_part[at.home(a), rows]
            for i in range(1, N_HID):
                arrived(gate_in.at[i, rows], gate_send.at[a, i], gate_recv.at[a, i], at.across)
                value = value + gate_in[i, rows]
            gate_sum[rows] = value
        for j in range(N_BLK):
            gate_out[j] = gate_sum[pl.ds(2 * j, 2)]
            src, dst = gate_out.at[j], gate_back.at[at.blk]
            if j == 0:
                pltpu.make_async_copy(src, dst, local_sem.at[4]).start()
            else:
                send(src, dst, back_send.at[j, 1], back_recv.at[j, 1], owners[j], sent)

    gate_part[...] = jnp.zeros_like(gate_part)

    @pl.loop(0, 9)
    def _(i):
        tile = pl.ds(pl.multiple_of(i * 128, 128), 128)
        up_t[:, tile] = up[tile, :].T
        down_t[tile, :] = down[:, tile].T

    spreads = [spread(g) for g in range(GROUPS)]
    reduces = [reduce(g) for g in range(GROUPS)]
    for tick in range(GROUPS + 6):
        for k in range(4):
            if 0 <= tick - k < GROUPS:
                spreads[tick - k][k]()
            if tick == 0 and k == 0:
                spread_info()
        done = tick - 3
        if done == 0:
            gather_info()
        if 0 <= done < GROUPS:
            forward(done)
            reduces[done][0]()
        for k in range(1, 4):
            if 0 <= done - k < GROUPS:
                reduces[done - k][k]()
        if 0 <= done < GROUPS:
            gates_of(done)
            if done == GROUPS - 1:
                gate_first()
            up_weights(done)
            down_weights(done)
        if done == GROUPS:
            gate_second()
    for j in range(N_BLK):
        e = at.later(j)
        if j == 0:
            pltpu.make_async_copy(total.at[0, :, pl.ds(0, CAP)], back.at[:, block_of(e)], local_sem.at[3]).wait()
            pltpu.make_async_copy(gate_out.at[0], gate_back.at[e], local_sem.at[4]).wait()
        else:
            arrived(back.at[:, block_of(e)], back_send.at[j, 0], back_recv.at[j, 0], at.across)
            arrived(gate_back.at[e], back_send.at[j, 1], back_recv.at[j, 1], at.across)
    for copy in sent:
        copy.wait_send()


def run_experts(px, pc, info, up, down):
    vmem = pl.BlockSpec(memory_space=pltpu.VMEM)
    bf16, f32 = jnp.bfloat16, jnp.float32
    width, hidden = up.shape
    dma = pltpu.SemaphoreType.DMA
    return pl.pallas_call(
        expert_kernel,
        out_shape=(
            jax.ShapeDtypeStruct((NARROW, SLOTS), bf16),
            jax.ShapeDtypeStruct((N_BLK, 2, 256), f32),
            jax.ShapeDtypeStruct((N_BLK, 2, 256), f32),
            jax.ShapeDtypeStruct((width, hidden), f32),
            jax.ShapeDtypeStruct((hidden, width), f32),
        ),
        in_specs=[vmem] * 5,
        out_specs=[vmem] * 5,
        scratch_shapes=[
            pltpu.VMEM((width, SLOTS), bf16),
            pltpu.VMEM((width, SLOTS), bf16),
            pltpu.VMEM((width, SLOTS), bf16),
            pltpu.VMEM((hidden, LANES), bf16),
            pltpu.VMEM((hidden, LANES), bf16),
            pltpu.VMEM((width, SLOTS), bf16),
            pltpu.VMEM((hidden, width), bf16),
            pltpu.VMEM((width, hidden), bf16),
            pltpu.VMEM((N_HID, N_BLK, 2, 256), f32),
            pltpu.VMEM((N_HID, 2 * N_BLK, 256), f32),
            pltpu.VMEM((N_HID, 2 * N_BLK, 256), f32),
            pltpu.VMEM((GROUPS, 2, NARROW, HALF), bf16),
            pltpu.VMEM((GROUPS, 4, NARROW, HALF), bf16),
            pltpu.VMEM((GROUPS, 4, NARROW, HALF), bf16),
            pltpu.VMEM((GROUPS, 4, NARROW, HALF), bf16),
            pltpu.VMEM((GROUPS, 8, NARROW, HALF // 2), bf16),
            pltpu.VMEM((GROUPS, 4, NARROW, HALF), bf16),
            pltpu.VMEM((GROUPS, NARROW, LANES), bf16),
            pltpu.VMEM((N_HID, 2 * N_BLK, 256), f32),
            pltpu.VMEM((2 * N_BLK, 256), f32),
            pltpu.VMEM((N_BLK, 2, 256), f32),
            dma((N_BLK, 3)),
            dma((N_BLK, 3)),
            dma((GROUPS, 14)),
            dma((GROUPS, 14)),
            dma((2, N_HID)),
            dma((2, N_HID)),
            dma((GROUPS, 18)),
            dma((GROUPS, 18)),
            dma((N_BLK, 2)),
            dma((N_BLK, 2)),
            dma((2, N_HID)),
            dma((2, N_HID)),
            dma((5,)),
        ],
        compiler_params=pltpu.CompilerParams(
            collective_id=0, has_side_effects=True, vmem_limit_bytes=60 * 2**20
        ),
    )(px, pc, info, up, down)


def finish_kernel(sums, grads, sums_all, grads_all, send_sem, recv_sem, local_sem):
    at = Place()
    hid_peers = [at.hid_peer(i) for i in range(1, N_HID)]
    blk_peers = [((at.blk + i) % N_BLK, at.hid) for i in range(1, N_BLK)]
    greet(hid_peers + blk_peers)
    sent = []
    keep = [
        pltpu.make_async_copy(sums, sums_all.at[at.hid], local_sem.at[0]),
        pltpu.make_async_copy(grads, grads_all.at[at.blk], local_sem.at[1]),
    ]
    for i, peer in enumerate(hid_peers):
        send(sums, sums_all.at[at.hid], send_sem.at[i], recv_sem.at[i], peer, sent)
    for i, peer in enumerate(blk_peers):
        send(grads, grads_all.at[at.blk], send_sem.at[8 + i], recv_sem.at[8 + i], peer, sent)
    for copy in keep:
        copy.start()
    for i in range(7):
        arrived(sums_all.at[(at.hid + 7 - i) % 8], send_sem.at[i], recv_sem.at[i], at.across)
    for i in range(15):
        arrived(grads_all.at[(at.blk + 15 - i) % 16], send_sem.at[8 + i], recv_sem.at[8 + i], at.across)
    for copy in keep:
        copy.wait()
    for copy in sent:
        copy.wait_send()


def finish(sums, grads):
    vmem = pl.BlockSpec(memory_space=pltpu.VMEM)
    return pl.pallas_call(
        finish_kernel,
        out_shape=(
            jax.ShapeDtypeStruct((N_HID, *sums.shape), jnp.float32),
            jax.ShapeDtypeStruct((N_BLK, *grads.shape), jnp.float32),
        ),
        in_specs=[vmem] * 2,
        out_specs=[vmem] * 2,
        scratch_shapes=[
            pltpu.SemaphoreType.DMA((23,)),
            pltpu.SemaphoreType.DMA((23,)),
            pltpu.SemaphoreType.DMA((2,)),
        ],
        compiler_params=pltpu.CompilerParams(collective_id=1, has_side_effects=True),
    )(sums, grads)


def on_device(
    tokens,
    cotangent,
    route_weight,
    expert_ids,
    timesteps,
    time_table,
    up_weight,
    down_weight,
    modulation_weight,
    modulation_bias,
):
    tok_count, width = tokens.shape
    f32, bf16 = jnp.float32, jnp.bfloat16
    column_first = lax.axis_index("hid") * NARROW
    image_count = timesteps.shape[0]
    per_image = tok_count // image_count

    condition = jax.nn.silu(
        jnp.concatenate(
            [lax.dynamic_slice_in_dim(time_table, timesteps[b], 1, 0) for b in range(image_count)], axis=0
        )
    )
    mod_part = (
        jnp.einsum("bi,icd->bcd", condition, modulation_weight, precision=lax.Precision.HIGHEST)
        + modulation_bias[None]
    )
    own_tok = jnp.repeat(mod_part, per_image, axis=0)
    inputs = tokens.astype(f32)
    row_mean = jnp.mean(inputs, axis=1, keepdims=True)
    spread = jnp.mean((inputs - row_mean) ** 2, axis=1, keepdims=True)
    inv_spread = 1.0 / jnp.sqrt(spread + norm_epsilon)
    own_inputs = lax.dynamic_slice_in_dim(tokens, column_first, NARROW, 1).astype(f32)
    normed_own = (own_inputs - row_mean) * inv_spread
    hin_own = (normed_own * (1.0 + own_tok[:, 1]) + own_tok[:, 0]).astype(bf16)

    experts = jnp.arange(N_BLK, dtype=jnp.int32)
    named = [(expert_ids[:, k, None] == experts[None, :]) for k in range(2)]
    both = (named[0] | named[1]).astype(bf16)
    earlier = jnp.tril(jnp.ones((tok_count, tok_count), bf16), -1)
    before = jnp.dot(earlier, both, preferred_element_type=f32)
    slot = [jnp.sum(jnp.where(n, before, 0.0), axis=1).astype(jnp.int32) for n in named]
    target = [expert_ids[:, k] * CAP + slot[k] for k in range(2)]
    slot_ids = jnp.arange(SLOTS, dtype=jnp.int32)
    hits = [(t[:, None] == slot_ids[None, :]) for t in target]
    chosen = (hits[0] | hits[1]).astype(bf16)
    weight_of_slot = jnp.sum(
        jnp.where(hits[0], route_weight[:, 0, None], 0.0) + jnp.where(hits[1], route_weight[:, 1, None], 0.0),
        axis=0,
    )

    def to_slots(values):
        return lax.dot_general(values, chosen, (((0,), (0,)), ((), ())), preferred_element_type=f32)

    px = to_slots(hin_own).astype(bf16)
    pc = (to_slots(cotangent) * weight_of_slot[None, :]).astype(bf16)
    first_count = before[per_image]
    condition_parts = condition.reshape(image_count, N_BLK, width // N_BLK).transpose(1, 0, 2)
    info = jnp.concatenate(
        [
            jnp.broadcast_to(mod_part[None, :, 2], (N_BLK, image_count, NARROW)),
            jnp.broadcast_to(first_count[:, None, None], (N_BLK, image_count, 16)),
            condition_parts,
            jnp.zeros((N_BLK, image_count, 256 - NARROW - 16 - width // N_BLK), f32),
        ],
        axis=2,
    )
    back, gate_back, own_info, up_grads, down_grads = run_experts(px, pc, info, up_weight[0], down_weight[0])

    mixed_grad = lax.dot_general(chosen, back, (((1,), (1,)), ((), ())), preferred_element_type=f32)
    shift_grad = jnp.sum(mixed_grad.reshape(image_count, per_image, NARROW), axis=1)
    scale_grad = jnp.sum((mixed_grad * normed_own).reshape(image_count, per_image, NARROW), axis=1)
    gate_grad = jnp.sum(gate_back, axis=0)[:, :NARROW]
    modulation_grads = jnp.concatenate([shift_grad, scale_grad, gate_grad], axis=0)
    norm_grad = mixed_grad * (1.0 + own_tok[:, 1])
    sums = jnp.stack([jnp.sum(norm_grad, axis=1), jnp.sum(norm_grad * normed_own, axis=1)])
    sums_all, grads_all = finish(
        jnp.pad(sums, ((0, 6), (0, 0))), jnp.pad(modulation_grads, ((0, 2), (0, 256 - NARROW)))
    )
    means = jnp.sum(sums_all[:, :2], axis=0) / width
    token_grads = (
        cotangent.astype(f32) + inv_spread * (norm_grad - means[0][:, None] - normed_own * means[1][:, None])
    ).astype(bf16)
    image_grads = grads_all[:, :6, :NARROW].reshape(N_BLK, 3, image_count, NARROW)
    at_blk = lax.axis_index("blk")
    order = jnp.array([shift(j) for j in range(N_BLK)], jnp.int32)
    sources = (at_blk // 8 + order[:, 0]) % 2 * 8 + (at_blk % 8 + 8 - order[:, 1]) % 8
    conditions = own_info[:, :, NARROW + 16 : NARROW + 16 + width // N_BLK]
    modulation_weight_grads = jnp.einsum(
        "jbi,jcbd->icd", conditions, image_grads[sources], precision=lax.Precision.HIGHEST
    )
    modulation_bias_grads = jnp.sum(image_grads, axis=(0, 2))
    return (token_grads, up_grads[None], down_grads[None], modulation_weight_grads, modulation_bias_grads)


def solution(mesh):
    in_specs = (
        P("blk", None),
        P("blk", "hid"),
        P("blk", None),
        P("blk", None),
        P("blk"),
        P(),
        P("blk", None, "hid"),
        P("blk", "hid", None),
        P(None, None, "hid"),
        P(None, "hid"),
    )
    out_specs = (
        P("blk", "hid"),
        P("blk", None, "hid"),
        P("blk", "hid", None),
        P("blk", None, "hid"),
        P(None, "hid"),
    )
    return jax.shard_map(
        on_device, mesh=mesh, in_specs=in_specs, out_specs=out_specs, check_vma=False
    )
```

```python
import math

import jax
import jax.numpy as jnp
from jax import lax
from jax.experimental import pallas as pl
from jax.experimental.pallas import tpu as pltpu
from jax.sharding import PartitionSpec as P

MESH = pl.DeviceIdType.MESH
norm_epsilon = 1e-06
gelu_cubic = 0.044715
gelu_factor = math.sqrt(2.0 / math.pi)

N_BLK, N_HID = 16, 8
WIDTH, NARROW, CAP = 1152, 144, 128
TOKENS, PATCHES = 512, 256
SLOTS = N_BLK * CAP
GROUPS = 4
LANES = SLOTS // GROUPS
HALF = LANES // 2
ORDER = (0, 1, 6, 2, 7, 3, 5, 4)


def shift(j):
    return j // 8, ORDER[j % 8]


class Place:
    def __init__(self):
        self.blk = lax.axis_index("blk")
        self.hid = lax.axis_index("hid")
        self.z_hi, self.m = self.blk // 8, self.blk % 8
        self.x, self.z_lo = self.hid // 2, self.hid % 2
        self.x_right, self.x_left, self.x_far = [(self.x + i) % 4 for i in (1, 3, 2)]
        self.right = (self.blk, self.x_right * 2 + self.z_lo)
        self.left = (self.blk, self.x_left * 2 + self.z_lo)
        self.across = (self.blk, self.home(1))

    def home(self, a):
        return self.hid if a == 0 else self.hid + 1 - 2 * self.z_lo

    def later(self, j):
        a, m = shift(j)
        return (self.z_hi + a) % 2 * 8 + (self.m + m) % 8

    def earlier(self, j):
        a, m = shift(j)
        return (self.z_hi + a) % 2 * 8 + (self.m + 8 - m) % 8

    def hid_peer(self, i):
        return (self.blk, (self.hid + i) % 8)


def greet(devices):
    barrier = pltpu.get_barrier_semaphore()
    for device in devices:
        pl.semaphore_signal(barrier, inc=1, device_id=device, device_id_type=MESH)
    pl.semaphore_wait(barrier, len(devices))


def send(src, dst, send_sem, recv_sem, device, sent):
    copy = pltpu.make_async_remote_copy(
        src_ref=src, dst_ref=dst, send_sem=send_sem, recv_sem=recv_sem, device_id=device, device_id_type=MESH
    )
    copy.start()
    sent.append(copy)


def arrived(region, send_sem, recv_sem, device):
    pltpu.make_async_remote_copy(
        src_ref=region, dst_ref=region, send_sem=send_sem, recv_sem=recv_sem, device_id=device, device_id_type=MESH
    ).wait_recv()


def rows_of(slice_index, count=1):
    return pl.ds(pl.multiple_of(slice_index * NARROW, 16), count * NARROW)


def block_of(index):
    return pl.ds(pl.multiple_of(index * CAP, CAP), CAP)


def gelu_both(values):
    square = values * values
    inner = gelu_factor * (values + gelu_cubic * values * square)
    tangent = jnp.tanh(inner)
    slope = 0.5 * (1.0 + tangent) + 0.5 * values * (1.0 - tangent * tangent) * gelu_factor * (
        1.0 + 3.0 * gelu_cubic * square
    )
    return 0.5 * values * (1.0 + tangent), slope


def dot(a, b, contract=(1, 0), precision=None):
    return lax.dot_general(
        a, b, (((contract[0],), (contract[1],)), ((), ())), precision=precision, preferred_element_type=jnp.float32
    )


def modulation_kernel(steps, table, weight, bias, ids, columns, info, rows, lookup_sem):
    f32 = jnp.float32
    copies = [
        pltpu.make_async_copy(table.at[pl.ds(steps[b], 1)], rows.at[pl.ds(b, 1)], lookup_sem.at[b]) for b in range(2)
    ]
    for copy in copies:
        copy.start()
    bias_columns = jnp.concatenate([bias[...], jnp.zeros((3, 256 - NARROW), f32)], axis=1)
    bias_columns = jnp.concatenate([bias_columns, jnp.zeros((125, 256), f32)], axis=0).T
    expert = lax.broadcasted_iota(jnp.int32, (N_BLK, 256), 0)
    named = ((expert == ids[0:1, :256]) | (expert == ids[1:2, :256])).astype(jnp.bfloat16)
    counts = dot(jnp.ones((8, 256), jnp.bfloat16), named, (1, 1))
    for copy in copies:
        copy.wait()
    looked = rows[pl.ds(0, 2)]
    condition = looked / (1.0 + jnp.exp(-looked))
    lane = lax.broadcasted_iota(jnp.int32, (NARROW, 128), 1)
    for c in range(3):
        part = weight[c * NARROW : (c + 1) * NARROW]
        sums = [
            jnp.sum(part * condition[b : b + 1], axis=1, keepdims=True) + bias_columns[:NARROW, c : c + 1]
            for b in range(2)
        ]
        columns[c] = jnp.where(lane == 0, sums[0], sums[1])
    gate = columns[2].astype(f32)
    gate = jnp.concatenate([gate, jnp.zeros((256 - NARROW, 128), f32)], axis=0).T[:8]
    high = gate.astype(jnp.bfloat16).astype(f32)
    middle = (gate - high).astype(jnp.bfloat16).astype(f32)
    low = (gate - high) - middle
    parts = jnp.concatenate([high[:2], middle[:2], low[:2], jnp.zeros((2, 256), f32)], axis=0)[:, :NARROW]
    repeated = jnp.concatenate([condition] * 4, axis=0)
    share = WIDTH // N_BLK
    for e in range(N_BLK):
        info[e] = jnp.concatenate(
            [parts, counts, repeated[:, e * share : (e + 1) * share], jnp.zeros((8, 96 - share), f32)], axis=1
        )


def modulation(timesteps, time_table, weight, bias, ids):
    vmem = pl.BlockSpec(memory_space=pltpu.VMEM)
    f32 = jnp.float32
    return pl.pallas_call(
        modulation_kernel,
        out_shape=(
            jax.ShapeDtypeStruct((3, NARROW, 128), f32),
            jax.ShapeDtypeStruct((N_BLK, 8, 256), f32),
        ),
        in_specs=[pl.BlockSpec(memory_space=pltpu.SMEM), pl.BlockSpec(memory_space=pl.ANY), vmem, vmem, vmem],
        out_specs=[vmem] * 2,
        scratch_shapes=[pltpu.VMEM((8, WIDTH), f32), pltpu.SemaphoreType.DMA((2,))],
        compiler_params=pltpu.CompilerParams(vmem_limit_bytes=24 * 2**20),
    )(timesteps, time_table, weight, bias, ids)


def expert_kernel(
    tokens, cotangent, route, ids, columns, info, up_t, down,
    token_grads, up_grads, down_grads, weight_grads, bias_grads,
    chosen, both, targets, stats, normed, payload, back, gate_back, sums, sums_all, grads, grads_all,
    xt, ct, hcot, act, pre_grad, part, up, down_t, table, gate_lanes, counts, gate_part,
    first_a, second_a, third_a, first_b, second_b, mine_b, total, gate_in, gate_sum, gate_out,
    a2a_send, a2a_recv, ring_send, ring_recv, info_send, info_recv,
    sum_send, sum_recv, back_send, back_recv, gate_send, gate_recv, end_send, end_recv, local_sem,
):
    at = Place()
    wide = jnp.float32
    bf16 = jnp.bfloat16
    peers = [(at.later(j), at.home(j // 8)) for j in range(N_BLK)]
    straight = [(at.later(j), at.hid) for j in range(N_BLK)]
    owners = [(at.earlier(j), at.home(j // 8)) for j in range(N_BLK)]
    straight_owners = [(at.earlier(j), at.hid) for j in range(N_BLK)]
    hid_peers = [at.hid_peer(i) for i in range(N_HID)]
    everyone = peers[1:] + straight[8:] + hid_peers[1:]
    barrier = pltpu.get_barrier_semaphore()
    for device in everyone:
        pl.semaphore_signal(barrier, inc=1, device_id=device, device_id_type=MESH)
    own = rows_of(at.hid)
    sent = []

    def put(ref, value):
        ref[...] = value.astype(ref.dtype)

    @pl.loop(0, TOKENS // 128)
    def _(i):
        rows = pl.ds(pl.multiple_of(i * 128, 128), 128)
        values = tokens[rows, :].astype(wide)
        mean = jnp.sum(values, axis=1, keepdims=True) / WIDTH
        spread_of = jnp.sum((values - mean) ** 2, axis=1, keepdims=True) / WIDTH
        inverse = 1.0 / jnp.sqrt(spread_of + norm_epsilon)
        lane = lax.broadcasted_iota(jnp.int32, (128, 128), 1)
        stats[:, rows] = jnp.where(lane == 0, mean, inverse).T[:8]

    row = lax.broadcasted_iota(jnp.int32, (NARROW, WIDTH), 0)
    column = lax.broadcasted_iota(jnp.int32, (NARROW, WIDTH), 1)
    pick = (column == row + at.hid * NARROW).astype(wide).astype(bf16)
    normed[...] = (dot(pick, tokens[...], (1, 1)) - stats[0:1, :]) * stats[1:2, :]
    for b in range(2):
        half = slice(b * PATCHES, (b + 1) * PATCHES)
        hin = normed[:, half] * (1.0 + columns[1, :, b : b + 1]) + columns[0, :, b : b + 1]
        for k in range(2):
            both[:NARROW, k * TOKENS + b * PATCHES : k * TOKENS + (b + 1) * PATCHES] = hin.astype(bf16)
    for k in range(2):
        weighted = cotangent[...].astype(wide) * route[k : k + 1, :]
        both[NARROW:, k * TOKENS : (k + 1) * TOKENS] = weighted.astype(bf16)

    expert = lax.broadcasted_iota(jnp.int32, (N_BLK, TOKENS), 0)
    named = [(expert == ids[k : k + 1, :]) for k in range(2)]
    earlier_row = lax.broadcasted_iota(jnp.int32, (TOKENS, TOKENS), 0)
    earlier_lane = lax.broadcasted_iota(jnp.int32, (TOKENS, TOKENS), 1)
    before = dot(
        (named[0] | named[1]).astype(wide).astype(bf16), (earlier_row < earlier_lane).astype(wide).astype(bf16)
    )
    for k in range(2):
        slot = jnp.sum(jnp.where(named[k], before, 0.0), axis=0, keepdims=True)
        targets[0:1, k * TOKENS : (k + 1) * TOKENS] = ids[k : k + 1, :] * CAP + slot.astype(jnp.int32)

    gate_part[...] = jnp.zeros_like(gate_part)
    pl.semaphore_wait(barrier, len(everyone))

    for j in range(N_BLK):
        target = at.later(j)
        if j == 0:
            info_local = pltpu.make_async_copy(info.at[target], table.at[0], local_sem.at[2])
            info_local.start()
        else:
            send(info.at[target], table.at[j], a2a_send.at[j, 2], a2a_recv.at[j, 2], straight[j], sent)

    def payload_parts(j):
        lanes = pl.ds(j * CAP, CAP)
        return (
            (payload.at[pl.ds(0, NARROW), lanes], xt.at[own, lanes]),
            (payload.at[pl.ds(NARROW, NARROW), lanes], ct.at[own, lanes]),
        )

    def make_payload(pair):
        hits = []
        for j in (2 * pair, 2 * pair + 1):
            slots = lax.broadcasted_iota(jnp.int32, (CAP, 2 * TOKENS), 0) + at.later(j) * CAP
            hit = (slots == targets[0:1, :]).astype(wide)
            chosen[block_of(at.later(j)), :] = (hit[:, :TOKENS] + hit[:, TOKENS:]).astype(bf16)
            hits.append(hit.astype(bf16))
        value = dot(both[...], jnp.concatenate(hits, axis=0), (1, 1))
        payload[:, 2 * pair * CAP : (2 * pair + 2) * CAP] = value.astype(bf16)
        for j in (2 * pair, 2 * pair + 1):
            for i, (src, dst) in enumerate(payload_parts(j)):
                if j == 0:
                    pltpu.make_async_copy(src, dst, local_sem.at[i]).start()
                else:
                    send(src, dst, a2a_send.at[j, i], a2a_recv.at[j, i], peers[j], sent)

    def from_peer(j, i, region):
        if j == 0:
            pltpu.make_async_copy(*payload_parts(0)[i], local_sem.at[i]).wait()
        else:
            arrived(region, a2a_send.at[j, i], a2a_recv.at[j, i], peers[j])

    def spread(g):
        a = g // (GROUPS // 2)
        f = at.home(a)
        other = at.home(1 - a)
        zf = f % 2
        lanes = pl.ds(g * LANES, LANES)
        halves = [pl.ds(g * LANES + i * HALF, HALF) for i in range(2)]
        far_slice = at.x_far * 2 + zf

        def go(array, rows, cols, k, device):
            region = array.at[rows, cols]
            send(region, region, ring_send.at[g, k], ring_recv.at[g, k], device, sent)

        def come(array, rows, cols, k):
            arrived(array.at[rows, cols], ring_send.at[g, k], ring_recv.at[g, k], at.across)

        def first():
            for j in range(g * LANES // CAP, (g + 1) * LANES // CAP):
                from_peer(j, 0, xt.at[rows_of(f), pl.ds(j * CAP, CAP)])
                from_peer(j, 1, ct.at[rows_of(f), pl.ds(j * CAP, CAP)])
            go(xt, rows_of(f), lanes, 0, at.across)
            go(ct, rows_of(f), lanes, 6, at.right)
            go(ct, rows_of(f), lanes, 7, at.left)
            go(ct, rows_of(f), lanes, 5, at.across)

        def second():
            come(xt, rows_of(other), lanes, 0)
            go(xt, rows_of(at.x * 2, 2), lanes, 1, at.right)
            go(xt, rows_of(at.x * 2, 2), lanes, 2, at.left)
            left, right = rows_of(at.x_left * 2 + zf), rows_of(at.x_right * 2 + zf)
            come(ct, left, lanes, 6)
            go(ct, left, halves[0], 8, at.right)
            go(ct, left, lanes, 10, at.across)
            come(ct, right, lanes, 7)
            go(ct, right, halves[1], 9, at.left)
            go(ct, right, lanes, 11, at.across)

        def third():
            come(xt, rows_of(at.x_left * 2, 2), lanes, 1)
            go(xt, rows_of(at.x_left * 2), lanes, 3, at.right)
            come(xt, rows_of(at.x_right * 2, 2), lanes, 2)
            go(xt, rows_of(at.x_right * 2 + 1), lanes, 4, at.left)
            for i in range(2):
                come(ct, rows_of(far_slice), halves[i], 8 + i)
                go(ct, rows_of(far_slice), halves[i], 12 + i, at.across)

        def fourth():
            come(xt, rows_of(at.x_far * 2), lanes, 3)
            come(xt, rows_of(at.x_far * 2 + 1), lanes, 4)
            come(ct, rows_of(other), lanes, 5)
            come(ct, rows_of(at.x_left * 2 + 1 - zf), lanes, 10)
            come(ct, rows_of(at.x_right * 2 + 1 - zf), lanes, 11)
            for i in range(2):
                come(ct, rows_of(at.x_far * 2 + 1 - zf), halves[i], 12 + i)

        return first, second, third, fourth

    def spread_info():
        info_local.wait()
        for j in range(1, N_BLK):
            arrived(table.at[j], a2a_send.at[j, 2], a2a_recv.at[j, 2], straight[j])
        rows = table[...].reshape(8 * N_BLK, 256)
        gate_lanes[own, :] = rows.T[:NARROW].astype(bf16)
        region = gate_lanes.at[own]
        for i in range(1, N_HID):
            send(region, region, info_send.at[i], info_recv.at[i], hid_peers[i], sent)
        lane = lax.broadcasted_iota(jnp.int32, (8 * N_BLK, 128), 1)
        mine = jnp.sum(jnp.where(lane == at.blk + 16, rows[:, 128:], 0.0), axis=1, keepdims=True)
        counts[...] = jnp.broadcast_to(mine, counts.shape)

    def gather_info():
        for i in range(1, N_HID):
            region = gate_lanes.at[rows_of((at.hid + 8 - i) % 8)]
            arrived(region, info_send.at[i], info_recv.at[i], at.across)

    def image_of_lane(g):
        shape = (8 * N_BLK, LANES)
        row = lax.broadcasted_iota(jnp.int32, shape, 0)
        lane = lax.broadcasted_iota(jnp.int32, shape, 1)
        block = lane // CAP + g * (LANES // CAP)
        first_count = jnp.concatenate([counts[...]] * (LANES // 128), axis=1)
        is_first = (lane % CAP).astype(wide) < first_count
        hit = (row // 8 == block) & (is_first == (row % 2 == 0)) & (row % 8 < 6)
        return jnp.where(hit, 1.0, 0.0).astype(bf16)

    def forward(g):
        lanes = pl.ds(g * LANES, LANES)
        images = image_of_lane(g)

        @pl.loop(0, 4)
        def _(i):
            rows = rows_of(2 * i, 2)
            gates = dot(gate_lanes[rows, :], images)
            hcot[rows, lanes] = (gates * ct[rows, lanes].astype(wide)).astype(bf16)

        @pl.loop(0, 3)
        def _(i):
            rows = pl.ds(pl.multiple_of(i * 192, 64), 192)
            activated, slope = gelu_both(dot(up_t[rows, :], xt[:, lanes]))
            act[rows, :] = activated.astype(bf16)
            pre_grad[rows, :] = (dot(down[rows, :], hcot[:, lanes]) * slope).astype(bf16)

        @pl.loop(0, 4)
        def _(i):
            rows = rows_of(2 * i, 2)
            part[rows, lanes] = dot(up[rows, :], pre_grad[...]).astype(bf16)

    def gates_of(g):
        lanes = pl.ds(g * LANES, LANES)
        spots = 2 * N_BLK
        narrow_row = lax.broadcasted_iota(jnp.int32, (spots, 8 * N_BLK), 0)
        wide_row = lax.broadcasted_iota(jnp.int32, (spots, 8 * N_BLK), 1)
        compact = (wide_row == narrow_row // 2 * 8 + narrow_row % 2).astype(wide).astype(bf16)
        images = dot(compact, image_of_lane(g)).astype(bf16)

        @pl.loop(0, 4)
        def _(i):
            rows = rows_of(2 * i, 2)
            product = (dot(down_t[rows, :], act[...]) * ct[rows, lanes].astype(wide)).astype(bf16)
            for k in range(2):
                value = dot(images, product[k * NARROW : (k + 1) * NARROW], (1, 1))
                gate_part[2 * i + k, :, pl.ds(0, NARROW)] += value

    def weights(grads_of, left, right, g):
        lanes = pl.ds(g * LANES, LANES)

        @pl.loop(0, 3)
        def _(i):
            rows = pl.ds(pl.multiple_of(i * 192, 64), 192)
            value = dot(left[rows, :], right[:, lanes], (1, 1))
            if g == 0:
                grads_of[rows, :] = value
            else:
                grads_of[rows, :] += value

    def reduce(g):
        a = g // (GROUPS // 2)
        zf = at.home(a) % 2
        lanes_a = pl.ds(g * LANES, HALF)
        lanes_b = pl.ds(g * LANES + HALF, HALF)

        def mine(x, z, lanes):
            return part.at[rows_of(x * 2 + z), lanes]

        def go(src, dst, k, device):
            send(src, dst, sum_send.at[g, k], sum_recv.at[g, k], device, sent)

        def come(region, k):
            arrived(region, sum_send.at[g, k], sum_recv.at[g, k], at.across)

        def first():
            for x in range(4):
                go(mine(x, 1 - zf, lanes_b), first_b.at[g, x], 8 + x, at.across)
            go(mine(at.x_far, 0, lanes_a), first_a.at[g, 0], 0, at.right)
            go(mine(at.x_far, 1, lanes_a), first_a.at[g, 1], 1, at.left)
            go(mine(at.x_right, 1, lanes_a), second_a.at[g, 1], 2, at.right)
            go(mine(at.x_left, 0, lanes_a), second_a.at[g, 2], 3, at.left)

        def second():
            come(first_a.at[g, 0], 0)
            put(
                third_a.at[g, 0],
                first_a[g, 0].astype(wide) + mine(at.x_right, 0, lanes_a)[...].astype(wide),
            )
            go(third_a.at[g, 0], second_a.at[g, 0], 4, at.right)
            come(first_a.at[g, 1], 1)
            put(
                third_a.at[g, 1],
                first_a[g, 1].astype(wide) + mine(at.x_left, 1, lanes_a)[...].astype(wide),
            )
            go(third_a.at[g, 1], second_a.at[g, 3], 5, at.left)
            for x in range(4):
                come(first_b.at[g, x], 8 + x)
            for i, x in enumerate((at.x_far, at.x_right, at.x_left, at.x)):
                put(
                    mine_b.at[g, i],
                    first_b[g, x].astype(wide) + mine(x, zf, lanes_b)[...].astype(wide),
                )
                if i == 0:
                    go(mine_b.at[g, 0, :, pl.ds(0, HALF // 2)], second_b.at[g, 0], 12, at.right)
                    go(mine_b.at[g, 0, :, pl.ds(HALF // 2, HALF // 2)], second_b.at[g, 1], 13, at.left)
                if i == 1:
                    go(mine_b.at[g, 1, :, pl.ds(HALF // 2, HALF // 2)], second_b.at[g, 2], 14, at.right)
                if i == 2:
                    go(mine_b.at[g, 2, :, pl.ds(0, HALF // 2)], second_b.at[g, 3], 15, at.left)

        def third():
            come(second_a.at[g, 0], 4)
            come(second_a.at[g, 1], 2)
            come(second_a.at[g, 2], 3)
            come(second_a.at[g, 3], 5)
            sums = [
                second_a[g, z].astype(wide)
                + second_a[g, 2 + z].astype(wide)
                + mine(at.x, z, lanes_a)[...].astype(wide)
                for z in range(2)
            ]
            keep = jnp.where(zf == 0, sums[0], sums[1])
            give = jnp.where(zf == 0, sums[1], sums[0])
            put(third_a.at[g, 2], give)
            go(third_a.at[g, 2], third_a.at[g, 3], 6, at.across)
            put(total.at[g, :, pl.ds(0, HALF)], keep)
            come(second_b.at[g, 0], 12)
            put(
                second_b.at[g, 4],
                second_b[g, 0].astype(wide) + mine_b[g, 1, :, pl.ds(0, HALF // 2)].astype(wide),
            )
            go(second_b.at[g, 4], second_b.at[g, 6], 16, at.right)
            come(second_b.at[g, 1], 13)
            put(
                second_b.at[g, 5],
                second_b[g, 1].astype(wide) + mine_b[g, 2, :, pl.ds(HALF // 2, HALF // 2)].astype(wide),
            )
            go(second_b.at[g, 5], second_b.at[g, 7], 17, at.left)

        def fourth():
            come(third_a.at[g, 3], 6)
            put(
                total.at[g, :, pl.ds(0, HALF)],
                total[g, :, pl.ds(0, HALF)].astype(wide) + third_a[g, 3].astype(wide),
            )
            come(second_b.at[g, 6], 16)
            come(second_b.at[g, 2], 14)
            come(second_b.at[g, 3], 15)
            come(second_b.at[g, 7], 17)
            for i, (l, r) in enumerate(((6, 3), (2, 7))):
                put(
                    total.at[g, :, pl.ds(HALF + i * (HALF // 2), HALF // 2)],
                    second_b[g, l].astype(wide)
                    + second_b[g, r].astype(wide)
                    + mine_b[g, 3, :, pl.ds(i * (HALF // 2), HALF // 2)].astype(wide),
                )
            for i in range(LANES // CAP):
                j = g * (LANES // CAP) + i
                src = total.at[g, :, pl.ds(i * CAP, CAP)]
                dst = back.at[:, block_of(at.blk)]
                if j == 0:
                    pltpu.make_async_copy(src, dst, local_sem.at[3]).start()
                else:
                    send(src, dst, back_send.at[j, 0], back_recv.at[j, 0], owners[j], sent)

        return first, second, third, fourth

    def gate_first():
        for i in range(1, N_HID):
            q = (at.hid + i) % 8
            send(gate_part.at[q], gate_in.at[i], gate_send.at[i], gate_recv.at[i], hid_peers[i], sent)

    def gate_second():
        value = gate_part[at.hid]
        for i in range(1, N_HID):
            arrived(gate_in.at[i], gate_send.at[i], gate_recv.at[i], at.across)
            value = value + gate_in[i]
        gate_sum[...] = value
        for j in range(N_BLK):
            gate_out[j] = gate_sum[pl.ds(2 * j, 2)]
            src, dst = gate_out.at[j], gate_back.at[at.blk]
            if j == 0:
                pltpu.make_async_copy(src, dst, local_sem.at[4]).start()
            else:
                send(src, dst, back_send.at[j, 1], back_recv.at[j, 1], straight_owners[j], sent)

    make_payload(0)
    make_payload(1)

    @pl.loop(0, 9)
    def _(i):
        tile = pl.ds(pl.multiple_of(i * 128, 128), 128)
        up[tile, :] = up_t[:, tile].T
        down_t[tile, :] = down[:, tile].T

    spreads = [spread(g) for g in range(GROUPS)]
    reduces = [reduce(g) for g in range(GROUPS)]
    for tick in range(GROUPS + 6):
        for k in range(4):
            if 0 <= tick - k < GROUPS:
                spreads[tick - k][k]()
            if tick == 0 and k == 0:
                for pair in range(2, N_BLK // 2):
                    make_payload(pair)
                spread_info()
        done = tick - 3
        if done == 0:
            gather_info()
        if 0 <= done < GROUPS:
            forward(done)
            reduces[done][0]()
        for k in range(1, 4):
            if 0 <= done - k < GROUPS:
                reduces[done - k][k]()
        if 0 <= done < GROUPS:
            gates_of(done)
            if done == GROUPS - 1:
                gate_first()
            weights(up_grads, pre_grad, xt, done)
            weights(down_grads, act, hcot, done)
        if done == GROUPS:
            gate_second()

    for j in range(N_BLK):
        e = at.later(j)
        if j == 0:
            pltpu.make_async_copy(total.at[0, :, pl.ds(0, CAP)], back.at[:, block_of(e)], local_sem.at[3]).wait()
            pltpu.make_async_copy(gate_out.at[0], gate_back.at[e], local_sem.at[4]).wait()
        else:
            arrived(back.at[:, block_of(e)], back_send.at[j, 0], back_recv.at[j, 0], at.across)
            arrived(gate_back.at[e], back_send.at[j, 1], back_recv.at[j, 1], at.across)

    mixed = dot(back[...], chosen[...])
    scale = jnp.concatenate(
        [jnp.broadcast_to(1.0 + columns[1, :, b : b + 1], (NARROW, PATCHES)) for b in range(2)], axis=1
    )
    norm_grad = mixed * scale
    sums[0:1, :] = jnp.sum(norm_grad, axis=0, keepdims=True)
    sums[1:2, :] = jnp.sum(norm_grad * normed[...], axis=0, keepdims=True)
    for i in range(1, N_HID):
        send(sums, sums_all.at[i], end_send.at[N_BLK + i], end_recv.at[N_BLK + i], hid_peers[i], sent)
    lane = lax.broadcasted_iota(jnp.int32, (NARROW, 128), 1)
    listed = jnp.zeros((NARROW, 128), wide)
    for c, values in enumerate((mixed, mixed * normed[...])):
        for b in range(2):
            value = jnp.sum(values[:, b * PATCHES : (b + 1) * PATCHES], axis=1, keepdims=True)
            listed = jnp.where(lane == 2 * c + b, value, listed)
    listed = jnp.concatenate([listed, jnp.zeros((256 - NARROW, 128), wide)], axis=0).T
    gate_grad = gate_back[0]
    for e in range(1, N_BLK):
        gate_grad = gate_grad + gate_back[e]
    grads[...] = jnp.concatenate([listed[:4], gate_grad, jnp.zeros((2, 256), wide)], axis=0)
    for j in range(1, N_BLK):
        send(grads, grads_all.at[j], end_send.at[j], end_recv.at[j], straight[j], sent)
    grads_all[0] = grads[...]
    first, second = sums[0:1, :], sums[1:2, :]
    for i in range(1, N_HID):
        arrived(sums_all.at[i], end_send.at[N_BLK + i], end_recv.at[N_BLK + i], at.across)
        first = first + sums_all[i, 0:1, :]
        second = second + sums_all[i, 1:2, :]
    token_grads[...] = (
        cotangent[...].astype(wide)
        + stats[1:2, :] * (norm_grad - first / WIDTH - normed[...] * (second / WIDTH))
    ).astype(bf16)
    for j in range(1, N_BLK):
        arrived(grads_all.at[j], end_send.at[j], end_recv.at[j], at.across)
    image_grads = grads_all[...].reshape(8 * N_BLK, 256)
    conditions = table[...].reshape(8 * N_BLK, 256)[:, 128:]
    kind = lax.broadcasted_iota(jnp.int32, (8 * N_BLK, 128), 0) % 8 // 2
    kind_wide = lax.broadcasted_iota(jnp.int32, (8 * N_BLK, 256), 0) % 8 // 2
    for c in range(3):
        value = dot(jnp.where(kind == c, conditions, 0.0), image_grads, (0, 0), lax.Precision.HIGHEST)
        weight_grads[c] = value[32 : 32 + WIDTH // N_BLK, :NARROW]
        bias_grads[c : c + 1, :] = jnp.sum(jnp.where(kind_wide == c, image_grads, 0.0), axis=0, keepdims=True)[
            :, :NARROW
        ]
    for copy in sent:
        copy.wait_send()


def run_experts(*operands):
    vmem = pl.BlockSpec(memory_space=pltpu.VMEM)
    bf16, f32 = jnp.bfloat16, jnp.float32
    hidden, width = operands[-1].shape
    dma = pltpu.SemaphoreType.DMA
    return pl.pallas_call(
        expert_kernel,
        out_shape=(
            jax.ShapeDtypeStruct((NARROW, TOKENS), bf16),
            jax.ShapeDtypeStruct((hidden, width), f32),
            jax.ShapeDtypeStruct((hidden, width), f32),
            jax.ShapeDtypeStruct((3, width // N_BLK, NARROW), f32),
            jax.ShapeDtypeStruct((3, NARROW), f32),
        ),
        in_specs=[vmem] * len(operands),
        out_specs=[vmem] * 5,
        scratch_shapes=[
            pltpu.VMEM((SLOTS, TOKENS), bf16),
            pltpu.VMEM((2 * NARROW, 2 * TOKENS), bf16),
            pltpu.VMEM((8, 2 * TOKENS), jnp.int32),
            pltpu.VMEM((8, TOKENS), f32),
            pltpu.VMEM((NARROW, TOKENS), f32),
            pltpu.VMEM((2 * NARROW, SLOTS), bf16),
            pltpu.VMEM((NARROW, SLOTS), bf16),
            pltpu.VMEM((N_BLK, 2, 256), f32),
            pltpu.VMEM((2, TOKENS), f32),
            pltpu.VMEM((N_HID, 2, TOKENS), f32),
            pltpu.VMEM((8, 256), f32),
            pltpu.VMEM((N_BLK, 8, 256), f32),
            pltpu.VMEM((width, SLOTS), bf16),
            pltpu.VMEM((width, SLOTS), bf16),
            pltpu.VMEM((width, SLOTS), bf16),
            pltpu.VMEM((hidden, LANES), bf16),
            pltpu.VMEM((hidden, LANES), bf16),
            pltpu.VMEM((width, SLOTS), bf16),
            pltpu.VMEM((width, hidden), bf16),
            pltpu.VMEM((width, hidden), bf16),
            pltpu.VMEM((N_BLK, 8, 256), f32),
            pltpu.VMEM((width, 128), bf16),
            pltpu.VMEM((8 * N_BLK, 128), f32),
            pltpu.VMEM((N_HID, 2 * N_BLK, 256), f32),
            pltpu.VMEM((GROUPS, 2, NARROW, HALF), bf16),
            pltpu.VMEM((GROUPS, 4, NARROW, HALF), bf16),
            pltpu.VMEM((GROUPS, 4, NARROW, HALF), bf16),
            pltpu.VMEM((GROUPS, 4, NARROW, HALF), bf16),
            pltpu.VMEM((GROUPS, 8, NARROW, HALF // 2), bf16),
            pltpu.VMEM((GROUPS, 4, NARROW, HALF), bf16),
            pltpu.VMEM((GROUPS, NARROW, LANES), bf16),
            pltpu.VMEM((N_HID, 2 * N_BLK, 256), f32),
            pltpu.VMEM((2 * N_BLK, 256), f32),
            pltpu.VMEM((N_BLK, 2, 256), f32),
            dma((N_BLK, 3)),
            dma((N_BLK, 3)),
            dma((GROUPS, 14)),
            dma((GROUPS, 14)),
            dma((N_HID,)),
            dma((N_HID,)),
            dma((GROUPS, 18)),
            dma((GROUPS, 18)),
            dma((N_BLK, 2)),
            dma((N_BLK, 2)),
            dma((N_HID,)),
            dma((N_HID,)),
            dma((N_BLK + N_HID,)),
            dma((N_BLK + N_HID,)),
            dma((5,)),
        ],
        compiler_params=pltpu.CompilerParams(
            collective_id=0, has_side_effects=True, vmem_limit_bytes=60 * 2**20
        ),
    )(*operands)


def on_device(
    tokens,
    cotangent,
    route_weight,
    expert_ids,
    timesteps,
    time_table,
    up_weight,
    down_weight,
    modulation_weight,
    modulation_bias,
):
    ids = expert_ids.T
    by_feature = modulation_weight.transpose(1, 2, 0).reshape(3 * NARROW, WIDTH)
    columns, info = modulation(timesteps, time_table, by_feature, modulation_bias, ids)
    token_grads, up_grads, down_grads, weight_grads, bias_grads = run_experts(
        tokens, cotangent.T, route_weight.T, ids, columns, info, up_weight[0].T, down_weight[0]
    )
    return (token_grads.T, up_grads.T[None], down_grads[None], weight_grads.transpose(1, 0, 2), bias_grads)


def solution(mesh):
    in_specs = (
        P("blk", None),
        P("blk", "hid"),
        P("blk", None),
        P("blk", None),
        P("blk"),
        P(),
        P("blk", None, "hid"),
        P("blk", "hid", None),
        P(None, None, "hid"),
        P(None, "hid"),
    )
    out_specs = (
        P("blk", "hid"),
        P("blk", None, "hid"),
        P("blk", "hid", None),
        P("blk", None, "hid"),
        P(None, "hid"),
    )
    return jax.shard_map(
        on_device, mesh=mesh, in_specs=in_specs, out_specs=out_specs, check_vma=False
    )
```

```python
import math

import jax
import jax.numpy as jnp
from jax import lax
from jax.experimental import pallas as pl
from jax.experimental.pallas import tpu as pltpu
from jax.sharding import PartitionSpec as P

MESH = pl.DeviceIdType.MESH
norm_epsilon = 1e-06
gelu_cubic = 0.044715
gelu_factor = math.sqrt(2.0 / math.pi)

N_BLK, N_HID = 16, 8
WIDTH, NARROW, CAP = 1152, 144, 128
TOKENS, PATCHES = 512, 256
SLOTS = N_BLK * CAP
GROUPS = 4
LANES = SLOTS // GROUPS
HALF = LANES // 2
ORDER = (0, 1, 6, 2, 7, 3, 5, 4)


def shift(j):
    return j // 8, ORDER[j % 8]


class Place:
    def __init__(self):
        self.blk = lax.axis_index("blk")
        self.hid = lax.axis_index("hid")
        self.z_hi, self.m = self.blk // 8, self.blk % 8
        self.x, self.z_lo = self.hid // 2, self.hid % 2
        self.x_right, self.x_left, self.x_far = [(self.x + i) % 4 for i in (1, 3, 2)]
        self.right = (self.blk, self.x_right * 2 + self.z_lo)
        self.left = (self.blk, self.x_left * 2 + self.z_lo)
        self.across = (self.blk, self.home(1))

    def home(self, a):
        return self.hid if a == 0 else self.hid + 1 - 2 * self.z_lo

    def later(self, j):
        a, m = shift(j)
        return (self.z_hi + a) % 2 * 8 + (self.m + m) % 8

    def earlier(self, j):
        a, m = shift(j)
        return (self.z_hi + a) % 2 * 8 + (self.m + 8 - m) % 8

    def hid_peer(self, i):
        return (self.blk, (self.hid + i) % 8)


def greet(devices):
    barrier = pltpu.get_barrier_semaphore()
    for device in devices:
        pl.semaphore_signal(barrier, inc=1, device_id=device, device_id_type=MESH)
    pl.semaphore_wait(barrier, len(devices))


def send(src, dst, send_sem, recv_sem, device, sent):
    copy = pltpu.make_async_remote_copy(
        src_ref=src, dst_ref=dst, send_sem=send_sem, recv_sem=recv_sem, device_id=device, device_id_type=MESH
    )
    copy.start()
    sent.append(copy)


def arrived(region, send_sem, recv_sem, device):
    pltpu.make_async_remote_copy(
        src_ref=region, dst_ref=region, send_sem=send_sem, recv_sem=recv_sem, device_id=device, device_id_type=MESH
    ).wait_recv()


def rows_of(slice_index, count=1):
    return pl.ds(pl.multiple_of(slice_index * NARROW, 16), count * NARROW)


def block_of(index):
    return pl.ds(pl.multiple_of(index * CAP, CAP), CAP)


def gelu_both(values):
    square = values * values
    inner = gelu_factor * (values + gelu_cubic * values * square)
    tangent = jnp.tanh(inner)
    slope = 0.5 * (1.0 + tangent) + 0.5 * values * (1.0 - tangent * tangent) * gelu_factor * (
        1.0 + 3.0 * gelu_cubic * square
    )
    return 0.5 * values * (1.0 + tangent), slope


def dot(a, b, contract=(1, 0), precision=None):
    return lax.dot_general(
        a, b, (((contract[0],), (contract[1],)), ((), ())), precision=precision, preferred_element_type=jnp.float32
    )


def modulation_kernel(steps, table, weight, bias, ids, columns, info, rows, lookup_sem):
    f32 = jnp.float32
    copies = [
        pltpu.make_async_copy(table.at[pl.ds(steps[b], 1)], rows.at[pl.ds(b, 1)], lookup_sem.at[b]) for b in range(2)
    ]
    for copy in copies:
        copy.start()
    bias_columns = jnp.concatenate([bias[...], jnp.zeros((3, 256 - NARROW), f32)], axis=1)
    bias_columns = jnp.concatenate([bias_columns, jnp.zeros((125, 256), f32)], axis=0).T
    expert = lax.broadcasted_iota(jnp.int32, (N_BLK, 256), 0)
    named = ((expert == ids[0:1, :256]) | (expert == ids[1:2, :256])).astype(jnp.bfloat16)
    counts = dot(jnp.ones((8, 256), jnp.bfloat16), named, (1, 1))
    for copy in copies:
        copy.wait()
    looked = rows[pl.ds(0, 2)]
    condition = looked / (1.0 + jnp.exp(-looked))
    lane = lax.broadcasted_iota(jnp.int32, (NARROW, 128), 1)
    for c in range(3):
        part = weight[c * NARROW : (c + 1) * NARROW]
        sums = [
            jnp.sum(part * condition[b : b + 1], axis=1, keepdims=True) + bias_columns[:NARROW, c : c + 1]
            for b in range(2)
        ]
        columns[c] = jnp.where(lane == 0, sums[0], sums[1])
    gate = columns[2].astype(f32)
    gate = jnp.concatenate([gate, jnp.zeros((256 - NARROW, 128), f32)], axis=0).T[:8]
    high = gate.astype(jnp.bfloat16).astype(f32)
    middle = (gate - high).astype(jnp.bfloat16).astype(f32)
    low = (gate - high) - middle
    parts = jnp.concatenate([high[:2], middle[:2], low[:2], jnp.zeros((2, 256), f32)], axis=0)[:, :NARROW]
    repeated = jnp.concatenate([condition] * 4, axis=0)
    share = WIDTH // N_BLK
    for e in range(N_BLK):
        info[e] = jnp.concatenate(
            [parts, counts, repeated[:, e * share : (e + 1) * share], jnp.zeros((8, 96 - share), f32)], axis=1
        )


def modulation(timesteps, time_table, weight, bias, ids):
    vmem = pl.BlockSpec(memory_space=pltpu.VMEM)
    f32 = jnp.float32
    return pl.pallas_call(
        modulation_kernel,
        out_shape=(
            jax.ShapeDtypeStruct((3, NARROW, 128), f32),
            jax.ShapeDtypeStruct((N_BLK, 8, 256), f32),
        ),
        in_specs=[pl.BlockSpec(memory_space=pltpu.SMEM), pl.BlockSpec(memory_space=pl.ANY), vmem, vmem, vmem],
        out_specs=[vmem] * 2,
        scratch_shapes=[pltpu.VMEM((8, WIDTH), f32), pltpu.SemaphoreType.DMA((2,))],
        compiler_params=pltpu.CompilerParams(vmem_limit_bytes=60 * 2**20),
    )(timesteps, time_table, weight, bias, ids)


def expert_kernel(
    tokens, cotangent, route, ids, columns, info, up_t, down,
    norm_grads, normed, stats, totals, grads_all, table, up_out, down_out,
    chosen, both, targets, payload, back, gate_back, sums, sums_all, grads, up_grads, down_grads,
    xt, ct, hcot, act, pre_grad, part, up, down_t, gate_lanes, counts, gate_part,
    first_a, second_a, third_a, first_b, second_b, mine_b, total, gate_in, gate_sum, gate_out,
    a2a_send, a2a_recv, ring_send, ring_recv, info_send, info_recv,
    sum_send, sum_recv, back_send, back_recv, gate_send, gate_recv, end_send, end_recv, local_sem,
):
    at = Place()
    wide = jnp.float32
    bf16 = jnp.bfloat16
    peers = [(at.later(j), at.home(j // 8)) for j in range(N_BLK)]
    straight = [(at.later(j), at.hid) for j in range(N_BLK)]
    owners = [(at.earlier(j), at.home(j // 8)) for j in range(N_BLK)]
    straight_owners = [(at.earlier(j), at.hid) for j in range(N_BLK)]
    hid_peers = [at.hid_peer(i) for i in range(N_HID)]
    everyone = peers[1:] + straight[8:] + hid_peers[1:]
    barrier = pltpu.get_barrier_semaphore()
    for device in everyone:
        pl.semaphore_signal(barrier, inc=1, device_id=device, device_id_type=MESH)
    own = rows_of(at.hid)
    sent = []

    def put(ref, value):
        ref[...] = value.astype(ref.dtype)

    @pl.loop(0, TOKENS // 128)
    def _(i):
        rows = pl.ds(pl.multiple_of(i * 128, 128), 128)
        values = tokens[rows, :].astype(wide)
        mean = jnp.sum(values, axis=1, keepdims=True) / WIDTH
        spread_of = jnp.sum((values - mean) ** 2, axis=1, keepdims=True) / WIDTH
        inverse = 1.0 / jnp.sqrt(spread_of + norm_epsilon)
        lane = lax.broadcasted_iota(jnp.int32, (128, 128), 1)
        stats[:, rows] = jnp.where(lane == 0, mean, inverse).T[:8]

    row = lax.broadcasted_iota(jnp.int32, (NARROW, WIDTH), 0)
    column = lax.broadcasted_iota(jnp.int32, (NARROW, WIDTH), 1)
    pick = (column == row + at.hid * NARROW).astype(wide).astype(bf16)
    normed[...] = (dot(pick, tokens[...], (1, 1)) - stats[0:1, :]) * stats[1:2, :]
    for b in range(2):
        half = slice(b * PATCHES, (b + 1) * PATCHES)
        hin = normed[:, half] * (1.0 + columns[1, :, b : b + 1]) + columns[0, :, b : b + 1]
        for k in range(2):
            both[:NARROW, k * TOKENS + b * PATCHES : k * TOKENS + (b + 1) * PATCHES] = hin.astype(bf16)
    for k in range(2):
        weighted = cotangent[...].astype(wide) * route[k : k + 1, :]
        both[NARROW:, k * TOKENS : (k + 1) * TOKENS] = weighted.astype(bf16)

    expert = lax.broadcasted_iota(jnp.int32, (N_BLK, TOKENS), 0)
    named = [(expert == ids[k : k + 1, :]) for k in range(2)]
    earlier_row = lax.broadcasted_iota(jnp.int32, (TOKENS, TOKENS), 0)
    earlier_lane = lax.broadcasted_iota(jnp.int32, (TOKENS, TOKENS), 1)
    before = dot(
        (named[0] | named[1]).astype(wide).astype(bf16), (earlier_row < earlier_lane).astype(wide).astype(bf16)
    )
    for k in range(2):
        slot = jnp.sum(jnp.where(named[k], before, 0.0), axis=0, keepdims=True)
        targets[0:1, k * TOKENS : (k + 1) * TOKENS] = ids[k : k + 1, :] * CAP + slot.astype(jnp.int32)

    gate_part[...] = jnp.zeros_like(gate_part)
    pl.semaphore_wait(barrier, len(everyone))

    for j in range(N_BLK):
        target = at.later(j)
        if j == 0:
            info_local = pltpu.make_async_copy(info.at[target], table.at[0], local_sem.at[2])
            info_local.start()
        else:
            send(info.at[target], table.at[j], a2a_send.at[j, 2], a2a_recv.at[j, 2], straight[j], sent)

    def payload_parts(j):
        lanes = pl.ds(j * CAP, CAP)
        return (
            (payload.at[pl.ds(0, NARROW), lanes], xt.at[own, lanes]),
            (payload.at[pl.ds(NARROW, NARROW), lanes], ct.at[own, lanes]),
        )

    def make_payload(pair):
        hits = []
        for j in (2 * pair, 2 * pair + 1):
            slots = lax.broadcasted_iota(jnp.int32, (CAP, 2 * TOKENS), 0) + at.later(j) * CAP
            hit = (slots == targets[0:1, :]).astype(wide)
            chosen[block_of(at.later(j)), :] = (hit[:, :TOKENS] + hit[:, TOKENS:]).astype(bf16)
            hits.append(hit.astype(bf16))
        value = dot(both[...], jnp.concatenate(hits, axis=0), (1, 1))
        payload[:, 2 * pair * CAP : (2 * pair + 2) * CAP] = value.astype(bf16)
        for j in (2 * pair, 2 * pair + 1):
            for i, (src, dst) in enumerate(payload_parts(j)):
                if j == 0:
                    pltpu.make_async_copy(src, dst, local_sem.at[i]).start()
                else:
                    send(src, dst, a2a_send.at[j, i], a2a_recv.at[j, i], peers[j], sent)

    def from_peer(j, i, region):
        if j == 0:
            pltpu.make_async_copy(*payload_parts(0)[i], local_sem.at[i]).wait()
        else:
            arrived(region, a2a_send.at[j, i], a2a_recv.at[j, i], peers[j])

    def spread(g):
        a = g // (GROUPS // 2)
        f = at.home(a)
        other = at.home(1 - a)
        zf = f % 2
        lanes = pl.ds(g * LANES, LANES)
        halves = [pl.ds(g * LANES + i * HALF, HALF) for i in range(2)]
        far_slice = at.x_far * 2 + zf

        def go(array, rows, cols, k, device):
            region = array.at[rows, cols]
            send(region, region, ring_send.at[g, k], ring_recv.at[g, k], device, sent)

        def come(array, rows, cols, k):
            arrived(array.at[rows, cols], ring_send.at[g, k], ring_recv.at[g, k], at.across)

        def first():
            for j in range(g * LANES // CAP, (g + 1) * LANES // CAP):
                from_peer(j, 0, xt.at[rows_of(f), pl.ds(j * CAP, CAP)])
                from_peer(j, 1, ct.at[rows_of(f), pl.ds(j * CAP, CAP)])
            go(xt, rows_of(f), lanes, 0, at.across)
            go(ct, rows_of(f), lanes, 6, at.right)
            go(ct, rows_of(f), lanes, 7, at.left)
            go(ct, rows_of(f), lanes, 5, at.across)

        def second():
            come(xt, rows_of(other), lanes, 0)
            go(xt, rows_of(at.x * 2, 2), lanes, 1, at.right)
            go(xt, rows_of(at.x * 2, 2), lanes, 2, at.left)
            left, right = rows_of(at.x_left * 2 + zf), rows_of(at.x_right * 2 + zf)
            come(ct, left, lanes, 6)
            go(ct, left, halves[0], 8, at.right)
            go(ct, left, lanes, 10, at.across)
            come(ct, right, lanes, 7)
            go(ct, right, halves[1], 9, at.left)
            go(ct, right, lanes, 11, at.across)

        def third():
            come(xt, rows_of(at.x_left * 2, 2), lanes, 1)
            go(xt, rows_of(at.x_left * 2), lanes, 3, at.right)
            come(xt, rows_of(at.x_right * 2, 2), lanes, 2)
            go(xt, rows_of(at.x_right * 2 + 1), lanes, 4, at.left)
            for i in range(2):
                come(ct, rows_of(far_slice), halves[i], 8 + i)
                go(ct, rows_of(far_slice), halves[i], 12 + i, at.across)

        def fourth():
            come(xt, rows_of(at.x_far * 2), lanes, 3)
            come(xt, rows_of(at.x_far * 2 + 1), lanes, 4)
            come(ct, rows_of(other), lanes, 5)
            come(ct, rows_of(at.x_left * 2 + 1 - zf), lanes, 10)
            come(ct, rows_of(at.x_right * 2 + 1 - zf), lanes, 11)
            for i in range(2):
                come(ct, rows_of(at.x_far * 2 + 1 - zf), halves[i], 12 + i)

        return first, second, third, fourth

    def spread_info():
        info_local.wait()
        for j in range(1, N_BLK):
            arrived(table.at[j], a2a_send.at[j, 2], a2a_recv.at[j, 2], straight[j])
        rows = table[...].reshape(8 * N_BLK, 256)
        gate_lanes[own, :] = rows.T[:NARROW].astype(bf16)
        region = gate_lanes.at[own]
        for i in range(1, N_HID):
            send(region, region, info_send.at[i], info_recv.at[i], hid_peers[i], sent)
        lane = lax.broadcasted_iota(jnp.int32, (8 * N_BLK, 128), 1)
        mine = jnp.sum(jnp.where(lane == at.blk + 16, rows[:, 128:], 0.0), axis=1, keepdims=True)
        counts[...] = jnp.broadcast_to(mine, counts.shape)

    def gather_info():
        for i in range(1, N_HID):
            region = gate_lanes.at[rows_of((at.hid + 8 - i) % 8)]
            arrived(region, info_send.at[i], info_recv.at[i], at.across)

    def image_of_lane(g):
        shape = (8 * N_BLK, LANES)
        row = lax.broadcasted_iota(jnp.int32, shape, 0)
        lane = lax.broadcasted_iota(jnp.int32, shape, 1)
        block = lane // CAP + g * (LANES // CAP)
        first_count = jnp.concatenate([counts[...]] * (LANES // 128), axis=1)
        is_first = (lane % CAP).astype(wide) < first_count
        hit = (row // 8 == block) & (is_first == (row % 2 == 0)) & (row % 8 < 6)
        return jnp.where(hit, 1.0, 0.0).astype(bf16)

    def forward(g):
        lanes = pl.ds(g * LANES, LANES)
        images = image_of_lane(g)

        @pl.loop(0, 4)
        def _(i):
            rows = rows_of(2 * i, 2)
            gates = dot(gate_lanes[rows, :], images)
            hcot[rows, lanes] = (gates * ct[rows, lanes].astype(wide)).astype(bf16)

        @pl.loop(0, 3)
        def _(i):
            rows = pl.ds(pl.multiple_of(i * 192, 64), 192)
            activated, slope = gelu_both(dot(up_t[rows, :], xt[:, lanes]))
            act[rows, :] = activated.astype(bf16)
            pre_grad[rows, :] = (dot(down[rows, :], hcot[:, lanes]) * slope).astype(bf16)

        @pl.loop(0, 4)
        def _(i):
            rows = rows_of(2 * i, 2)
            part[rows, lanes] = dot(up[rows, :], pre_grad[...]).astype(bf16)

    def gates_of(g):
        lanes = pl.ds(g * LANES, LANES)
        spots = 2 * N_BLK
        narrow_row = lax.broadcasted_iota(jnp.int32, (spots, 8 * N_BLK), 0)
        wide_row = lax.broadcasted_iota(jnp.int32, (spots, 8 * N_BLK), 1)
        compact = (wide_row == narrow_row // 2 * 8 + narrow_row % 2).astype(wide).astype(bf16)
        images = dot(compact, image_of_lane(g)).astype(bf16)

        @pl.loop(0, 4)
        def _(i):
            rows = rows_of(2 * i, 2)
            product = (dot(down_t[rows, :], act[...]) * ct[rows, lanes].astype(wide)).astype(bf16)
            for k in range(2):
                value = dot(images, product[k * NARROW : (k + 1) * NARROW], (1, 1))
                gate_part[2 * i + k, :, pl.ds(0, NARROW)] += value

    def weights(grads_of, left, right, g):
        lanes = pl.ds(g * LANES, LANES)

        @pl.loop(0, 3)
        def _(i):
            rows = pl.ds(pl.multiple_of(i * 192, 64), 192)
            value = dot(left[rows, :], right[:, lanes], (1, 1))
            if g == 0:
                grads_of[rows, :] = value
            else:
                grads_of[rows, :] += value

    def reduce(g):
        a = g // (GROUPS // 2)
        zf = at.home(a) % 2
        lanes_a = pl.ds(g * LANES, HALF)
        lanes_b = pl.ds(g * LANES + HALF, HALF)

        def mine(x, z, lanes):
            return part.at[rows_of(x * 2 + z), lanes]

        def go(src, dst, k, device):
            send(src, dst, sum_send.at[g, k], sum_recv.at[g, k], device, sent)

        def come(region, k):
            arrived(region, sum_send.at[g, k], sum_recv.at[g, k], at.across)

        def first():
            for x in range(4):
                go(mine(x, 1 - zf, lanes_b), first_b.at[g, x], 8 + x, at.across)
            go(mine(at.x_far, 0, lanes_a), first_a.at[g, 0], 0, at.right)
            go(mine(at.x_far, 1, lanes_a), first_a.at[g, 1], 1, at.left)
            go(mine(at.x_right, 1, lanes_a), second_a.at[g, 1], 2, at.right)
            go(mine(at.x_left, 0, lanes_a), second_a.at[g, 2], 3, at.left)

        def second():
            come(first_a.at[g, 0], 0)
            put(
                third_a.at[g, 0],
                first_a[g, 0].astype(wide) + mine(at.x_right, 0, lanes_a)[...].astype(wide),
            )
            go(third_a.at[g, 0], second_a.at[g, 0], 4, at.right)
            come(first_a.at[g, 1], 1)
            put(
                third_a.at[g, 1],
                first_a[g, 1].astype(wide) + mine(at.x_left, 1, lanes_a)[...].astype(wide),
            )
            go(third_a.at[g, 1], second_a.at[g, 3], 5, at.left)
            for x in range(4):
                come(first_b.at[g, x], 8 + x)
            for i, x in enumerate((at.x_far, at.x_right, at.x_left, at.x)):
                put(
                    mine_b.at[g, i],
                    first_b[g, x].astype(wide) + mine(x, zf, lanes_b)[...].astype(wide),
                )
                if i == 0:
                    go(mine_b.at[g, 0, :, pl.ds(0, HALF // 2)], second_b.at[g, 0], 12, at.right)
                    go(mine_b.at[g, 0, :, pl.ds(HALF // 2, HALF // 2)], second_b.at[g, 1], 13, at.left)
                if i == 1:
                    go(mine_b.at[g, 1, :, pl.ds(HALF // 2, HALF // 2)], second_b.at[g, 2], 14, at.right)
                if i == 2:
                    go(mine_b.at[g, 2, :, pl.ds(0, HALF // 2)], second_b.at[g, 3], 15, at.left)

        def third():
            come(second_a.at[g, 0], 4)
            come(second_a.at[g, 1], 2)
            come(second_a.at[g, 2], 3)
            come(second_a.at[g, 3], 5)
            sums = [
                second_a[g, z].astype(wide)
                + second_a[g, 2 + z].astype(wide)
                + mine(at.x, z, lanes_a)[...].astype(wide)
                for z in range(2)
            ]
            keep = jnp.where(zf == 0, sums[0], sums[1])
            give = jnp.where(zf == 0, sums[1], sums[0])
            put(third_a.at[g, 2], give)
            go(third_a.at[g, 2], third_a.at[g, 3], 6, at.across)
            put(total.at[g, :, pl.ds(0, HALF)], keep)
            come(second_b.at[g, 0], 12)
            put(
                second_b.at[g, 4],
                second_b[g, 0].astype(wide) + mine_b[g, 1, :, pl.ds(0, HALF // 2)].astype(wide),
            )
            go(second_b.at[g, 4], second_b.at[g, 6], 16, at.right)
            come(second_b.at[g, 1], 13)
            put(
                second_b.at[g, 5],
                second_b[g, 1].astype(wide) + mine_b[g, 2, :, pl.ds(HALF // 2, HALF // 2)].astype(wide),
            )
            go(second_b.at[g, 5], second_b.at[g, 7], 17, at.left)

        def fourth():
            come(third_a.at[g, 3], 6)
            put(
                total.at[g, :, pl.ds(0, HALF)],
                total[g, :, pl.ds(0, HALF)].astype(wide) + third_a[g, 3].astype(wide),
            )
            come(second_b.at[g, 6], 16)
            come(second_b.at[g, 2], 14)
            come(second_b.at[g, 3], 15)
            come(second_b.at[g, 7], 17)
            for i, (l, r) in enumerate(((6, 3), (2, 7))):
                put(
                    total.at[g, :, pl.ds(HALF + i * (HALF // 2), HALF // 2)],
                    second_b[g, l].astype(wide)
                    + second_b[g, r].astype(wide)
                    + mine_b[g, 3, :, pl.ds(i * (HALF // 2), HALF // 2)].astype(wide),
                )
            for i in range(LANES // CAP):
                j = g * (LANES // CAP) + i
                src = total.at[g, :, pl.ds(i * CAP, CAP)]
                dst = back.at[:, block_of(at.blk)]
                if j == 0:
                    pltpu.make_async_copy(src, dst, local_sem.at[3]).start()
                else:
                    send(src, dst, back_send.at[j, 0], back_recv.at[j, 0], owners[j], sent)

        return first, second, third, fourth

    def gate_first():
        for i in range(1, N_HID):
            q = (at.hid + i) % 8
            send(gate_part.at[q], gate_in.at[i], gate_send.at[i], gate_recv.at[i], hid_peers[i], sent)

    def gate_second():
        value = gate_part[at.hid]
        for i in range(1, N_HID):
            arrived(gate_in.at[i], gate_send.at[i], gate_recv.at[i], at.across)
            value = value + gate_in[i]
        gate_sum[...] = value
        for j in range(N_BLK):
            gate_out[j] = gate_sum[pl.ds(2 * j, 2)]
            src, dst = gate_out.at[j], gate_back.at[at.blk]
            if j == 0:
                pltpu.make_async_copy(src, dst, local_sem.at[4]).start()
            else:
                send(src, dst, back_send.at[j, 1], back_recv.at[j, 1], straight_owners[j], sent)

    make_payload(0)
    make_payload(1)

    @pl.loop(0, 9)
    def _(i):
        tile = pl.ds(pl.multiple_of(i * 128, 128), 128)
        up[tile, :] = up_t[:, tile].T
        down_t[tile, :] = down[:, tile].T

    results = [
        pltpu.make_async_copy(up_grads, up_out, local_sem.at[5]),
        pltpu.make_async_copy(down_grads, down_out, local_sem.at[6]),
    ]
    spreads = [spread(g) for g in range(GROUPS)]
    reduces = [reduce(g) for g in range(GROUPS)]
    for tick in range(GROUPS + 6):
        for k in range(4):
            if 0 <= tick - k < GROUPS:
                spreads[tick - k][k]()
            if tick == 0 and k == 0:
                for pair in range(2, N_BLK // 2):
                    make_payload(pair)
                spread_info()
        done = tick - 3
        if done == 0:
            gather_info()
        if 0 <= done < GROUPS:
            forward(done)
            reduces[done][0]()
        for k in range(1, 4):
            if 0 <= done - k < GROUPS:
                reduces[done - k][k]()
        if 0 <= done < GROUPS:
            gates_of(done)
            if done == GROUPS - 1:
                gate_first()
            weights(up_grads, pre_grad, xt, done)
            weights(down_grads, act, hcot, done)
            if done == GROUPS - 1:
                for copy in results:
                    copy.start()
        if done == GROUPS + 1:
            gate_second()

    for j in range(N_BLK):
        e = at.later(j)
        if j == 0:
            pltpu.make_async_copy(total.at[0, :, pl.ds(0, CAP)], back.at[:, block_of(e)], local_sem.at[3]).wait()
            pltpu.make_async_copy(gate_out.at[0], gate_back.at[e], local_sem.at[4]).wait()
        else:
            arrived(back.at[:, block_of(e)], back_send.at[j, 0], back_recv.at[j, 0], at.across)
            arrived(gate_back.at[e], back_send.at[j, 1], back_recv.at[j, 1], at.across)

    mixed = dot(back[...], chosen[...])
    scale = jnp.concatenate(
        [jnp.broadcast_to(1.0 + columns[1, :, b : b + 1], (NARROW, PATCHES)) for b in range(2)], axis=1
    )
    norm_grad = mixed * scale
    sums[0:1, :] = jnp.sum(norm_grad, axis=0, keepdims=True)
    sums[1:2, :] = jnp.sum(norm_grad * normed[...], axis=0, keepdims=True)
    for i in range(1, N_HID):
        send(sums, sums_all.at[i], end_send.at[N_BLK + i], end_recv.at[N_BLK + i], hid_peers[i], sent)
    lane = lax.broadcasted_iota(jnp.int32, (NARROW, 128), 1)
    listed = jnp.zeros((NARROW, 128), wide)
    for c, values in enumerate((mixed, mixed * normed[...])):
        for b in range(2):
            value = jnp.sum(values[:, b * PATCHES : (b + 1) * PATCHES], axis=1, keepdims=True)
            listed = jnp.where(lane == 2 * c + b, value, listed)
    listed = jnp.concatenate([listed, jnp.zeros((256 - NARROW, 128), wide)], axis=0).T
    gate_grad = gate_back[0]
    for e in range(1, N_BLK):
        gate_grad = gate_grad + gate_back[e]
    grads[...] = jnp.concatenate([listed[:4], gate_grad, jnp.zeros((2, 256), wide)], axis=0)
    for j in range(1, N_BLK):
        send(grads, grads_all.at[j], end_send.at[j], end_recv.at[j], straight[j], sent)
    grads_all[0] = grads[...]
    first, second = sums[0:1, :], sums[1:2, :]
    for i in range(1, N_HID):
        arrived(sums_all.at[i], end_send.at[N_BLK + i], end_recv.at[N_BLK + i], at.across)
        first = first + sums_all[i, 0:1, :]
        second = second + sums_all[i, 1:2, :]
    norm_grads[...] = norm_grad
    totals[...] = jnp.concatenate([first, second], axis=0)
    for j in range(1, N_BLK):
        arrived(grads_all.at[j], end_send.at[j], end_recv.at[j], at.across)
    for copy in results:
        copy.wait()
    for copy in sent:
        copy.wait_send()


def result_kernel(
    cotangent, norm_grads, normed, stats, totals, grads_all, table, up_in, down_in,
    token_grads, up_grads, down_grads, weight_grads, bias_grads, held, move_sem,
):
    f32 = jnp.float32
    share = up_in.shape[0] // 4
    loads, stores = [], []
    for i, (src, dst) in enumerate(((up_in, up_grads), (down_in, down_grads))):
        for k in range(4):
            rows = pl.ds(k * share, share)
            loads.append(pltpu.make_async_copy(src.at[rows], held.at[i, rows], move_sem.at[0, i, k]))
            stores.append(pltpu.make_async_copy(held.at[i, rows], dst.at[rows], move_sem.at[1, i, k]))
    for load in loads:
        load.start()
    token_grads[...] = (
        cotangent[...].astype(f32)
        + stats[1:2, :] * (norm_grads[...] - totals[0:1, :] / WIDTH - normed[...] * (totals[1:2, :] / WIDTH))
    ).astype(token_grads.dtype)
    for load, store in zip(loads, stores):
        load.wait()
        store.start()
    image_grads = grads_all[...].reshape(8 * N_BLK, 256)
    conditions = table[...].reshape(8 * N_BLK, 256)[:, 128:]
    kind = lax.broadcasted_iota(jnp.int32, (8 * N_BLK, 128), 0) % 8 // 2
    kind_wide = lax.broadcasted_iota(jnp.int32, (8 * N_BLK, 256), 0) % 8 // 2
    for c in range(3):
        value = dot(jnp.where(kind == c, conditions, 0.0), image_grads, (0, 0), lax.Precision.HIGHEST)
        weight_grads[c] = value[32 : 32 + WIDTH // N_BLK, :NARROW]
        bias_grads[c : c + 1, :] = jnp.sum(jnp.where(kind_wide == c, image_grads, 0.0), axis=0, keepdims=True)[
            :, :NARROW
        ]
    for store in stores:
        store.wait()


def results_of(*operands):
    vmem, anywhere = pl.BlockSpec(memory_space=pltpu.VMEM), pl.BlockSpec(memory_space=pl.ANY)
    f32 = jnp.float32
    hidden, width = operands[-1].shape
    return pl.pallas_call(
        result_kernel,
        out_shape=(
            jax.ShapeDtypeStruct((NARROW, TOKENS), jnp.bfloat16),
            jax.ShapeDtypeStruct((hidden, width), f32),
            jax.ShapeDtypeStruct((hidden, width), f32),
            jax.ShapeDtypeStruct((3, width // N_BLK, NARROW), f32),
            jax.ShapeDtypeStruct((3, NARROW), f32),
        ),
        in_specs=[vmem] * 7 + [anywhere] * 2,
        out_specs=[vmem, anywhere, anywhere, vmem, vmem],
        scratch_shapes=[pltpu.VMEM((2, hidden, width), f32), pltpu.SemaphoreType.DMA((2, 2, 4))],
        compiler_params=pltpu.CompilerParams(vmem_limit_bytes=60 * 2**20),
    )(*operands)


def run_experts(*operands):
    vmem = pl.BlockSpec(memory_space=pltpu.VMEM)
    bf16, f32 = jnp.bfloat16, jnp.float32
    hidden, width = operands[-1].shape
    dma = pltpu.SemaphoreType.DMA
    return pl.pallas_call(
        expert_kernel,
        out_shape=(
            jax.ShapeDtypeStruct((NARROW, TOKENS), f32),
            jax.ShapeDtypeStruct((NARROW, TOKENS), f32),
            jax.ShapeDtypeStruct((8, TOKENS), f32),
            jax.ShapeDtypeStruct((2, TOKENS), f32),
            jax.ShapeDtypeStruct((N_BLK, 8, 256), f32),
            jax.ShapeDtypeStruct((N_BLK, 8, 256), f32),
            jax.ShapeDtypeStruct((hidden, width), f32),
            jax.ShapeDtypeStruct((hidden, width), f32),
        ),
        in_specs=[vmem] * len(operands),
        out_specs=[vmem] * 6 + [pl.BlockSpec(memory_space=pl.ANY)] * 2,
        scratch_shapes=[
            pltpu.VMEM((SLOTS, TOKENS), bf16),
            pltpu.VMEM((2 * NARROW, 2 * TOKENS), bf16),
            pltpu.VMEM((8, 2 * TOKENS), jnp.int32),
            pltpu.VMEM((2 * NARROW, SLOTS), bf16),
            pltpu.VMEM((NARROW, SLOTS), bf16),
            pltpu.VMEM((N_BLK, 2, 256), f32),
            pltpu.VMEM((2, TOKENS), f32),
            pltpu.VMEM((N_HID, 2, TOKENS), f32),
            pltpu.VMEM((8, 256), f32),
            pltpu.VMEM((hidden, width), f32),
            pltpu.VMEM((hidden, width), f32),
            pltpu.VMEM((width, SLOTS), bf16),
            pltpu.VMEM((width, SLOTS), bf16),
            pltpu.VMEM((width, SLOTS), bf16),
            pltpu.VMEM((hidden, LANES), bf16),
            pltpu.VMEM((hidden, LANES), bf16),
            pltpu.VMEM((width, SLOTS), bf16),
            pltpu.VMEM((width, hidden), bf16),
            pltpu.VMEM((width, hidden), bf16),
            pltpu.VMEM((width, 128), bf16),
            pltpu.VMEM((8 * N_BLK, 128), f32),
            pltpu.VMEM((N_HID, 2 * N_BLK, 256), f32),
            pltpu.VMEM((GROUPS, 2, NARROW, HALF), bf16),
            pltpu.VMEM((GROUPS, 4, NARROW, HALF), bf16),
            pltpu.VMEM((GROUPS, 4, NARROW, HALF), bf16),
            pltpu.VMEM((GROUPS, 4, NARROW, HALF), bf16),
            pltpu.VMEM((GROUPS, 8, NARROW, HALF // 2), bf16),
            pltpu.VMEM((GROUPS, 4, NARROW, HALF), bf16),
            pltpu.VMEM((GROUPS, NARROW, LANES), bf16),
            pltpu.VMEM((N_HID, 2 * N_BLK, 256), f32),
            pltpu.VMEM((2 * N_BLK, 256), f32),
            pltpu.VMEM((N_BLK, 2, 256), f32),
            dma((N_BLK, 3)),
            dma((N_BLK, 3)),
            dma((GROUPS, 14)),
            dma((GROUPS, 14)),
            dma((N_HID,)),
            dma((N_HID,)),
            dma((GROUPS, 18)),
            dma((GROUPS, 18)),
            dma((N_BLK, 2)),
            dma((N_BLK, 2)),
            dma((N_HID,)),
            dma((N_HID,)),
            dma((N_BLK + N_HID,)),
            dma((N_BLK + N_HID,)),
            dma((7,)),
        ],
        compiler_params=pltpu.CompilerParams(
            collective_id=0, has_side_effects=True, vmem_limit_bytes=60 * 2**20
        ),
    )(*operands)


def on_device(
    tokens,
    cotangent,
    route_weight,
    expert_ids,
    timesteps,
    time_table,
    up_weight,
    down_weight,
    modulation_weight,
    modulation_bias,
):
    ids = expert_ids.T
    by_feature = modulation_weight.transpose(1, 2, 0).reshape(3 * NARROW, WIDTH)
    columns, info = modulation(timesteps, time_table, by_feature, modulation_bias, ids)
    turned = cotangent.T
    partial_results = run_experts(
        tokens, turned, route_weight.T, ids, columns, info, up_weight[0].T, down_weight[0]
    )
    token_grads, up_grads, down_grads, weight_grads, bias_grads = results_of(turned, *partial_results)
    return (token_grads.T, up_grads.T[None], down_grads[None], weight_grads.transpose(1, 0, 2), bias_grads)


def solution(mesh):
    in_specs = (
        P("blk", None),
        P("blk", "hid"),
        P("blk", None),
        P("blk", None),
        P("blk"),
        P(),
        P("blk", None, "hid"),
        P("blk", "hid", None),
        P(None, None, "hid"),
        P(None, "hid"),
    )
    out_specs = (
        P("blk", "hid"),
        P("blk", None, "hid"),
        P("blk", "hid", None),
        P("blk", None, "hid"),
        P(None, "hid"),
    )
    return jax.shard_map(
        on_device, mesh=mesh, in_specs=in_specs, out_specs=out_specs, check_vma=False
    )
```

```python
import math

import jax
import jax.numpy as jnp
from jax import lax
from jax.experimental import pallas as pl
from jax.experimental.pallas import tpu as pltpu
from jax.sharding import PartitionSpec as P

MESH = pl.DeviceIdType.MESH
norm_epsilon = 1e-06
gelu_cubic = 0.044715
gelu_factor = math.sqrt(2.0 / math.pi)

N_BLK, N_HID = 16, 8
WIDTH, NARROW, CAP = 1152, 144, 128
TOKENS, PATCHES = 512, 256
SLOTS = N_BLK * CAP
GROUPS = 4
LANES = SLOTS // GROUPS
HALF = LANES // 2
ORDER = (0, 1, 6, 2, 7, 3, 5, 4)


def shift(j):
    return j // 8, ORDER[j % 8]


class Place:
    def __init__(self):
        self.blk = lax.axis_index("blk")
        self.hid = lax.axis_index("hid")
        self.z_hi, self.m = self.blk // 8, self.blk % 8
        self.x, self.z_lo = self.hid // 2, self.hid % 2
        self.x_right, self.x_left, self.x_far = [(self.x + i) % 4 for i in (1, 3, 2)]
        self.right = (self.blk, self.x_right * 2 + self.z_lo)
        self.left = (self.blk, self.x_left * 2 + self.z_lo)
        self.across = (self.blk, self.home(1))

    def home(self, a):
        return self.hid if a == 0 else self.hid + 1 - 2 * self.z_lo

    def later(self, j):
        a, m = shift(j)
        return (self.z_hi + a) % 2 * 8 + (self.m + m) % 8

    def earlier(self, j):
        a, m = shift(j)
        return (self.z_hi + a) % 2 * 8 + (self.m + 8 - m) % 8

    def hid_peer(self, i):
        return (self.blk, (self.hid + i) % 8)


def greet(devices):
    barrier = pltpu.get_barrier_semaphore()
    for device in devices:
        pl.semaphore_signal(barrier, inc=1, device_id=device, device_id_type=MESH)
    pl.semaphore_wait(barrier, len(devices))


def send(src, dst, send_sem, recv_sem, device, sent):
    copy = pltpu.make_async_remote_copy(
        src_ref=src, dst_ref=dst, send_sem=send_sem, recv_sem=recv_sem, device_id=device, device_id_type=MESH
    )
    copy.start()
    sent.append(copy)


def arrived(region, send_sem, recv_sem, device):
    pltpu.make_async_remote_copy(
        src_ref=region, dst_ref=region, send_sem=send_sem, recv_sem=recv_sem, device_id=device, device_id_type=MESH
    ).wait_recv()


def rows_of(slice_index, count=1):
    return pl.ds(pl.multiple_of(slice_index * NARROW, 16), count * NARROW)


def block_of(index):
    return pl.ds(pl.multiple_of(index * CAP, CAP), CAP)


def gelu_both(values):
    square = values * values
    inner = gelu_factor * (values + gelu_cubic * values * square)
    tangent = jnp.tanh(inner)
    slope = 0.5 * (1.0 + tangent) + 0.5 * values * (1.0 - tangent * tangent) * gelu_factor * (
        1.0 + 3.0 * gelu_cubic * square
    )
    return 0.5 * values * (1.0 + tangent), slope


def dot(a, b, contract=(1, 0), precision=None):
    return lax.dot_general(
        a, b, (((contract[0],), (contract[1],)), ((), ())), precision=precision, preferred_element_type=jnp.float32
    )


def modulation_kernel(steps, table, weight, bias, ids, columns, info, rows, lookup_sem):
    f32 = jnp.float32
    copies = [
        pltpu.make_async_copy(table.at[pl.ds(steps[b], 1)], rows.at[pl.ds(b, 1)], lookup_sem.at[b]) for b in range(2)
    ]
    for copy in copies:
        copy.start()
    bias_columns = jnp.concatenate([bias[...], jnp.zeros((3, 256 - NARROW), f32)], axis=1)
    bias_columns = jnp.concatenate([bias_columns, jnp.zeros((125, 256), f32)], axis=0).T
    expert = lax.broadcasted_iota(jnp.int32, (N_BLK, 256), 0)
    named = ((expert == ids[0:1, :256]) | (expert == ids[1:2, :256])).astype(jnp.bfloat16)
    counts = dot(jnp.ones((8, 256), jnp.bfloat16), named, (1, 1))
    for copy in copies:
        copy.wait()
    looked = rows[pl.ds(0, 2)]
    condition = looked / (1.0 + jnp.exp(-looked))
    lane = lax.broadcasted_iota(jnp.int32, (NARROW, 128), 1)
    for c in range(3):
        part = weight[c * NARROW : (c + 1) * NARROW]
        sums = [
            jnp.sum(part * condition[b : b + 1], axis=1, keepdims=True) + bias_columns[:NARROW, c : c + 1]
            for b in range(2)
        ]
        value = jnp.where(lane % 2 == 0, sums[0], sums[1])
        listed = value if c == 0 else jnp.where(lane // 2 == c, value, listed)
    columns[...] = listed
    gate = value
    gate = jnp.concatenate([gate, jnp.zeros((256 - NARROW, 128), f32)], axis=0).T[:8]
    high = gate.astype(jnp.bfloat16).astype(f32)
    middle = (gate - high).astype(jnp.bfloat16).astype(f32)
    low = (gate - high) - middle
    parts = jnp.concatenate([high[:2], middle[:2], low[:2], jnp.zeros((2, 256), f32)], axis=0)[:, :NARROW]
    repeated = jnp.concatenate([condition] * 4, axis=0)
    share = WIDTH // N_BLK
    for e in range(N_BLK):
        info[e] = jnp.concatenate(
            [parts, counts, repeated[:, e * share : (e + 1) * share], jnp.zeros((8, 96 - share), f32)], axis=1
        )


def modulation(timesteps, time_table, weight, bias, ids):
    vmem = pl.BlockSpec(memory_space=pltpu.VMEM)
    f32 = jnp.float32
    return pl.pallas_call(
        modulation_kernel,
        out_shape=(
            jax.ShapeDtypeStruct((NARROW, 128), f32),
            jax.ShapeDtypeStruct((N_BLK, 8, 256), f32),
        ),
        in_specs=[pl.BlockSpec(memory_space=pltpu.SMEM), pl.BlockSpec(memory_space=pl.ANY), vmem, vmem, vmem],
        out_specs=[vmem] * 2,
        scratch_shapes=[pltpu.VMEM((8, WIDTH), f32), pltpu.SemaphoreType.DMA((2,))],
        compiler_params=pltpu.CompilerParams(vmem_limit_bytes=60 * 2**20),
    )(timesteps, time_table, weight, bias, ids)


def expert_kernel(
    tokens, cotangent, route, ids, columns, info, up_t, down,
    norm_grads, normed, stats, totals, grads_all, table, up_out, down_out,
    chosen, both, four, four_normed, four_columns, targets, payload, four_payload, back, gate_back, sums, sums_all, grads, up_grads, down_grads,
    xt, ct, hcot, act, pre_grad, part, up, down_t, gate_lanes, counts, gate_part,
    first_a, second_a, third_a, first_b, second_b, mine_b, total, gate_in, gate_sum, gate_out,
    a2a_send, a2a_recv, ring_send, ring_recv, info_send, info_recv,
    sum_send, sum_recv, back_send, back_recv, gate_send, gate_recv, end_send, end_recv, near_send, near_recv, local_sem,
):
    at = Place()
    wide = jnp.float32
    bf16 = jnp.bfloat16
    peers = [(at.later(j), at.home(j // 8)) for j in range(N_BLK)]
    straight = [(at.later(j), at.hid) for j in range(N_BLK)]
    owners = [(at.earlier(j), at.home(j // 8)) for j in range(N_BLK)]
    straight_owners = [(at.earlier(j), at.hid) for j in range(N_BLK)]
    hid_peers = [at.hid_peer(i) for i in range(N_HID)]
    everyone = peers[1:] + straight[8:] + hid_peers[1:]
    barrier = pltpu.get_barrier_semaphore()
    for device in everyone:
        pl.semaphore_signal(barrier, inc=1, device_id=device, device_id_type=MESH)
    own = rows_of(at.hid)
    sent = []

    def put(ref, value):
        ref[...] = value.astype(ref.dtype)

    @pl.loop(0, TOKENS // 128)
    def _(i):
        rows = pl.ds(pl.multiple_of(i * 128, 128), 128)
        values = tokens[rows, :].astype(wide)
        mean = jnp.sum(values, axis=1, keepdims=True) / WIDTH
        spread_of = jnp.sum((values - mean) ** 2, axis=1, keepdims=True) / WIDTH
        inverse = 1.0 / jnp.sqrt(spread_of + norm_epsilon)
        lane = lax.broadcasted_iota(jnp.int32, (128, 128), 1)
        stats[:, rows] = jnp.where(lane == 0, mean, inverse).T[:8]

    row = lax.broadcasted_iota(jnp.int32, (NARROW, WIDTH), 0)
    column = lax.broadcasted_iota(jnp.int32, (NARROW, WIDTH), 1)
    pick = (column == row + at.hid * NARROW).astype(wide).astype(bf16)
    normed[...] = (dot(pick, tokens[...], (1, 1)) - stats[0:1, :]) * stats[1:2, :]
    for b in range(2):
        half = slice(b * PATCHES, (b + 1) * PATCHES)
        hin = normed[:, half] * (1.0 + columns[:, 2 + b : 3 + b]) + columns[:, b : b + 1]
        for k in range(2):
            both[:NARROW, k * TOKENS + b * PATCHES : k * TOKENS + (b + 1) * PATCHES] = hin.astype(bf16)
    for k in range(2):
        weighted = cotangent[...].astype(wide) * route[k : k + 1, :]
        both[NARROW:, k * TOKENS : (k + 1) * TOKENS] = weighted.astype(bf16)

    expert = lax.broadcasted_iota(jnp.int32, (N_BLK, TOKENS), 0)
    named = [(expert == ids[k : k + 1, :]) for k in range(2)]
    earlier_row = lax.broadcasted_iota(jnp.int32, (TOKENS, TOKENS), 0)
    earlier_lane = lax.broadcasted_iota(jnp.int32, (TOKENS, TOKENS), 1)
    before = dot(
        (named[0] | named[1]).astype(wide).astype(bf16), (earlier_row < earlier_lane).astype(wide).astype(bf16)
    )
    for k in range(2):
        slot = jnp.sum(jnp.where(named[k], before, 0.0), axis=0, keepdims=True)
        targets[0:1, k * TOKENS : (k + 1) * TOKENS] = ids[k : k + 1, :] * CAP + slot.astype(jnp.int32)

    gate_part[...] = jnp.zeros_like(gate_part)
    row = lax.broadcasted_iota(jnp.int32, (4 * NARROW, WIDTH), 0)
    column = lax.broadcasted_iota(jnp.int32, (4 * NARROW, WIDTH), 1)
    wanted = row + jnp.where(row < 2 * NARROW, at.x * 2 * NARROW, (at.x_far - 1) * 2 * NARROW)
    pick = (column == wanted).astype(wide).astype(bf16)
    four_normed[...] = (dot(pick, tokens[...], (1, 1)) - stats[0:1, :]) * stats[1:2, :]
    four_columns[at.z_lo] = columns[...]
    pl.semaphore_wait(barrier, len(everyone))

    near = (at.across, (at.blk, at.x_far * 2 + at.z_lo), (at.blk, at.x_far * 2 + 1 - at.z_lo))
    near_place = (at.z_lo, 2 + at.z_lo, 2 + at.z_lo)
    near_from = (1 - at.z_lo, 2 + at.z_lo, 3 - at.z_lo)
    for i in range(3):
        send(columns, four_columns.at[near_place[i]], near_send.at[i], near_recv.at[i], near[i], sent)

    for j in range(N_BLK):
        target = at.later(j)
        if j == 0:
            info_local = pltpu.make_async_copy(info.at[target], table.at[0], local_sem.at[2])
            info_local.start()
        else:
            send(info.at[target], table.at[j], a2a_send.at[j, 2], a2a_recv.at[j, 2], straight[j], sent)

    def payload_parts(j):
        lanes = pl.ds(j * CAP, CAP)
        return (
            (payload.at[pl.ds(0, NARROW), lanes], xt.at[own, lanes]),
            (payload.at[pl.ds(NARROW, NARROW), lanes], ct.at[own, lanes]),
        )

    def hits_of(pair):
        hits = []
        for j in (2 * pair, 2 * pair + 1):
            slots = lax.broadcasted_iota(jnp.int32, (CAP, 2 * TOKENS), 0) + at.later(j) * CAP
            hit = (slots == targets[0:1, :]).astype(wide)
            chosen[block_of(at.later(j)), :] = (hit[:, :TOKENS] + hit[:, TOKENS:]).astype(bf16)
            hits.append(hit.astype(bf16))
        return jnp.concatenate(hits, axis=0)

    def make_payload(pair):
        value = dot(both[...], hits_of(pair), (1, 1))
        payload[:, 2 * pair * CAP : (2 * pair + 2) * CAP] = value.astype(bf16)
        for j in (2 * pair, 2 * pair + 1):
            for i, (src, dst) in enumerate(payload_parts(j)):
                if j == 0:
                    pltpu.make_async_copy(src, dst, local_sem.at[i]).start()
                else:
                    send(src, dst, a2a_send.at[j, i], a2a_recv.at[j, i], peers[j], sent)

    def make_four():
        for i in range(3):
            arrived(four_columns.at[near_from[i]], near_send.at[i], near_recv.at[i], near[i])
        for q in range(4):
            rows = slice(q * NARROW, (q + 1) * NARROW)
            for b in range(2):
                half = slice(b * PATCHES, (b + 1) * PATCHES)
                hin = four_normed[rows, half] * (1.0 + four_columns[q, :, 2 + b : 3 + b])
                hin = (hin + four_columns[q, :, b : b + 1]).astype(bf16)
                for k in range(2):
                    four[rows, k * TOKENS + b * PATCHES : k * TOKENS + (b + 1) * PATCHES] = hin

        four[4 * NARROW :, :] = both[NARROW:, :]

    four_rows = (pl.ds(0, 2 * NARROW), pl.ds(2 * NARROW, 2 * NARROW), pl.ds(4 * NARROW, NARROW))

    def four_parts(j):
        lanes = pl.ds(j * CAP, CAP)
        targets_of = (xt.at[rows_of(at.x * 2, 2), lanes], xt.at[rows_of(at.x_far * 2, 2), lanes], ct.at[own, lanes])
        return [
            (four_payload.at[rows, pl.ds(j * CAP - LANES, CAP)], dst) for rows, dst in zip(four_rows, targets_of)
        ]

    def make_four_payload(g):
        for pair in range(g * LANES // CAP // 2, (g + 1) * LANES // CAP // 2):
            hits = hits_of(pair)
            start = 2 * pair * CAP - LANES
            for rows in four_rows:
                four_payload[rows, start : start + 2 * CAP] = dot(four[rows, :], hits, (1, 1)).astype(bf16)
            for j in (2 * pair, 2 * pair + 1):
                for k, (src, dst) in zip((0, 3, 1), four_parts(j)):
                    send(src, dst, a2a_send.at[j, k], a2a_recv.at[j, k], peers[j], sent)

    def from_peer(j, i, region):
        if j == 0:
            pltpu.make_async_copy(*payload_parts(0)[i], local_sem.at[i]).wait()
        else:
            arrived(region, a2a_send.at[j, i], a2a_recv.at[j, i], peers[j])

    def spread(g):
        a = g // (GROUPS // 2)
        f = at.home(a)
        other = at.home(1 - a)
        zf = f % 2
        lanes = pl.ds(g * LANES, LANES)
        halves = [pl.ds(g * LANES + i * HALF, HALF) for i in range(2)]
        far_slice = at.x_far * 2 + zf

        def go(array, rows, cols, k, device):
            region = array.at[rows, cols]
            send(region, region, ring_send.at[g, k], ring_recv.at[g, k], device, sent)

        def come(array, rows, cols, k):
            arrived(array.at[rows, cols], ring_send.at[g, k], ring_recv.at[g, k], at.across)

        def first():
            for j in range(g * LANES // CAP, (g + 1) * LANES // CAP):
                block = pl.ds(j * CAP, CAP)
                from_peer(j, 1, ct.at[rows_of(f), block])
                if g == 0:
                    from_peer(j, 0, xt.at[rows_of(f), block])
                else:
                    from_peer(j, 0, xt.at[rows_of(at.x * 2, 2), block])
                    from_peer(j, 3, xt.at[rows_of(at.x_far * 2, 2), block])
            if g == 0:
                go(xt, rows_of(f), lanes, 0, at.across)
            go(ct, rows_of(f), lanes, 6, at.right)
            go(ct, rows_of(f), lanes, 7, at.left)
            go(ct, rows_of(f), lanes, 5, at.across)
            if g > 0:
                go(xt, rows_of(at.x * 2, 2), lanes, 1, at.right)
                go(xt, rows_of(at.x * 2, 2), lanes, 2, at.left)

        def second():
            if g == 0:
                come(xt, rows_of(other), lanes, 0)
                go(xt, rows_of(at.x * 2, 2), lanes, 1, at.right)
                go(xt, rows_of(at.x * 2, 2), lanes, 2, at.left)
            left, right = rows_of(at.x_left * 2 + zf), rows_of(at.x_right * 2 + zf)
            come(ct, left, lanes, 6)
            go(ct, left, halves[0], 8, at.right)
            go(ct, left, lanes, 10, at.across)
            come(ct, right, lanes, 7)
            go(ct, right, halves[1], 9, at.left)
            go(ct, right, lanes, 11, at.across)

        def third():
            if g == 0:
                come(xt, rows_of(at.x_left * 2, 2), lanes, 1)
                go(xt, rows_of(at.x_left * 2), lanes, 3, at.right)
                come(xt, rows_of(at.x_right * 2, 2), lanes, 2)
                go(xt, rows_of(at.x_right * 2 + 1), lanes, 4, at.left)
            for i in range(2):
                come(ct, rows_of(far_slice), halves[i], 8 + i)
                go(ct, rows_of(far_slice), halves[i], 12 + i, at.across)

        def fourth():
            if g == 0:
                come(xt, rows_of(at.x_far * 2), lanes, 3)
                come(xt, rows_of(at.x_far * 2 + 1), lanes, 4)
            else:
                come(xt, rows_of(at.x_left * 2, 2), lanes, 1)
                come(xt, rows_of(at.x_right * 2, 2), lanes, 2)
            come(ct, rows_of(other), lanes, 5)
            come(ct, rows_of(at.x_left * 2 + 1 - zf), lanes, 10)
            come(ct, rows_of(at.x_right * 2 + 1 - zf), lanes, 11)
            for i in range(2):
                come(ct, rows_of(at.x_far * 2 + 1 - zf), halves[i], 12 + i)

        return first, second, third, fourth

    def spread_info():
        info_local.wait()
        for j in range(1, N_BLK):
            arrived(table.at[j], a2a_send.at[j, 2], a2a_recv.at[j, 2], straight[j])
        rows = table[...].reshape(8 * N_BLK, 256)
        gate_lanes[own, :] = rows.T[:NARROW].astype(bf16)
        region = gate_lanes.at[own]
        for i in range(1, N_HID):
            send(region, region, info_send.at[i], info_recv.at[i], hid_peers[i], sent)
        lane = lax.broadcasted_iota(jnp.int32, (8 * N_BLK, 128), 1)
        mine = jnp.sum(jnp.where(lane == at.blk + 16, rows[:, 128:], 0.0), axis=1, keepdims=True)
        counts[...] = jnp.broadcast_to(mine, counts.shape)

    def gather_info():
        for i in range(1, N_HID):
            region = gate_lanes.at[rows_of((at.hid + 8 - i) % 8)]
            arrived(region, info_send.at[i], info_recv.at[i], at.across)

    def image_of_lane(g):
        shape = (8 * N_BLK, LANES)
        row = lax.broadcasted_iota(jnp.int32, shape, 0)
        lane = lax.broadcasted_iota(jnp.int32, shape, 1)
        block = lane // CAP + g * (LANES // CAP)
        first_count = jnp.concatenate([counts[...]] * (LANES // 128), axis=1)
        is_first = (lane % CAP).astype(wide) < first_count
        hit = (row // 8 == block) & (is_first == (row % 2 == 0)) & (row % 8 < 6)
        return jnp.where(hit, 1.0, 0.0).astype(bf16)

    def forward(g):
        lanes = pl.ds(g * LANES, LANES)
        images = image_of_lane(g)

        @pl.loop(0, 4)
        def _(i):
            rows = rows_of(2 * i, 2)
            gates = dot(gate_lanes[rows, :], images)
            hcot[rows, lanes] = (gates * ct[rows, lanes].astype(wide)).astype(bf16)

        @pl.loop(0, 3)
        def _(i):
            rows = pl.ds(pl.multiple_of(i * 192, 64), 192)
            activated, slope = gelu_both(dot(up_t[rows, :], xt[:, lanes]))
            act[rows, :] = activated.astype(bf16)
            pre_grad[rows, :] = (dot(down[rows, :], hcot[:, lanes]) * slope).astype(bf16)

        @pl.loop(0, 4)
        def _(i):
            rows = rows_of(2 * i, 2)
            part[rows, lanes] = dot(up[rows, :], pre_grad[...]).astype(bf16)

    def gates_of(g):
        lanes = pl.ds(g * LANES, LANES)
        spots = 2 * N_BLK
        narrow_row = lax.broadcasted_iota(jnp.int32, (spots, 8 * N_BLK), 0)
        wide_row = lax.broadcasted_iota(jnp.int32, (spots, 8 * N_BLK), 1)
        compact = (wide_row == narrow_row // 2 * 8 + narrow_row % 2).astype(wide).astype(bf16)
        images = dot(compact, image_of_lane(g)).astype(bf16)

        @pl.loop(0, 4)
        def _(i):
            rows = rows_of(2 * i, 2)
            product = (dot(down_t[rows, :], act[...]) * ct[rows, lanes].astype(wide)).astype(bf16)
            for k in range(2):
                value = dot(images, product[k * NARROW : (k + 1) * NARROW], (1, 1))
                gate_part[2 * i + k, :, pl.ds(0, NARROW)] += value

    def weights(grads_of, left, right, g):
        lanes = pl.ds(g * LANES, LANES)

        @pl.loop(0, 3)
        def _(i):
            rows = pl.ds(pl.multiple_of(i * 192, 64), 192)
            value = dot(left[rows, :], right[:, lanes], (1, 1))
            if g == 0:
                grads_of[rows, :] = value
            else:
                grads_of[rows, :] += value

    def reduce(g, along_x):
        a = g // (GROUPS // 2)
        zf = at.home(a) % 2
        lanes_a = pl.ds(g * LANES, along_x)
        along_z = LANES - along_x
        lanes_b = pl.ds(g * LANES + along_x, along_z)
        low, high = pl.ds(0, along_z // 2), pl.ds(along_z // 2, along_z // 2)

        def mine(x, z, lanes):
            return part.at[rows_of(x * 2 + z), lanes]

        def go(src, dst, k, device):
            send(src, dst, sum_send.at[g, k], sum_recv.at[g, k], device, sent)

        def come(region, k):
            arrived(region, sum_send.at[g, k], sum_recv.at[g, k], at.across)

        def view(buffer, i):
            return buffer.at[g, i, :, pl.ds(0, along_x)]

        def from_z(x):
            return first_b.at[g, x, :, pl.ds(0, along_z)]

        def from_x(i):
            return second_b.at[g, i, :, low]

        def first():
            if along_z:
                for x in range(4):
                    go(mine(x, 1 - zf, lanes_b), from_z(x), 8 + x, at.across)
            if along_x:
                go(mine(at.x_far, 0, lanes_a), view(first_a, 0), 0, at.right)
                go(mine(at.x_far, 1, lanes_a), view(first_a, 1), 1, at.left)
                go(mine(at.x_right, 1, lanes_a), view(second_a, 1), 2, at.right)
                go(mine(at.x_left, 0, lanes_a), view(second_a, 2), 3, at.left)

        def second():
            if along_x:
                come(view(first_a, 0), 0)
                put(view(third_a, 0), view(first_a, 0)[...].astype(wide) + mine(at.x_right, 0, lanes_a)[...].astype(wide))
                go(view(third_a, 0), view(second_a, 0), 4, at.right)
                come(view(first_a, 1), 1)
                put(view(third_a, 1), view(first_a, 1)[...].astype(wide) + mine(at.x_left, 1, lanes_a)[...].astype(wide))
                go(view(third_a, 1), view(second_a, 3), 5, at.left)
            if not along_z:
                return
            for x in range(4):
                come(from_z(x), 8 + x)
            for i, x in enumerate((at.x_far, at.x_right, at.x_left, at.x)):
                put(
                    mine_b.at[g, i, :, pl.ds(0, along_z)],
                    from_z(x)[...].astype(wide) + mine(x, zf, lanes_b)[...].astype(wide),
                )
                if i == 0:
                    go(mine_b.at[g, 0, :, low], from_x(0), 12, at.right)
                    go(mine_b.at[g, 0, :, high], from_x(1), 13, at.left)
                if i == 1:
                    go(mine_b.at[g, 1, :, high], from_x(2), 14, at.right)
                if i == 2:
                    go(mine_b.at[g, 2, :, low], from_x(3), 15, at.left)

        def third():
            if along_x:
                for i, k in enumerate((4, 2, 3, 5)):
                    come(view(second_a, i), k)
                sums_of = [
                    view(second_a, z)[...].astype(wide)
                    + view(second_a, 2 + z)[...].astype(wide)
                    + mine(at.x, z, lanes_a)[...].astype(wide)
                    for z in range(2)
                ]
                put(view(third_a, 2), jnp.where(zf == 0, sums_of[1], sums_of[0]))
                go(view(third_a, 2), view(third_a, 3), 6, at.across)
                put(total.at[g, :, pl.ds(0, along_x)], jnp.where(zf == 0, sums_of[0], sums_of[1]))
            if not along_z:
                return
            come(from_x(0), 12)
            put(from_x(4), from_x(0)[...].astype(wide) + mine_b[g, 1, :, low].astype(wide))
            go(from_x(4), from_x(6), 16, at.right)
            come(from_x(1), 13)
            put(from_x(5), from_x(1)[...].astype(wide) + mine_b[g, 2, :, high].astype(wide))
            go(from_x(5), from_x(7), 17, at.left)

        def fourth():
            if along_x:
                come(view(third_a, 3), 6)
                region = total.at[g, :, pl.ds(0, along_x)]
                put(region, region[...].astype(wide) + view(third_a, 3)[...].astype(wide))
            for i, k in ((6, 16), (2, 14), (3, 15), (7, 17)):
                if along_z:
                    come(from_x(i), k)
            for i, (l, r, cols) in enumerate(((6, 3, low), (2, 7, high)) if along_z else ()):
                put(
                    total.at[g, :, pl.ds(along_x + i * (along_z // 2), along_z // 2)],
                    from_x(l)[...].astype(wide) + from_x(r)[...].astype(wide) + mine_b[g, 3, :, cols].astype(wide),
                )
            for i in range(LANES // CAP):
                j = g * (LANES // CAP) + i
                src = total.at[g, :, pl.ds(i * CAP, CAP)]
                dst = back.at[:, block_of(at.blk)]
                if j == 0:
                    pltpu.make_async_copy(src, dst, local_sem.at[3]).start()
                else:
                    send(src, dst, back_send.at[j, 0], back_recv.at[j, 0], owners[j], sent)

        return first, second, third, fourth

    def gate_first():
        for i in range(1, N_HID):
            q = (at.hid + i) % 8
            send(gate_part.at[q], gate_in.at[i], gate_send.at[i], gate_recv.at[i], hid_peers[i], sent)

    def gate_second():
        value = gate_part[at.hid]
        for i in range(1, N_HID):
            arrived(gate_in.at[i], gate_send.at[i], gate_recv.at[i], at.across)
            value = value + gate_in[i]
        gate_sum[...] = value
        for j in range(N_BLK):
            gate_out[j] = gate_sum[pl.ds(2 * j, 2)]
            src, dst = gate_out.at[j], gate_back.at[at.blk]
            if j == 0:
                pltpu.make_async_copy(src, dst, local_sem.at[4]).start()
            else:
                send(src, dst, back_send.at[j, 1], back_recv.at[j, 1], straight_owners[j], sent)

    make_payload(0)
    make_payload(1)

    @pl.loop(0, 9)
    def _(i):
        tile = pl.ds(pl.multiple_of(i * 128, 128), 128)
        up[tile, :] = up_t[:, tile].T
        down_t[tile, :] = down[:, tile].T

    results = [
        pltpu.make_async_copy(up_grads, up_out, local_sem.at[5]),
        pltpu.make_async_copy(down_grads, down_out, local_sem.at[6]),
    ]
    spreads = [spread(g) for g in range(GROUPS)]
    reduces = [reduce(g, along_x) for g, along_x in enumerate((HALF, LANES, HALF, HALF))]
    def finish_group(g):
        gates_of(g)
        if g == GROUPS - 1:
            gate_first()
        weights(up_grads, pre_grad, xt, g)
        weights(down_grads, act, hcot, g)

    spreads[0][0]()
    spread_info()
    make_four()
    make_four_payload(1)
    make_four_payload(2)
    spreads[0][1]()
    spreads[1][0]()
    make_four_payload(3)
    spreads[0][2]()
    spreads[1][1]()
    spreads[2][0]()
    spreads[0][3]()
    gather_info()
    forward(0)
    reduces[0][0]()
    spreads[2][1]()
    spreads[1][2]()
    spreads[3][0]()
    finish_group(0)
    for g in range(1, GROUPS + 3):
        for k in (1, 2, 3):
            if g + 3 - k < GROUPS:
                spreads[g + 3 - k][k]()
        if g < GROUPS:
            forward(g)
            reduces[g][0]()
        for k in (1, 2, 3):
            if 0 <= g - k < GROUPS:
                reduces[g - k][k]()
        if g < GROUPS:
            finish_group(g)
        if g == GROUPS - 1:
            for copy in results:
                copy.start()
        if g == GROUPS + 1:
            gate_second()

    for j in range(N_BLK):
        e = at.later(j)
        if j == 0:
            pltpu.make_async_copy(total.at[0, :, pl.ds(0, CAP)], back.at[:, block_of(e)], local_sem.at[3]).wait()
            pltpu.make_async_copy(gate_out.at[0], gate_back.at[e], local_sem.at[4]).wait()
        else:
            arrived(back.at[:, block_of(e)], back_send.at[j, 0], back_recv.at[j, 0], at.across)
            arrived(gate_back.at[e], back_send.at[j, 1], back_recv.at[j, 1], at.across)

    mixed = dot(back[...], chosen[...])
    scale = jnp.concatenate(
        [jnp.broadcast_to(1.0 + columns[:, 2 + b : 3 + b], (NARROW, PATCHES)) for b in range(2)], axis=1
    )
    norm_grad = mixed * scale
    sums[0:1, :] = jnp.sum(norm_grad, axis=0, keepdims=True)
    sums[1:2, :] = jnp.sum(norm_grad * normed[...], axis=0, keepdims=True)
    for i in range(1, N_HID):
        send(sums, sums_all.at[i], end_send.at[N_BLK + i], end_recv.at[N_BLK + i], hid_peers[i], sent)
    lane = lax.broadcasted_iota(jnp.int32, (NARROW, 128), 1)
    listed = jnp.zeros((NARROW, 128), wide)
    for c, values in enumerate((mixed, mixed * normed[...])):
        for b in range(2):
            value = jnp.sum(values[:, b * PATCHES : (b + 1) * PATCHES], axis=1, keepdims=True)
            listed = jnp.where(lane == 2 * c + b, value, listed)
    listed = jnp.concatenate([listed, jnp.zeros((256 - NARROW, 128), wide)], axis=0).T
    gate_grad = gate_back[0]
    for e in range(1, N_BLK):
        gate_grad = gate_grad + gate_back[e]
    grads[...] = jnp.concatenate([listed[:4], gate_grad, jnp.zeros((2, 256), wide)], axis=0)
    for j in range(1, N_BLK):
        send(grads, grads_all.at[j], end_send.at[j], end_recv.at[j], straight[j], sent)
    grads_all[0] = grads[...]
    first, second = sums[0:1, :], sums[1:2, :]
    for i in range(1, N_HID):
        arrived(sums_all.at[i], end_send.at[N_BLK + i], end_recv.at[N_BLK + i], at.across)
        first = first + sums_all[i, 0:1, :]
        second = second + sums_all[i, 1:2, :]
    norm_grads[...] = norm_grad
    totals[...] = jnp.concatenate([first, second], axis=0)
    for j in range(1, N_BLK):
        arrived(grads_all.at[j], end_send.at[j], end_recv.at[j], at.across)
    for copy in results:
        copy.wait()
    for copy in sent:
        copy.wait_send()


def result_kernel(
    cotangent, norm_grads, normed, stats, totals, grads_all, table, up_in, down_in,
    token_grads, up_grads, down_grads, weight_grads, bias_grads, held, move_sem,
):
    f32 = jnp.float32
    share = up_in.shape[0] // 4
    loads, stores = [], []
    for i, (src, dst) in enumerate(((up_in, up_grads), (down_in, down_grads))):
        for k in range(4):
            rows = pl.ds(k * share, share)
            loads.append(pltpu.make_async_copy(src.at[rows], held.at[i, rows], move_sem.at[0, i, k]))
            stores.append(pltpu.make_async_copy(held.at[i, rows], dst.at[rows], move_sem.at[1, i, k]))
    for load in loads:
        load.start()
    token_grads[...] = (
        cotangent[...].astype(f32)
        + stats[1:2, :] * (norm_grads[...] - totals[0:1, :] / WIDTH - normed[...] * (totals[1:2, :] / WIDTH))
    ).astype(token_grads.dtype)
    for load, store in zip(loads, stores):
        load.wait()
        store.start()
    image_grads = grads_all[...].reshape(8 * N_BLK, 256)
    conditions = table[...].reshape(8 * N_BLK, 256)[:, 128:]
    kind = lax.broadcasted_iota(jnp.int32, (8 * N_BLK, 128), 0) % 8 // 2
    kind_wide = lax.broadcasted_iota(jnp.int32, (8 * N_BLK, 256), 0) % 8 // 2
    for c in range(3):
        value = dot(jnp.where(kind == c, conditions, 0.0), image_grads, (0, 0), lax.Precision.HIGHEST)
        weight_grads[c] = value[32 : 32 + WIDTH // N_BLK, :NARROW]
        bias_grads[c : c + 1, :] = jnp.sum(jnp.where(kind_wide == c, image_grads, 0.0), axis=0, keepdims=True)[
            :, :NARROW
        ]
    for store in stores:
        store.wait()


def results_of(*operands):
    vmem, anywhere = pl.BlockSpec(memory_space=pltpu.VMEM), pl.BlockSpec(memory_space=pl.ANY)
    f32 = jnp.float32
    hidden, width = operands[-1].shape
    return pl.pallas_call(
        result_kernel,
        out_shape=(
            jax.ShapeDtypeStruct((NARROW, TOKENS), jnp.bfloat16),
            jax.ShapeDtypeStruct((hidden, width), f32),
            jax.ShapeDtypeStruct((hidden, width), f32),
            jax.ShapeDtypeStruct((3, width // N_BLK, NARROW), f32),
            jax.ShapeDtypeStruct((3, NARROW), f32),
        ),
        in_specs=[vmem] * 7 + [anywhere] * 2,
        out_specs=[vmem, anywhere, anywhere, vmem, vmem],
        scratch_shapes=[pltpu.VMEM((2, hidden, width), f32), pltpu.SemaphoreType.DMA((2, 2, 4))],
        compiler_params=pltpu.CompilerParams(vmem_limit_bytes=60 * 2**20),
    )(*operands)


def run_experts(*operands):
    vmem = pl.BlockSpec(memory_space=pltpu.VMEM)
    bf16, f32 = jnp.bfloat16, jnp.float32
    hidden, width = operands[-1].shape
    dma = pltpu.SemaphoreType.DMA
    return pl.pallas_call(
        expert_kernel,
        out_shape=(
            jax.ShapeDtypeStruct((NARROW, TOKENS), f32),
            jax.ShapeDtypeStruct((NARROW, TOKENS), f32),
            jax.ShapeDtypeStruct((8, TOKENS), f32),
            jax.ShapeDtypeStruct((2, TOKENS), f32),
            jax.ShapeDtypeStruct((N_BLK, 8, 256), f32),
            jax.ShapeDtypeStruct((N_BLK, 8, 256), f32),
            jax.ShapeDtypeStruct((hidden, width), f32),
            jax.ShapeDtypeStruct((hidden, width), f32),
        ),
        in_specs=[vmem] * len(operands),
        out_specs=[vmem] * 6 + [pl.BlockSpec(memory_space=pl.ANY)] * 2,
        scratch_shapes=[
            pltpu.VMEM((SLOTS, TOKENS), bf16),
            pltpu.VMEM((2 * NARROW, 2 * TOKENS), bf16),
            pltpu.VMEM((5 * NARROW, 2 * TOKENS), bf16),
            pltpu.VMEM((4 * NARROW, TOKENS), f32),
            pltpu.VMEM((4, NARROW, 128), f32),
            pltpu.VMEM((8, 2 * TOKENS), jnp.int32),
            pltpu.VMEM((2 * NARROW, LANES), bf16),
            pltpu.VMEM((5 * NARROW, SLOTS - LANES), bf16),
            pltpu.VMEM((NARROW, SLOTS), bf16),
            pltpu.VMEM((N_BLK, 2, 256), f32),
            pltpu.VMEM((2, TOKENS), f32),
            pltpu.VMEM((N_HID, 2, TOKENS), f32),
            pltpu.VMEM((8, 256), f32),
            pltpu.VMEM((hidden, width), f32),
            pltpu.VMEM((hidden, width), f32),
            pltpu.VMEM((width, SLOTS), bf16),
            pltpu.VMEM((width, SLOTS), bf16),
            pltpu.VMEM((width, SLOTS), bf16),
            pltpu.VMEM((hidden, LANES), bf16),
            pltpu.VMEM((hidden, LANES), bf16),
            pltpu.VMEM((width, SLOTS), bf16),
            pltpu.VMEM((width, hidden), bf16),
            pltpu.VMEM((width, hidden), bf16),
            pltpu.VMEM((width, 128), bf16),
            pltpu.VMEM((8 * N_BLK, 128), f32),
            pltpu.VMEM((N_HID, 2 * N_BLK, 256), f32),
            pltpu.VMEM((GROUPS, 2, NARROW, LANES), bf16),
            pltpu.VMEM((GROUPS, 4, NARROW, LANES), bf16),
            pltpu.VMEM((GROUPS, 4, NARROW, LANES), bf16),
            pltpu.VMEM((GROUPS, 4, NARROW, HALF), bf16),
            pltpu.VMEM((GROUPS, 8, NARROW, HALF // 2), bf16),
            pltpu.VMEM((GROUPS, 4, NARROW, HALF), bf16),
            pltpu.VMEM((GROUPS, NARROW, LANES), bf16),
            pltpu.VMEM((N_HID, 2 * N_BLK, 256), f32),
            pltpu.VMEM((2 * N_BLK, 256), f32),
            pltpu.VMEM((N_BLK, 2, 256), f32),
            dma((N_BLK, 4)),
            dma((N_BLK, 4)),
            dma((GROUPS, 14)),
            dma((GROUPS, 14)),
            dma((N_HID,)),
            dma((N_HID,)),
            dma((GROUPS, 18)),
            dma((GROUPS, 18)),
            dma((N_BLK, 2)),
            dma((N_BLK, 2)),
            dma((N_HID,)),
            dma((N_HID,)),
            dma((N_BLK + N_HID,)),
            dma((N_BLK + N_HID,)),
            dma((3,)),
            dma((3,)),
            dma((7,)),
        ],
        compiler_params=pltpu.CompilerParams(
            collective_id=0, has_side_effects=True, vmem_limit_bytes=60 * 2**20
        ),
    )(*operands)


def on_device(
    tokens,
    cotangent,
    route_weight,
    expert_ids,
    timesteps,
    time_table,
    up_weight,
    down_weight,
    modulation_weight,
    modulation_bias,
):
    ids = expert_ids.T
    by_feature = modulation_weight.transpose(1, 2, 0).reshape(3 * NARROW, WIDTH)
    columns, info = modulation(timesteps, time_table, by_feature, modulation_bias, ids)
    turned = cotangent.T
    partial_results = run_experts(
        tokens, turned, route_weight.T, ids, columns, info, up_weight[0].T, down_weight[0]
    )
    token_grads, up_grads, down_grads, weight_grads, bias_grads = results_of(turned, *partial_results)
    return (token_grads.T, up_grads.T[None], down_grads[None], weight_grads.transpose(1, 0, 2), bias_grads)


def solution(mesh):
    in_specs = (
        P("blk", None),
        P("blk", "hid"),
        P("blk", None),
        P("blk", None),
        P("blk"),
        P(),
        P("blk", None, "hid"),
        P("blk", "hid", None),
        P(None, None, "hid"),
        P(None, "hid"),
    )
    out_specs = (
        P("blk", "hid"),
        P("blk", None, "hid"),
        P("blk", "hid", None),
        P("blk", None, "hid"),
        P(None, "hid"),
    )
    return jax.shard_map(
        on_device, mesh=mesh, in_specs=in_specs, out_specs=out_specs, check_vma=False
    )
```

```python
import math

import jax
import jax.numpy as jnp
from jax import lax
from jax.experimental import pallas as pl
from jax.experimental.pallas import tpu as pltpu
from jax.sharding import PartitionSpec as P

MESH = pl.DeviceIdType.MESH
norm_epsilon = 1e-06
gelu_cubic = 0.044715
gelu_factor = math.sqrt(2.0 / math.pi)

N_BLK, N_HID = 16, 8
WIDTH, NARROW, CAP = 1152, 144, 128
TOKENS, PATCHES = 512, 256
SLOTS = N_BLK * CAP
GROUPS = 4
LANES = SLOTS // GROUPS
HALF = LANES // 2
ORDER = (0, 1, 6, 2, 7, 3, 5, 4)


def shift(j):
    return j // 8, ORDER[j % 8]


class Place:
    def __init__(self):
        self.blk = lax.axis_index("blk")
        self.hid = lax.axis_index("hid")
        self.z_hi, self.m = self.blk // 8, self.blk % 8
        self.x, self.z_lo = self.hid // 2, self.hid % 2
        self.x_right, self.x_left, self.x_far = [(self.x + i) % 4 for i in (1, 3, 2)]
        self.right = (self.blk, self.x_right * 2 + self.z_lo)
        self.left = (self.blk, self.x_left * 2 + self.z_lo)
        self.across = (self.blk, self.home(1))

    def home(self, a):
        return self.hid if a == 0 else self.hid + 1 - 2 * self.z_lo

    def later(self, j):
        a, m = shift(j)
        return (self.z_hi + a) % 2 * 8 + (self.m + m) % 8

    def earlier(self, j):
        a, m = shift(j)
        return (self.z_hi + a) % 2 * 8 + (self.m + 8 - m) % 8

    def hid_peer(self, i):
        return (self.blk, (self.hid + i) % 8)


def greet(devices):
    barrier = pltpu.get_barrier_semaphore()
    for device in devices:
        pl.semaphore_signal(barrier, inc=1, device_id=device, device_id_type=MESH)
    pl.semaphore_wait(barrier, len(devices))


def send(src, dst, send_sem, recv_sem, device, sent):
    copy = pltpu.make_async_remote_copy(
        src_ref=src, dst_ref=dst, send_sem=send_sem, recv_sem=recv_sem, device_id=device, device_id_type=MESH
    )
    copy.start()
    sent.append(copy)


def arrived(region, send_sem, recv_sem, device):
    pltpu.make_async_remote_copy(
        src_ref=region, dst_ref=region, send_sem=send_sem, recv_sem=recv_sem, device_id=device, device_id_type=MESH
    ).wait_recv()


def rows_of(slice_index, count=1):
    return pl.ds(pl.multiple_of(slice_index * NARROW, 16), count * NARROW)


def block_of(index):
    return pl.ds(pl.multiple_of(index * CAP, CAP), CAP)


def gelu_both(values):
    square = values * values
    inner = gelu_factor * (values + gelu_cubic * values * square)
    tangent = jnp.tanh(inner)
    slope = 0.5 * (1.0 + tangent) + 0.5 * values * (1.0 - tangent * tangent) * gelu_factor * (
        1.0 + 3.0 * gelu_cubic * square
    )
    return 0.5 * values * (1.0 + tangent), slope


def dot(a, b, contract=(1, 0), precision=None):
    return lax.dot_general(
        a, b, (((contract[0],), (contract[1],)), ((), ())), precision=precision, preferred_element_type=jnp.float32
    )


def modulation_kernel(steps, table, weight, bias, ids, columns, info, rows, lookup_sem):
    f32 = jnp.float32
    copies = [
        pltpu.make_async_copy(table.at[pl.ds(steps[b], 1)], rows.at[pl.ds(b, 1)], lookup_sem.at[b]) for b in range(2)
    ]
    for copy in copies:
        copy.start()
    bias_columns = jnp.concatenate([bias[...], jnp.zeros((3, 256 - NARROW), f32)], axis=1)
    bias_columns = jnp.concatenate([bias_columns, jnp.zeros((125, 256), f32)], axis=0).T
    expert = lax.broadcasted_iota(jnp.int32, (N_BLK, 256), 0)
    named = ((expert == ids[0:1, :256]) | (expert == ids[1:2, :256])).astype(jnp.bfloat16)
    counts = dot(jnp.ones((8, 256), jnp.bfloat16), named, (1, 1))
    for copy in copies:
        copy.wait()
    looked = rows[pl.ds(0, 2)]
    condition = looked / (1.0 + jnp.exp(-looked))
    lane = lax.broadcasted_iota(jnp.int32, (NARROW, 128), 1)
    for c in range(3):
        part = weight[c * NARROW : (c + 1) * NARROW]
        sums = [
            jnp.sum(part * condition[b : b + 1], axis=1, keepdims=True) + bias_columns[:NARROW, c : c + 1]
            for b in range(2)
        ]
        value = jnp.where(lane % 2 == 0, sums[0], sums[1])
        listed = value if c == 0 else jnp.where(lane // 2 == c, value, listed)
    columns[...] = listed
    gate = value
    gate = jnp.concatenate([gate, jnp.zeros((256 - NARROW, 128), f32)], axis=0).T[:8]
    high = gate.astype(jnp.bfloat16).astype(f32)
    middle = (gate - high).astype(jnp.bfloat16).astype(f32)
    low = (gate - high) - middle
    parts = jnp.concatenate([high[:2], middle[:2], low[:2], jnp.zeros((2, 256), f32)], axis=0)[:, :NARROW]
    repeated = jnp.concatenate([condition] * 4, axis=0)
    share = WIDTH // N_BLK
    for e in range(N_BLK):
        info[e] = jnp.concatenate(
            [parts, counts, repeated[:, e * share : (e + 1) * share], jnp.zeros((8, 96 - share), f32)], axis=1
        )


def modulation(timesteps, time_table, weight, bias, ids):
    vmem = pl.BlockSpec(memory_space=pltpu.VMEM)
    f32 = jnp.float32
    return pl.pallas_call(
        modulation_kernel,
        out_shape=(
            jax.ShapeDtypeStruct((NARROW, 128), f32),
            jax.ShapeDtypeStruct((N_BLK, 8, 256), f32),
        ),
        in_specs=[pl.BlockSpec(memory_space=pltpu.SMEM), pl.BlockSpec(memory_space=pl.ANY), vmem, vmem, vmem],
        out_specs=[vmem] * 2,
        scratch_shapes=[pltpu.VMEM((8, WIDTH), f32), pltpu.SemaphoreType.DMA((2,))],
        compiler_params=pltpu.CompilerParams(vmem_limit_bytes=60 * 2**20),
    )(timesteps, time_table, weight, bias, ids)


def expert_kernel(
    tokens, cotangent, route, ids, columns, info, up_t, down,
    norm_grads, normed, stats, totals, grads_all, table, up_out, down_out,
    chosen, both, four, four_normed, four_columns, targets, payload, four_payload, back, gate_back, sums, sums_all, grads, up_grads, down_grads,
    xt, ct, hcot, act, pre_grad, part, up, down_t, gate_lanes, counts, gate_part,
    first_a, second_a, third_a, first_b, second_b, mine_b, total, gate_in, gate_sum, gate_out,
    a2a_send, a2a_recv, ring_send, ring_recv, info_send, info_recv,
    sum_send, sum_recv, back_send, back_recv, gate_send, gate_recv, end_send, end_recv, near_send, near_recv, local_sem,
):
    at = Place()
    wide = jnp.float32
    bf16 = jnp.bfloat16
    peers = [(at.later(j), at.home(j // 8)) for j in range(N_BLK)]
    straight = [(at.later(j), at.hid) for j in range(N_BLK)]
    owners = [(at.earlier(j), at.home(j // 8)) for j in range(N_BLK)]
    straight_owners = [(at.earlier(j), at.hid) for j in range(N_BLK)]
    hid_peers = [at.hid_peer(i) for i in range(N_HID)]
    everyone = peers[1:] + straight[8:] + hid_peers[1:]
    barrier = pltpu.get_barrier_semaphore()
    for device in everyone:
        pl.semaphore_signal(barrier, inc=1, device_id=device, device_id_type=MESH)
    own = rows_of(at.hid)
    sent = []

    def put(ref, value):
        ref[...] = value.astype(ref.dtype)

    @pl.loop(0, TOKENS // 128)
    def _(i):
        rows = pl.ds(pl.multiple_of(i * 128, 128), 128)
        values = tokens[rows, :].astype(wide)
        mean = jnp.sum(values, axis=1, keepdims=True) / WIDTH
        spread_of = jnp.sum((values - mean) ** 2, axis=1, keepdims=True) / WIDTH
        inverse = 1.0 / jnp.sqrt(spread_of + norm_epsilon)
        lane = lax.broadcasted_iota(jnp.int32, (128, 128), 1)
        stats[:, rows] = jnp.where(lane == 0, mean, inverse).T[:8]

    row = lax.broadcasted_iota(jnp.int32, (NARROW, WIDTH), 0)
    column = lax.broadcasted_iota(jnp.int32, (NARROW, WIDTH), 1)
    pick = (column == row + at.hid * NARROW).astype(wide).astype(bf16)
    normed[...] = (dot(pick, tokens[...], (1, 1)) - stats[0:1, :]) * stats[1:2, :]
    for b in range(2):
        half = slice(b * PATCHES, (b + 1) * PATCHES)
        hin = normed[:, half] * (1.0 + columns[:, 2 + b : 3 + b]) + columns[:, b : b + 1]
        for k in range(2):
            both[:NARROW, k * TOKENS + b * PATCHES : k * TOKENS + (b + 1) * PATCHES] = hin.astype(bf16)
    for k in range(2):
        weighted = cotangent[...].astype(wide) * route[k : k + 1, :]
        both[NARROW:, k * TOKENS : (k + 1) * TOKENS] = weighted.astype(bf16)

    expert = lax.broadcasted_iota(jnp.int32, (N_BLK, TOKENS), 0)
    named = [(expert == ids[k : k + 1, :]) for k in range(2)]
    earlier_row = lax.broadcasted_iota(jnp.int32, (TOKENS, TOKENS), 0)
    earlier_lane = lax.broadcasted_iota(jnp.int32, (TOKENS, TOKENS), 1)
    before = dot(
        (named[0] | named[1]).astype(wide).astype(bf16), (earlier_row < earlier_lane).astype(wide).astype(bf16)
    )
    for k in range(2):
        slot = jnp.sum(jnp.where(named[k], before, 0.0), axis=0, keepdims=True)
        targets[0:1, k * TOKENS : (k + 1) * TOKENS] = ids[k : k + 1, :] * CAP + slot.astype(jnp.int32)

    gate_part[...] = jnp.zeros_like(gate_part)
    row = lax.broadcasted_iota(jnp.int32, (4 * NARROW, WIDTH), 0)
    column = lax.broadcasted_iota(jnp.int32, (4 * NARROW, WIDTH), 1)
    wanted = row + jnp.where(row < 2 * NARROW, at.x * 2 * NARROW, (at.x_far - 1) * 2 * NARROW)
    pick = (column == wanted).astype(wide).astype(bf16)
    four_normed[...] = (dot(pick, tokens[...], (1, 1)) - stats[0:1, :]) * stats[1:2, :]
    four_columns[at.z_lo] = columns[...]
    pl.semaphore_wait(barrier, len(everyone))

    near = (at.across, (at.blk, at.x_far * 2 + at.z_lo), (at.blk, at.x_far * 2 + 1 - at.z_lo))
    near_place = (at.z_lo, 2 + at.z_lo, 2 + at.z_lo)
    near_from = (1 - at.z_lo, 2 + at.z_lo, 3 - at.z_lo)
    for i in range(3):
        send(columns, four_columns.at[near_place[i]], near_send.at[i], near_recv.at[i], near[i], sent)

    for j in range(N_BLK):
        target = at.later(j)
        if j == 0:
            info_local = pltpu.make_async_copy(info.at[target], table.at[0], local_sem.at[2])
            info_local.start()
        else:
            send(info.at[target], table.at[j], a2a_send.at[j, 2], a2a_recv.at[j, 2], straight[j], sent)

    def payload_parts(j):
        lanes = pl.ds(j * CAP, CAP)
        return (
            (payload.at[pl.ds(0, NARROW), lanes], xt.at[own, lanes]),
            (payload.at[pl.ds(NARROW, NARROW), lanes], ct.at[own, lanes]),
        )

    def hits_of(pair):
        hits = []
        for j in (2 * pair, 2 * pair + 1):
            slots = lax.broadcasted_iota(jnp.int32, (CAP, 2 * TOKENS), 0) + at.later(j) * CAP
            hit = (slots == targets[0:1, :]).astype(wide)
            chosen[block_of(at.later(j)), :] = (hit[:, :TOKENS] + hit[:, TOKENS:]).astype(bf16)
            hits.append(hit.astype(bf16))
        return jnp.concatenate(hits, axis=0)

    def make_payload(pair):
        value = dot(both[...], hits_of(pair), (1, 1))
        payload[:, 2 * pair * CAP : (2 * pair + 2) * CAP] = value.astype(bf16)
        for j in (2 * pair, 2 * pair + 1):
            for i, (src, dst) in enumerate(payload_parts(j)):
                if j == 0:
                    pltpu.make_async_copy(src, dst, local_sem.at[i]).start()
                else:
                    send(src, dst, a2a_send.at[j, i], a2a_recv.at[j, i], peers[j], sent)

    def make_four():
        for i in range(3):
            arrived(four_columns.at[near_from[i]], near_send.at[i], near_recv.at[i], near[i])
        for q in range(4):
            rows = slice(q * NARROW, (q + 1) * NARROW)
            for b in range(2):
                half = slice(b * PATCHES, (b + 1) * PATCHES)
                hin = four_normed[rows, half] * (1.0 + four_columns[q, :, 2 + b : 3 + b])
                hin = (hin + four_columns[q, :, b : b + 1]).astype(bf16)
                for k in range(2):
                    four[rows, k * TOKENS + b * PATCHES : k * TOKENS + (b + 1) * PATCHES] = hin

        four[4 * NARROW :, :] = both[NARROW:, :]

    four_rows = (pl.ds(0, 2 * NARROW), pl.ds(2 * NARROW, 2 * NARROW), pl.ds(4 * NARROW, NARROW))

    def four_parts(j):
        lanes = pl.ds(j * CAP, CAP)
        targets_of = (xt.at[rows_of(at.x * 2, 2), lanes], xt.at[rows_of(at.x_far * 2, 2), lanes], ct.at[own, lanes])
        return [
            (four_payload.at[rows, pl.ds(j * CAP - LANES, CAP)], dst) for rows, dst in zip(four_rows, targets_of)
        ]

    def make_four_payload(g):
        for pair in range(g * LANES // CAP // 2, (g + 1) * LANES // CAP // 2):
            hits = hits_of(pair)
            start = 2 * pair * CAP - LANES
            for rows in four_rows:
                four_payload[rows, start : start + 2 * CAP] = dot(four[rows, :], hits, (1, 1)).astype(bf16)
            for j in (2 * pair, 2 * pair + 1):
                for k, (src, dst) in zip((0, 3, 1), four_parts(j)):
                    send(src, dst, a2a_send.at[j, k], a2a_recv.at[j, k], peers[j], sent)

    def from_peer(j, i, region):
        if j == 0:
            pltpu.make_async_copy(*payload_parts(0)[i], local_sem.at[i]).wait()
        else:
            arrived(region, a2a_send.at[j, i], a2a_recv.at[j, i], peers[j])

    def spread(g):
        a = g // (GROUPS // 2)
        f = at.home(a)
        other = at.home(1 - a)
        zf = f % 2
        lanes = pl.ds(g * LANES, LANES)
        halves = [pl.ds(g * LANES + i * HALF, HALF) for i in range(2)]
        far_slice = at.x_far * 2 + zf

        def go(array, rows, cols, k, device):
            region = array.at[rows, cols]
            send(region, region, ring_send.at[g, k], ring_recv.at[g, k], device, sent)

        def come(array, rows, cols, k):
            arrived(array.at[rows, cols], ring_send.at[g, k], ring_recv.at[g, k], at.across)

        def first():
            for j in range(g * LANES // CAP, (g + 1) * LANES // CAP):
                block = pl.ds(j * CAP, CAP)
                from_peer(j, 1, ct.at[rows_of(f), block])
                if g == 0:
                    from_peer(j, 0, xt.at[rows_of(f), block])
                else:
                    from_peer(j, 0, xt.at[rows_of(at.x * 2, 2), block])
                    from_peer(j, 3, xt.at[rows_of(at.x_far * 2, 2), block])
            if g == 0:
                go(xt, rows_of(f), lanes, 0, at.across)
            go(ct, rows_of(f), lanes, 6, at.right)
            go(ct, rows_of(f), lanes, 7, at.left)
            go(ct, rows_of(f), lanes, 5, at.across)
            if g > 0:
                go(xt, rows_of(at.x * 2, 2), lanes, 1, at.right)
                go(xt, rows_of(at.x * 2, 2), lanes, 2, at.left)

        def second():
            if g == 0:
                come(xt, rows_of(other), lanes, 0)
                go(xt, rows_of(at.x * 2, 2), lanes, 1, at.right)
                go(xt, rows_of(at.x * 2, 2), lanes, 2, at.left)
            left, right = rows_of(at.x_left * 2 + zf), rows_of(at.x_right * 2 + zf)
            come(ct, left, lanes, 6)
            go(ct, left, halves[0], 8, at.right)
            go(ct, left, lanes, 10, at.across)
            come(ct, right, lanes, 7)
            go(ct, right, halves[1], 9, at.left)
            go(ct, right, lanes, 11, at.across)

        def third():
            if g == 0:
                come(xt, rows_of(at.x_left * 2, 2), lanes, 1)
                go(xt, rows_of(at.x_left * 2), lanes, 3, at.right)
                come(xt, rows_of(at.x_right * 2, 2), lanes, 2)
                go(xt, rows_of(at.x_right * 2 + 1), lanes, 4, at.left)
            for i in range(2):
                come(ct, rows_of(far_slice), halves[i], 8 + i)
                go(ct, rows_of(far_slice), halves[i], 12 + i, at.across)

        def fourth():
            if g == 0:
                come(xt, rows_of(at.x_far * 2), lanes, 3)
                come(xt, rows_of(at.x_far * 2 + 1), lanes, 4)
            else:
                come(xt, rows_of(at.x_left * 2, 2), lanes, 1)
                come(xt, rows_of(at.x_right * 2, 2), lanes, 2)
            come(ct, rows_of(other), lanes, 5)
            come(ct, rows_of(at.x_left * 2 + 1 - zf), lanes, 10)
            come(ct, rows_of(at.x_right * 2 + 1 - zf), lanes, 11)
            for i in range(2):
                come(ct, rows_of(at.x_far * 2 + 1 - zf), halves[i], 12 + i)

        return first, second, third, fourth

    def spread_info():
        info_local.wait()
        for j in range(1, N_BLK):
            arrived(table.at[j], a2a_send.at[j, 2], a2a_recv.at[j, 2], straight[j])
        rows = table[...].reshape(8 * N_BLK, 256)
        gate_lanes[own, :] = rows.T[:NARROW].astype(bf16)
        region = gate_lanes.at[own]
        for i in range(1, N_HID):
            send(region, region, info_send.at[i], info_recv.at[i], hid_peers[i], sent)
        lane = lax.broadcasted_iota(jnp.int32, (8 * N_BLK, 128), 1)
        mine = jnp.sum(jnp.where(lane == at.blk + 16, rows[:, 128:], 0.0), axis=1, keepdims=True)
        counts[...] = jnp.broadcast_to(mine, counts.shape)

    def gather_info():
        for i in range(1, N_HID):
            region = gate_lanes.at[rows_of((at.hid + 8 - i) % 8)]
            arrived(region, info_send.at[i], info_recv.at[i], at.across)

    def image_of_lane(g):
        shape = (8 * N_BLK, LANES)
        row = lax.broadcasted_iota(jnp.int32, shape, 0)
        lane = lax.broadcasted_iota(jnp.int32, shape, 1)
        block = lane // CAP + g * (LANES // CAP)
        first_count = jnp.concatenate([counts[...]] * (LANES // 128), axis=1)
        is_first = (lane % CAP).astype(wide) < first_count
        hit = (row // 8 == block) & (is_first == (row % 2 == 0)) & (row % 8 < 6)
        return jnp.where(hit, 1.0, 0.0).astype(bf16)

    def forward(g, pair_ready):
        lanes = pl.ds(g * LANES, LANES)
        images = image_of_lane(g)

        @pl.loop(0, 4)
        def _(i):
            rows = rows_of(2 * i, 2)
            gates = dot(gate_lanes[rows, :], images)
            hcot[rows, lanes] = (gates * ct[rows, lanes].astype(wide)).astype(bf16)

        @pl.loop(0, 3)
        def _(i):
            rows = pl.ds(pl.multiple_of(i * 192, 64), 192)
            activated, slope = gelu_both(dot(up_t[rows, :], xt[:, lanes]))
            act[rows, :] = activated.astype(bf16)
            pre_grad[rows, :] = (dot(down[rows, :], hcot[:, lanes]) * slope).astype(bf16)

        for i in range(4):
            rows = rows_of(2 * i, 2)
            part[rows, lanes] = dot(up[rows, :], pre_grad[...]).astype(bf16)
            pair_ready(i)

    def gates_of(g):
        lanes = pl.ds(g * LANES, LANES)
        spots = 2 * N_BLK
        narrow_row = lax.broadcasted_iota(jnp.int32, (spots, 8 * N_BLK), 0)
        wide_row = lax.broadcasted_iota(jnp.int32, (spots, 8 * N_BLK), 1)
        compact = (wide_row == narrow_row // 2 * 8 + narrow_row % 2).astype(wide).astype(bf16)
        images = dot(compact, image_of_lane(g)).astype(bf16)

        @pl.loop(0, 4)
        def _(i):
            rows = rows_of(2 * i, 2)
            product = (dot(down_t[rows, :], act[...]) * ct[rows, lanes].astype(wide)).astype(bf16)
            for k in range(2):
                value = dot(images, product[k * NARROW : (k + 1) * NARROW], (1, 1))
                gate_part[2 * i + k, :, pl.ds(0, NARROW)] += value

    def weights(grads_of, left, right, g):
        lanes = pl.ds(g * LANES, LANES)

        @pl.loop(0, 3)
        def _(i):
            rows = pl.ds(pl.multiple_of(i * 192, 64), 192)
            value = dot(left[rows, :], right[:, lanes], (1, 1))
            if g == 0:
                grads_of[rows, :] = value
            else:
                grads_of[rows, :] += value

    def reduce(g, along_x):
        a = g // (GROUPS // 2)
        zf = at.home(a) % 2
        lanes_a = pl.ds(g * LANES, along_x)
        along_z = LANES - along_x
        lanes_b = pl.ds(g * LANES + along_x, along_z)
        low, high = pl.ds(0, along_z // 2), pl.ds(along_z // 2, along_z // 2)

        def mine(x, z, lanes):
            return part.at[rows_of(x * 2 + z), lanes]

        def go(src, dst, k, device):
            send(src, dst, sum_send.at[g, k], sum_recv.at[g, k], device, sent)

        def come(region, k):
            arrived(region, sum_send.at[g, k], sum_recv.at[g, k], at.across)

        def view(buffer, i):
            return buffer.at[g, i, :, pl.ds(0, along_x)]

        def from_z(x):
            return first_b.at[g, x, :, pl.ds(0, along_z)]

        def from_x(i):
            return second_b.at[g, i, :, low]

        def pair_ready(x):
            if along_z:
                go(mine(x, 1 - zf, lanes_b), from_z(x), 8 + x, at.across)

        def first():
            if along_x:
                go(mine(at.x_far, 0, lanes_a), view(first_a, 0), 0, at.right)
                go(mine(at.x_far, 1, lanes_a), view(first_a, 1), 1, at.left)
                go(mine(at.x_right, 1, lanes_a), view(second_a, 1), 2, at.right)
                go(mine(at.x_left, 0, lanes_a), view(second_a, 2), 3, at.left)

        def second():
            if along_x:
                come(view(first_a, 0), 0)
                put(view(third_a, 0), view(first_a, 0)[...].astype(wide) + mine(at.x_right, 0, lanes_a)[...].astype(wide))
                go(view(third_a, 0), view(second_a, 0), 4, at.right)
                come(view(first_a, 1), 1)
                put(view(third_a, 1), view(first_a, 1)[...].astype(wide) + mine(at.x_left, 1, lanes_a)[...].astype(wide))
                go(view(third_a, 1), view(second_a, 3), 5, at.left)
            if not along_z:
                return
            for x in range(4):
                come(from_z(x), 8 + x)
            for i, x in enumerate((at.x_far, at.x_right, at.x_left, at.x)):
                put(
                    mine_b.at[g, i, :, pl.ds(0, along_z)],
                    from_z(x)[...].astype(wide) + mine(x, zf, lanes_b)[...].astype(wide),
                )
                if i == 0:
                    go(mine_b.at[g, 0, :, low], from_x(0), 12, at.right)
                    go(mine_b.at[g, 0, :, high], from_x(1), 13, at.left)
                if i == 1:
                    go(mine_b.at[g, 1, :, high], from_x(2), 14, at.right)
                if i == 2:
                    go(mine_b.at[g, 2, :, low], from_x(3), 15, at.left)

        def third():
            if along_x:
                for i, k in enumerate((4, 2, 3, 5)):
                    come(view(second_a, i), k)
                sums_of = [
                    view(second_a, z)[...].astype(wide)
                    + view(second_a, 2 + z)[...].astype(wide)
                    + mine(at.x, z, lanes_a)[...].astype(wide)
                    for z in range(2)
                ]
                put(view(third_a, 2), jnp.where(zf == 0, sums_of[1], sums_of[0]))
                go(view(third_a, 2), view(third_a, 3), 6, at.across)
                put(total.at[g, :, pl.ds(0, along_x)], jnp.where(zf == 0, sums_of[0], sums_of[1]))
            if not along_z:
                return
            come(from_x(0), 12)
            put(from_x(4), from_x(0)[...].astype(wide) + mine_b[g, 1, :, low].astype(wide))
            go(from_x(4), from_x(6), 16, at.right)
            come(from_x(1), 13)
            put(from_x(5), from_x(1)[...].astype(wide) + mine_b[g, 2, :, high].astype(wide))
            go(from_x(5), from_x(7), 17, at.left)

        def fourth():
            if along_x:
                come(view(third_a, 3), 6)
                region = total.at[g, :, pl.ds(0, along_x)]
                put(region, region[...].astype(wide) + view(third_a, 3)[...].astype(wide))
            for i, k in ((6, 16), (2, 14), (3, 15), (7, 17)):
                if along_z:
                    come(from_x(i), k)
            for i, (l, r, cols) in enumerate(((6, 3, low), (2, 7, high)) if along_z else ()):
                put(
                    total.at[g, :, pl.ds(along_x + i * (along_z // 2), along_z // 2)],
                    from_x(l)[...].astype(wide) + from_x(r)[...].astype(wide) + mine_b[g, 3, :, cols].astype(wide),
                )
            for i in range(LANES // CAP):
                j = g * (LANES // CAP) + i
                src = total.at[g, :, pl.ds(i * CAP, CAP)]
                dst = back.at[:, block_of(at.blk)]
                if j == 0:
                    pltpu.make_async_copy(src, dst, local_sem.at[3]).start()
                else:
                    send(src, dst, back_send.at[j, 0], back_recv.at[j, 0], owners[j], sent)

        return first, second, third, fourth, pair_ready

    def gate_first():
        for i in range(1, N_HID):
            q = (at.hid + i) % 8
            send(gate_part.at[q], gate_in.at[i], gate_send.at[i], gate_recv.at[i], hid_peers[i], sent)

    def gate_second():
        value = gate_part[at.hid]
        for i in range(1, N_HID):
            arrived(gate_in.at[i], gate_send.at[i], gate_recv.at[i], at.across)
            value = value + gate_in[i]
        gate_sum[...] = value
        for j in range(N_BLK):
            gate_out[j] = gate_sum[pl.ds(2 * j, 2)]
            src, dst = gate_out.at[j], gate_back.at[at.blk]
            if j == 0:
                pltpu.make_async_copy(src, dst, local_sem.at[4]).start()
            else:
                send(src, dst, back_send.at[j, 1], back_recv.at[j, 1], straight_owners[j], sent)

    make_payload(0)
    make_payload(1)

    @pl.loop(0, 9)
    def _(i):
        tile = pl.ds(pl.multiple_of(i * 128, 128), 128)
        up[tile, :] = up_t[:, tile].T
        down_t[tile, :] = down[:, tile].T

    results = [
        pltpu.make_async_copy(up_grads, up_out, local_sem.at[5]),
        pltpu.make_async_copy(down_grads, down_out, local_sem.at[6]),
    ]
    spreads = [spread(g) for g in range(GROUPS)]
    reduces = [reduce(g, along_x) for g, along_x in enumerate((HALF, LANES, HALF, HALF))]
    def finish_group(g):
        gates_of(g)
        if g == GROUPS - 1:
            gate_first()
        weights(up_grads, pre_grad, xt, g)
        weights(down_grads, act, hcot, g)

    spreads[0][0]()
    spread_info()
    make_four()
    make_four_payload(1)
    make_four_payload(2)
    spreads[0][1]()
    spreads[1][0]()
    make_four_payload(3)
    spreads[0][2]()
    spreads[1][1]()
    spreads[2][0]()
    spreads[0][3]()
    gather_info()
    forward(0, reduces[0][4])
    reduces[0][0]()
    spreads[2][1]()
    spreads[1][2]()
    spreads[3][0]()
    finish_group(0)
    for g in range(1, GROUPS + 3):
        for k in (1, 2, 3):
            if g + 3 - k < GROUPS:
                spreads[g + 3 - k][k]()
        if g < GROUPS:
            forward(g, reduces[g][4])
            reduces[g][0]()
        for k in (1, 2, 3):
            if 0 <= g - k < GROUPS:
                reduces[g - k][k]()
        if g < GROUPS:
            finish_group(g)
        if g == GROUPS - 1:
            for copy in results:
                copy.start()
        if g == GROUPS + 1:
            gate_second()

    for j in range(N_BLK):
        e = at.later(j)
        if j == 0:
            pltpu.make_async_copy(total.at[0, :, pl.ds(0, CAP)], back.at[:, block_of(e)], local_sem.at[3]).wait()
            pltpu.make_async_copy(gate_out.at[0], gate_back.at[e], local_sem.at[4]).wait()
        else:
            arrived(back.at[:, block_of(e)], back_send.at[j, 0], back_recv.at[j, 0], at.across)
            arrived(gate_back.at[e], back_send.at[j, 1], back_recv.at[j, 1], at.across)

    mixed = dot(back[...], chosen[...])
    scale = jnp.concatenate(
        [jnp.broadcast_to(1.0 + columns[:, 2 + b : 3 + b], (NARROW, PATCHES)) for b in range(2)], axis=1
    )
    norm_grad = mixed * scale
    sums[0:1, :] = jnp.sum(norm_grad, axis=0, keepdims=True)
    sums[1:2, :] = jnp.sum(norm_grad * normed[...], axis=0, keepdims=True)
    for i in range(1, N_HID):
        send(sums, sums_all.at[i], end_send.at[N_BLK + i], end_recv.at[N_BLK + i], hid_peers[i], sent)
    lane = lax.broadcasted_iota(jnp.int32, (NARROW, 128), 1)
    listed = jnp.zeros((NARROW, 128), wide)
    for c, values in enumerate((mixed, mixed * normed[...])):
        for b in range(2):
            value = jnp.sum(values[:, b * PATCHES : (b + 1) * PATCHES], axis=1, keepdims=True)
            listed = jnp.where(lane == 2 * c + b, value, listed)
    listed = jnp.concatenate([listed, jnp.zeros((256 - NARROW, 128), wide)], axis=0).T
    gate_grad = gate_back[0]
    for e in range(1, N_BLK):
        gate_grad = gate_grad + gate_back[e]
    grads[...] = jnp.concatenate([listed[:4], gate_grad, jnp.zeros((2, 256), wide)], axis=0)
    for j in range(1, N_BLK):
        send(grads, grads_all.at[j], end_send.at[j], end_recv.at[j], straight[j], sent)
    grads_all[0] = grads[...]
    first, second = sums[0:1, :], sums[1:2, :]
    for i in range(1, N_HID):
        arrived(sums_all.at[i], end_send.at[N_BLK + i], end_recv.at[N_BLK + i], at.across)
        first = first + sums_all[i, 0:1, :]
        second = second + sums_all[i, 1:2, :]
    norm_grads[...] = norm_grad
    totals[...] = jnp.concatenate([first, second], axis=0)
    for j in range(1, N_BLK):
        arrived(grads_all.at[j], end_send.at[j], end_recv.at[j], at.across)
    for copy in results:
        copy.wait()
    for copy in sent:
        copy.wait_send()


def result_kernel(
    cotangent, norm_grads, normed, stats, totals, grads_all, table, up_in, down_in,
    token_grads, up_grads, down_grads, weight_grads, bias_grads, held, move_sem,
):
    f32 = jnp.float32
    share = up_in.shape[0] // 2
    loads, stores = [], []
    for i, (src, dst) in enumerate(((up_in, up_grads), (down_in, down_grads))):
        for k in range(2):
            rows = pl.ds(k * share, share)
            loads.append(pltpu.make_async_copy(src.at[rows], held.at[i, rows], move_sem.at[0, i, k]))
            stores.append(pltpu.make_async_copy(held.at[i, rows], dst.at[rows], move_sem.at[1, i, k]))
    for load in loads:
        load.start()
    token_grads[...] = (
        cotangent[...].astype(f32)
        + stats[1:2, :] * (norm_grads[...] - totals[0:1, :] / WIDTH - normed[...] * (totals[1:2, :] / WIDTH))
    ).astype(token_grads.dtype)
    for load, store in zip(loads, stores):
        load.wait()
        store.start()
    image_grads = grads_all[...].reshape(8 * N_BLK, 256)
    conditions = table[...].reshape(8 * N_BLK, 256)[:, 128:]
    kind = lax.broadcasted_iota(jnp.int32, (8 * N_BLK, 128), 0) % 8 // 2
    kind_wide = lax.broadcasted_iota(jnp.int32, (8 * N_BLK, 256), 0) % 8 // 2
    for c in range(3):
        value = dot(jnp.where(kind == c, conditions, 0.0), image_grads, (0, 0), lax.Precision.HIGHEST)
        weight_grads[c] = value[32 : 32 + WIDTH // N_BLK, :NARROW]
        bias_grads[c : c + 1, :] = jnp.sum(jnp.where(kind_wide == c, image_grads, 0.0), axis=0, keepdims=True)[
            :, :NARROW
        ]
    for store in stores:
        store.wait()


def results_of(*operands):
    vmem, anywhere = pl.BlockSpec(memory_space=pltpu.VMEM), pl.BlockSpec(memory_space=pl.ANY)
    f32 = jnp.float32
    hidden, width = operands[-1].shape
    return pl.pallas_call(
        result_kernel,
        out_shape=(
            jax.ShapeDtypeStruct((NARROW, TOKENS), jnp.bfloat16),
            jax.ShapeDtypeStruct((hidden, width), f32),
            jax.ShapeDtypeStruct((hidden, width), f32),
            jax.ShapeDtypeStruct((3, width // N_BLK, NARROW), f32),
            jax.ShapeDtypeStruct((3, NARROW), f32),
        ),
        in_specs=[vmem] * 7 + [anywhere] * 2,
        out_specs=[vmem, anywhere, anywhere, vmem, vmem],
        scratch_shapes=[pltpu.VMEM((2, hidden, width), f32), pltpu.SemaphoreType.DMA((2, 2, 2))],
        compiler_params=pltpu.CompilerParams(vmem_limit_bytes=60 * 2**20),
    )(*operands)


def run_experts(*operands):
    vmem = pl.BlockSpec(memory_space=pltpu.VMEM)
    bf16, f32 = jnp.bfloat16, jnp.float32
    hidden, width = operands[-1].shape
    dma = pltpu.SemaphoreType.DMA
    return pl.pallas_call(
        expert_kernel,
        out_shape=(
            jax.ShapeDtypeStruct((NARROW, TOKENS), f32),
            jax.ShapeDtypeStruct((NARROW, TOKENS), f32),
            jax.ShapeDtypeStruct((8, TOKENS), f32),
            jax.ShapeDtypeStruct((2, TOKENS), f32),
            jax.ShapeDtypeStruct((N_BLK, 8, 256), f32),
            jax.ShapeDtypeStruct((N_BLK, 8, 256), f32),
            jax.ShapeDtypeStruct((hidden, width), f32),
            jax.ShapeDtypeStruct((hidden, width), f32),
        ),
        in_specs=[vmem] * len(operands),
        out_specs=[vmem] * 6 + [pl.BlockSpec(memory_space=pl.ANY)] * 2,
        scratch_shapes=[
            pltpu.VMEM((SLOTS, TOKENS), bf16),
            pltpu.VMEM((2 * NARROW, 2 * TOKENS), bf16),
            pltpu.VMEM((5 * NARROW, 2 * TOKENS), bf16),
            pltpu.VMEM((4 * NARROW, TOKENS), f32),
            pltpu.VMEM((4, NARROW, 128), f32),
            pltpu.VMEM((8, 2 * TOKENS), jnp.int32),
            pltpu.VMEM((2 * NARROW, LANES), bf16),
            pltpu.VMEM((5 * NARROW, SLOTS - LANES), bf16),
            pltpu.VMEM((NARROW, SLOTS), bf16),
            pltpu.VMEM((N_BLK, 2, 256), f32),
            pltpu.VMEM((2, TOKENS), f32),
            pltpu.VMEM((N_HID, 2, TOKENS), f32),
            pltpu.VMEM((8, 256), f32),
            pltpu.VMEM((hidden, width), f32),
            pltpu.VMEM((hidden, width), f32),
            pltpu.VMEM((width, SLOTS), bf16),
            pltpu.VMEM((width, SLOTS), bf16),
            pltpu.VMEM((width, SLOTS), bf16),
            pltpu.VMEM((hidden, LANES), bf16),
            pltpu.VMEM((hidden, LANES), bf16),
            pltpu.VMEM((width, SLOTS), bf16),
            pltpu.VMEM((width, hidden), bf16),
            pltpu.VMEM((width, hidden), bf16),
            pltpu.VMEM((width, 128), bf16),
            pltpu.VMEM((8 * N_BLK, 128), f32),
            pltpu.VMEM((N_HID, 2 * N_BLK, 256), f32),
            pltpu.VMEM((GROUPS, 2, NARROW, LANES), bf16),
            pltpu.VMEM((GROUPS, 4, NARROW, LANES), bf16),
            pltpu.VMEM((GROUPS, 4, NARROW, LANES), bf16),
            pltpu.VMEM((GROUPS, 4, NARROW, HALF), bf16),
            pltpu.VMEM((GROUPS, 8, NARROW, HALF // 2), bf16),
            pltpu.VMEM((GROUPS, 4, NARROW, HALF), bf16),
            pltpu.VMEM((GROUPS, NARROW, LANES), bf16),
            pltpu.VMEM((N_HID, 2 * N_BLK, 256), f32),
            pltpu.VMEM((2 * N_BLK, 256), f32),
            pltpu.VMEM((N_BLK, 2, 256), f32),
            dma((N_BLK, 4)),
            dma((N_BLK, 4)),
            dma((GROUPS, 14)),
            dma((GROUPS, 14)),
            dma((N_HID,)),
            dma((N_HID,)),
            dma((GROUPS, 18)),
            dma((GROUPS, 18)),
            dma((N_BLK, 2)),
            dma((N_BLK, 2)),
            dma((N_HID,)),
            dma((N_HID,)),
            dma((N_BLK + N_HID,)),
            dma((N_BLK + N_HID,)),
            dma((3,)),
            dma((3,)),
            dma((7,)),
        ],
        compiler_params=pltpu.CompilerParams(
            collective_id=0, has_side_effects=True, vmem_limit_bytes=60 * 2**20
        ),
    )(*operands)


def on_device(
    tokens,
    cotangent,
    route_weight,
    expert_ids,
    timesteps,
    time_table,
    up_weight,
    down_weight,
    modulation_weight,
    modulation_bias,
):
    ids = expert_ids.T
    by_feature = modulation_weight.transpose(1, 2, 0).reshape(3 * NARROW, WIDTH)
    columns, info = modulation(timesteps, time_table, by_feature, modulation_bias, ids)
    turned = cotangent.T
    partial_results = run_experts(
        tokens, turned, route_weight.T, ids, columns, info, up_weight[0].T, down_weight[0]
    )
    token_grads, up_grads, down_grads, weight_grads, bias_grads = results_of(turned, *partial_results)
    return (token_grads.T, up_grads.T[None], down_grads[None], weight_grads.transpose(1, 0, 2), bias_grads)


def solution(mesh):
    in_specs = (
        P("blk", None),
        P("blk", "hid"),
        P("blk", None),
        P("blk", None),
        P("blk"),
        P(),
        P("blk", None, "hid"),
        P("blk", "hid", None),
        P(None, None, "hid"),
        P(None, "hid"),
    )
    out_specs = (
        P("blk", "hid"),
        P("blk", None, "hid"),
        P("blk", "hid", None),
        P("blk", None, "hid"),
        P(None, "hid"),
    )
    return jax.shard_map(
        on_device, mesh=mesh, in_specs=in_specs, out_specs=out_specs, check_vma=False
    )
```
